128 devices in a mesh: row: 8 (over y_lo, z), col: 2 (over core), fib: 8 (over y_hi, x).
Axes of the slice: x: 4, y: 4 (y_hi: 2, y_lo: 2; y = y_hi * 2 + y_lo), z: 4, core: 2. Of those that a mesh axis runs over, the one named last changes fastest.
Arguments:
- features: bfloat16 [32768, 1024], P(('row', 'col'), 'fib'), may hold values from -6 to 6
- pre_activation: bfloat16 [32768, 1024], P(('row', 'col'), 'fib'), may hold values from -8 to 8
- out_grad: bfloat16 [32768, 1024], P(('row', 'col'), 'fib'), may hold values from -1.5 to 1.5
- weight: bfloat16 [1024, 1024], P('fib'), may hold values from -0.1875 to 0.1875
- tile_values: bfloat16 [8, 2, 128, 256, 256], P('row', 'col'), may hold values from 0.0019989014 to 0.059814453
- tile_rows: int32 [8, 2, 128], P('row', 'col'), may hold values from 0 to 15, as said below
- tile_cols: int32 [8, 2, 128], P('row', 'col'), may hold values from 0 to 63, as said below
- tile_counts: int32 [8, 2], P('row', 'col'), may hold values from 16 to 128, as said below
Outputs:
- grad_features: bfloat16 [32768, 1024], P(('row', 'col'), 'fib')
- grad_weight: float32 [1024, 1024], P('fib')
The draws below stay inside these ranges and needn't reach their ends.
Inputs may be any that keep to these rules, and one draw needn't show every extreme that they name: `tile_rows`: within one block the used slots name distinct tiles, rows below 16. `tile_cols`: columns below 64. `tile_counts`: some block uses all 128 slots.
All inputs are finite; a program needn't handle non-finite values.
Results may differ from the reference program's by a relative error of at most 0.0058.
Values may be sent and summed in bfloat16 or wider, within the bound.
A program may use at most 128 MiB of HBM per device.

```python
import math
import jax
import jax.numpy as jnp
from jax import lax

F = 1024
TILE = 256
NODE_DEV = 2048
TILE_SLOTS = 128
NODES = 32768
ROW_TILES = 16
COL_TILES = 64
N_ROW = 8
N_COL = 2


def tile_slots(key):

    def pick_block(block_index):
        shuffled = jax.random.permutation(jax.random.fold_in(key, block_index), ROW_TILES * COL_TILES)
        return shuffled[:TILE_SLOTS]
    chosen = jax.vmap(pick_block)(jnp.arange(N_ROW * N_COL, dtype=jnp.int32))
    return chosen.reshape(N_ROW, N_COL, TILE_SLOTS).astype(jnp.int32)


def draw_tile_rows(key, part):
    return (tile_slots(jax.random.fold_in(key, 7)) // COL_TILES).astype(jnp.int32)


def draw_tile_cols(key, part):
    return (tile_slots(jax.random.fold_in(key, 7)) % COL_TILES).astype(jnp.int32)


def draw_tile_counts(key, part):
    counts_drawn = jax.random.randint(jax.random.fold_in(key, 11), (N_ROW * N_COL,), TILE_SLOTS // 8, TILE_SLOTS // 2 + 1)
    busiest = jax.random.randint(jax.random.fold_in(key, 13), (), 0, N_ROW * N_COL)
    counts_drawn = jnp.where(jnp.arange(N_ROW * N_COL) == busiest, TILE_SLOTS, counts_drawn)
    return counts_drawn.reshape(N_ROW, N_COL).astype(jnp.int32)


def block_levels(rng, extent, shards, least, high):
    def one(axis_at, parts):
        steps = jax.random.uniform(jax.random.fold_in(jax.random.fold_in(rng, 6), axis_at), (parts,), jnp.float32, least / len(shards), high / len(shards))
        return jnp.repeat(jnp.exp(steps), extent[axis_at] // parts).reshape((-1,) + (1,) * (len(extent) - axis_at - 1))

    level = one(*shards[0])
    for cut in shards[1:]:
        level = level * one(*cut)
    return level


def noise(rng, dims, scale, reach, pieces=(), kind=jnp.bfloat16):
    drawn = jax.random.normal(rng, dims, jnp.float32) * scale
    if len(pieces) > 0:
        drawn = block_levels(rng, dims, pieces, -0.22, 0.18) * drawn
    return jnp.clip(drawn, min=-reach, max=reach).astype(kind)


def setup_inputs(seed: int = 0) -> dict:
    key_of = jax.random.split(jax.random.key(seed), 9)
    return {
        "features": noise(key_of[0], (NODES, F), 1.0, 6.0, ((0, 16), (1, 8))),
        "pre_activation": noise(key_of[1], (NODES, F), 1.5, 8.0, ((0, 16), (1, 8))),
        "out_grad": noise(key_of[2], (NODES, F), 0.25, 1.5, ((0, 16), (1, 8))),
        "weight": noise(key_of[3], (F, F), F ** -0.5, 0.1875, ((0, 8),)),
        "tile_values": jnp.clip(jnp.exp(math.log(0.059814453) - 3.3986496 * jax.random.uniform(key_of[4], (N_ROW, N_COL, TILE_SLOTS, TILE, TILE), jnp.float32) ** block_levels(key_of[4], (N_ROW, N_COL, TILE_SLOTS, TILE, TILE), ((0, 8), (1, 2)), -0.2, 0.2)), 0.0019989014, 0.059814453).astype(jnp.bfloat16),
        "tile_rows": draw_tile_rows(jax.random.fold_in(key_of[8], 71), 0),
        "tile_cols": draw_tile_cols(jax.random.fold_in(key_of[8], 71), 0),
        "tile_counts": draw_tile_counts(jax.random.fold_in(key_of[8], 71), 0),
    }


def block_product(tile_block, row_index, col_index, live_count, panel_source, out_tiles, transpose):
    feature_cols = panel_source.shape[1]
    live_mask = (jnp.arange(tile_block.shape[0], dtype=jnp.int32) < live_count).astype(jnp.float32)
    panels = panel_source.reshape(-1, TILE, feature_cols)
    if transpose:
        products = jnp.einsum('sij,sif->sjf', tile_block.astype(jnp.float32), panels[row_index].astype(jnp.float32))
        target = col_index
    else:
        products = jnp.einsum('sij,sjf->sif', tile_block.astype(jnp.float32), panels[col_index].astype(jnp.float32))
        target = row_index
    products = products * live_mask[:, None, None]
    running = jnp.zeros((out_tiles, TILE, feature_cols), jnp.float32).at[target].add(products)
    return running.reshape(out_tiles * TILE, feature_cols)


def reference(features, pre_activation, out_grad, weight, tile_values, tile_rows, tile_cols, tile_counts):
    pre_value = pre_activation.astype(jnp.float32)
    sigmoid_value = jax.nn.sigmoid(pre_value)
    grad_local = (out_grad.astype(jnp.float32) * sigmoid_value * (1.0 + pre_value * (1.0 - sigmoid_value))).astype(jnp.bfloat16)
    projected = lax.dot_general(grad_local, weight, (((1,), (1,)), ((), ())), preferred_element_type=jnp.float32).astype(jnp.bfloat16)
    node_view = features.reshape(N_ROW, N_COL, NODE_DEV, F)
    projected_view = projected.reshape(N_ROW, N_COL * NODE_DEV, F)
    aggregated = jnp.zeros((N_ROW, N_COL * NODE_DEV, F), jnp.float32)
    transposed = jnp.zeros((N_COL, N_ROW * NODE_DEV, F), jnp.float32)
    for row_pos in range(N_ROW):
        for col_pos in range(N_COL):
            column_block = node_view[:, col_pos].reshape(N_ROW * NODE_DEV, F)
            tile_block = tile_values[row_pos, col_pos]
            row_index = tile_rows[row_pos, col_pos]
            col_index = tile_cols[row_pos, col_pos]
            live_count = tile_counts[row_pos, col_pos]
            aggregated = aggregated.at[row_pos].add(block_product(tile_block, row_index, col_index, live_count, column_block, ROW_TILES, False))
            transposed = transposed.at[col_pos].add(block_product(tile_block, row_index, col_index, live_count, projected_view[row_pos], COL_TILES, True))
    rounded = aggregated.reshape(NODES, F).astype(jnp.bfloat16)
    grad_weight = lax.dot_general(rounded, grad_local, (((0,), (0,)), ((), ())), preferred_element_type=jnp.float32)
    grad_features = transposed.reshape(N_COL, N_ROW, NODE_DEV, F).transpose(1, 0, 2, 3).reshape(NODES, F).astype(jnp.bfloat16)
    return grad_features, grad_weight
```

```python
import jax
import jax.numpy as jnp
from jax import lax
from jax.experimental import pallas as pl
from jax.experimental.pallas import tpu as pltpu
from jax.sharding import PartitionSpec as P

GROUP = 8


def tile_kernel(rows_ref, cols_ref, count_ref, grad_ref, tiles_ref, out_ref, held, total, sems):
    slots, tile, _ = tiles_ref.shape
    groups = slots // GROUP
    out_tiles = out_ref.shape[0]
    row_tiles = grad_ref.shape[0]
    count = jnp.clip(count_ref[0, 0], 0, slots)
    used = (count + GROUP - 1) // GROUP

    def copy(g):
        part = pl.ds(g * GROUP, GROUP)
        return pltpu.make_async_copy(tiles_ref.at[part], held.at[part], sems.at[g])

    @pl.loop(0, used)
    def _(g):
        copy(g).start()

    @pl.loop(0, out_tiles + 1)
    def _(t):
        total[t] = jnp.zeros(total.shape[1:], total.dtype)

    @pl.loop(0, used)
    def _(g):
        copy(g).wait()
        for j in range(GROUP):
            slot = g * GROUP + j
            row = jnp.clip(rows_ref[0, 0, slot], 0, row_tiles - 1)
            col = jnp.clip(cols_ref[0, 0, slot], 0, out_tiles - 1)
            target = jnp.where(slot < count, col, out_tiles)
            total[target] += jnp.dot(
                grad_ref[row], held[slot], preferred_element_type=jnp.float32
            )

    @pl.loop(0, out_tiles)
    def _(t):
        out_ref[t] = total[t].astype(out_ref.dtype)


def tile_products(rows, cols, count, grad, tiles, out_tiles):
    slots, tile, _ = tiles.shape
    width = grad.shape[1]
    smem = pl.BlockSpec(memory_space=pltpu.SMEM)
    vmem = pl.BlockSpec(memory_space=pltpu.VMEM)
    return pl.pallas_call(
        tile_kernel,
        out_shape=jax.ShapeDtypeStruct((out_tiles, width, tile), jnp.bfloat16),
        in_specs=[smem, smem, smem, vmem, pl.BlockSpec(memory_space=pl.ANY)],
        out_specs=vmem,
        scratch_shapes=[
            pltpu.VMEM((slots, tile, tile), jnp.bfloat16),
            pltpu.VMEM((out_tiles + 1, width, tile), jnp.float32),
            pltpu.SemaphoreType.DMA((slots // GROUP,)),
        ],
        compiler_params=pltpu.CompilerParams(vmem_limit_bytes=40 << 20),
        cost_estimate=pl.CostEstimate(
            flops=2 * slots * width * tile * tile,
            bytes_accessed=2 * slots * tile * tile,
            transcendentals=0,
        ),
        name="tile_products",
    )(rows, cols, count, grad, tiles)


def on_device(features, pre_activation, out_grad, weight, tiles, rows, cols, counts):
    nodes, width = features.shape
    tile = tiles.shape[-1]
    fib = lax.axis_size("fib")
    own_tiles = nodes // tile
    pre = pre_activation.astype(jnp.float32)
    sigmoid = jax.nn.sigmoid(pre)
    grad = (out_grad.astype(jnp.float32) * sigmoid * (1.0 + pre * (1.0 - sigmoid))).astype(
        jnp.bfloat16
    )
    grad = grad.reshape(own_tiles, tile, width).transpose(0, 2, 1)
    grad = lax.all_gather(grad, "col", axis=0, tiled=True)
    partial_t = tile_products(
        rows, cols, counts, grad, tiles[0, 0], own_tiles * lax.axis_size("row")
    )
    summed = lax.psum_scatter(partial_t, "row", scatter_dimension=0, tiled=True)
    whole = lax.all_gather(summed, "fib", axis=0)
    left = weight.reshape(width, fib, width)
    grad_features = jnp.einsum("ifo,fton->tni", left, whole, preferred_element_type=jnp.float32)
    grad_features = grad_features.astype(jnp.bfloat16).reshape(nodes, width)
    part = jnp.einsum(
        "fton,tni->foi",
        whole,
        features.reshape(own_tiles, tile, width),
        preferred_element_type=jnp.float32,
    )
    part = part.reshape(fib * width, width)
    piece = lax.psum_scatter(part, ("row", "col"), scatter_dimension=0, tiled=True)
    grad_weight = lax.all_gather(piece, ("row", "col"), axis=0, tiled=True).T
    return grad_features, grad_weight


def solution(mesh):
    in_specs = (
        P(("row", "col"), "fib"),
        P(("row", "col"), "fib"),
        P(("row", "col"), "fib"),
        P("fib", None),
        P("row", "col", None, None, None),
        P("row", "col", None),
        P("row", "col", None),
        P("row", "col"),
    )
    out_specs = (P(("row", "col"), "fib"), P("fib", None))
    return jax.shard_map(
        on_device, mesh=mesh, in_specs=in_specs, out_specs=out_specs, check_vma=False
    )
```

```python
import functools

import jax
import jax.numpy as jnp
from jax import lax
from jax.experimental import pallas as pl
from jax.experimental.pallas import tpu as pltpu
from jax.sharding import PartitionSpec as P

GROUP = 8
RING = 4
MESH = pl.DeviceIdType.MESH
SMEM = pl.BlockSpec(memory_space=pltpu.SMEM)
VMEM = pl.BlockSpec(memory_space=pltpu.VMEM)


def greet(peers):
    barrier = pltpu.get_barrier_semaphore()
    for peer in peers:
        pl.semaphore_signal(barrier, inc=1, device_id=peer, device_id_type=MESH)
    pl.semaphore_wait(barrier, len(peers))


def position():
    return lax.axis_index("row"), lax.axis_index("col"), lax.axis_index("fib")


def grad_kernel(pre_ref, out_grad_ref, grad_ref, send_sems, recv_sems):
    row, col, fib = position()
    own_tiles = grad_ref.shape[0] // 2
    tile = grad_ref.shape[2]
    partner = (row, 1 - col, fib)
    greet([partner])

    def copy(t):
        slot = grad_ref.at[col * own_tiles + t]
        return pltpu.make_async_remote_copy(
            slot, slot, send_sems.at[t], recv_sems.at[t], device_id=partner, device_id_type=MESH
        )

    @pl.loop(0, own_tiles)
    def _(t):
        part = pl.ds(pl.multiple_of(t * tile, tile), tile)
        pre = pre_ref[part, :].astype(jnp.float32)
        sigmoid = jax.nn.sigmoid(pre)
        grad = out_grad_ref[part, :].astype(jnp.float32) * sigmoid * (1.0 + pre * (1.0 - sigmoid))
        grad_ref[col * own_tiles + t] = grad.T.astype(grad_ref.dtype)
        copy(t).start()

    def arrived(t):
        slot = grad_ref.at[(1 - col) * own_tiles + t]
        return pltpu.make_async_remote_copy(
            slot, slot, send_sems.at[t], recv_sems.at[t], device_id=partner, device_id_type=MESH
        )

    @pl.loop(0, own_tiles)
    def _(t):
        copy(t).wait_send()
        arrived(t).wait_recv()


def local_grads(pre, out_grad, tile):
    nodes, width = pre.shape
    own_tiles = nodes // tile
    return pl.pallas_call(
        grad_kernel,
        out_shape=jax.ShapeDtypeStruct((2 * own_tiles, width, tile), jnp.bfloat16),
        in_specs=[VMEM, VMEM],
        out_specs=VMEM,
        scratch_shapes=[pltpu.SemaphoreType.DMA((own_tiles,))] * 2,
        compiler_params=pltpu.CompilerParams(
            collective_id=0, has_side_effects=True, vmem_limit_bytes=16 << 20
        ),
        cost_estimate=pl.CostEstimate(
            flops=10 * nodes * width, bytes_accessed=8 * nodes * width, transcendentals=nodes * width
        ),
        name="local_grads",
    )(pre, out_grad)


def tile_kernel(rows_ref, cols_ref, count_ref, grad_ref, tiles_ref, out_ref, held, total, sems):
    slots, tile, _ = tiles_ref.shape
    groups = slots // GROUP
    out_tiles = out_ref.shape[0]
    row_tiles = grad_ref.shape[0]
    count = jnp.clip(count_ref[0, 0], 0, slots)
    used = (count + GROUP - 1) // GROUP

    def copy(g):
        part = pl.ds(g * GROUP, GROUP)
        return pltpu.make_async_copy(tiles_ref.at[part], held.at[part], sems.at[g])

    @pl.loop(0, used)
    def _(g):
        copy(g).start()

    @pl.loop(0, out_tiles + 1)
    def _(t):
        total[t] = jnp.zeros(total.shape[1:], total.dtype)

    @pl.loop(0, used)
    def _(g):
        copy(g).wait()
        for j in range(GROUP):
            slot = g * GROUP + j
            row = jnp.clip(rows_ref[0, 0, slot], 0, row_tiles - 1)
            col = jnp.clip(cols_ref[0, 0, slot], 0, out_tiles - 1)
            target = jnp.where(slot < count, col, out_tiles)
            total[target] += jnp.dot(
                grad_ref[row], held[slot], preferred_element_type=jnp.float32
            )

    @pl.loop(0, out_tiles)
    def _(t):
        out_ref[t] = total[t].astype(out_ref.dtype)


def tile_products(rows, cols, count, grad, tiles, out_tiles):
    slots, tile, _ = tiles.shape
    width = grad.shape[1]
    return pl.pallas_call(
        tile_kernel,
        out_shape=jax.ShapeDtypeStruct((out_tiles, width, tile), jnp.bfloat16),
        in_specs=[SMEM, SMEM, SMEM, VMEM, pl.BlockSpec(memory_space=pl.ANY)],
        out_specs=VMEM,
        scratch_shapes=[
            pltpu.VMEM((slots, tile, tile), jnp.bfloat16),
            pltpu.VMEM((out_tiles + 1, width, tile), jnp.float32),
            pltpu.SemaphoreType.DMA((slots // GROUP,)),
        ],
        compiler_params=pltpu.CompilerParams(vmem_limit_bytes=40 << 20),
        cost_estimate=pl.CostEstimate(
            flops=2 * slots * width * tile * tile,
            bytes_accessed=2 * slots * tile * tile,
            transcendentals=0,
        ),
        name="tile_products",
    )(rows, cols, count, grad, tiles)


def flow_kernel(
    part_ref, weight_ref, feat_ref, gf_ref, gw_ref,
    first, second, merged, half, pair_in, total, whole, send_sems, recv_sems,
):
    row, col, fib = position()
    l, z = row // RING, lax.rem(row, RING)
    h, x = fib // RING, lax.rem(fib, RING)
    chunks, tile = part_ref.shape[2], part_ref.shape[4]
    z_up, z_down, z_far = (lax.rem(z + d, RING) for d in (1, RING - 1, 2))
    x_up, x_down, x_far = (lax.rem(x + d, RING) for d in (1, RING - 1, 2))
    to_z_up, to_z_down = (l * RING + z_up, col, fib), (l * RING + z_down, col, fib)
    to_x_up, to_x_down = (row, col, h * RING + x_up), (row, col, h * RING + x_down)
    to_pair = ((1 - l) * RING + z, col, fib)
    to_cross = ((1 - l) * RING + z, col, (1 - h) * RING + x)
    greet([to_z_up, to_z_down, to_x_up, to_x_down, to_pair, to_cross])

    def copy(kind, t, source, target, peer):
        return pltpu.make_async_remote_copy(
            source,
            target,
            send_sems.at[kind, t],
            recv_sems.at[kind, t],
            device_id=peer,
            device_id_type=MESH,
        )

    def link(kind, t):
        if kind == 0:
            return copy(0, t, part_ref.at[0, z_far, t], first.at[0, t], to_z_up)
        if kind == 1:
            return copy(1, t, part_ref.at[1, z_far, t], first.at[1, t], to_z_down)
        if kind == 2:
            return copy(2, t, part_ref.at[1, z_up, t], second.at[0, t, 1], to_z_up)
        if kind == 3:
            return copy(3, t, part_ref.at[0, z_down, t], second.at[1, t, 0], to_z_down)
        if kind == 4:
            return copy(4, t, merged.at[0, t], second.at[0, t, 0], to_z_up)
        if kind == 5:
            return copy(5, t, merged.at[1, t], second.at[1, t, 1], to_z_down)
        if kind == 6:
            return copy(6, t, half.at[t], pair_in.at[t], to_pair)
        if kind == 7:
            return copy(7, t, total.at[t], whole.at[t, x, h], to_pair)
        if kind == 8:
            return copy(8, t, total.at[t], whole.at[t, x, h], to_cross)
        if kind == 9:
            return copy(9, t, whole.at[t, x], whole.at[t, x], to_x_up)
        if kind == 10:
            return copy(10, t, whole.at[t, x], whole.at[t, x], to_x_down)
        if kind == 11:
            return copy(11, t, whole.at[t, x_down, 0], whole.at[t, x_down, 0], to_x_up)
        return copy(12, t, whole.at[t, x_up, 1], whole.at[t, x_up, 1], to_x_down)

    def arrived(kind, t):
        if kind == 7:
            slot = whole.at[t, x, h]
        elif kind == 8:
            slot = whole.at[t, x, 1 - h]
        elif kind == 9:
            slot = whole.at[t, x_down]
        elif kind == 10:
            slot = whole.at[t, x_up]
        elif kind == 11:
            slot = whole.at[t, x_far, 0]
        elif kind == 12:
            slot = whole.at[t, x_far, 1]
        else:
            link(kind, t).wait_recv()
            return
        copy(kind, t, slot, slot, to_pair).wait_recv()

    def added(*refs):
        terms = [r[...].astype(jnp.float32) for r in refs]
        return functools.reduce(lambda a, b: a + b, terms)

    gw_ref[...] = jnp.zeros_like(gw_ref)

    def send_shares(t):
        for kind in range(4):
            link(kind, t).start()

    def merge(t):
        arrived(0, t)
        merged[0, t] = added(part_ref.at[0, z_up, t], first.at[0, t]).astype(merged.dtype)
        link(4, t).start()
        arrived(1, t)
        merged[1, t] = added(part_ref.at[1, z_down, t], first.at[1, t]).astype(merged.dtype)
        link(5, t).start()

    def sum_over_z(t):
        for kind in (2, 3, 4, 5):
            arrived(kind, t)
        half[t] = added(part_ref.at[l, z, t], second.at[0, t, l], second.at[1, t, l]).astype(half.dtype)
        link(6, t).start()

    def sum_over_y(t):
        o = 1 - l
        arrived(6, t)
        total[t] = added(
            part_ref.at[o, z, t], second.at[0, t, o], second.at[1, t, o], pair_in.at[t]
        ).astype(total.dtype)
        link(7, t).start()
        link(8, t).start()

    def spread(t):
        arrived(7, t)
        arrived(8, t)
        link(9, t).start()
        link(10, t).start()

    def forward(t):
        arrived(9, t)
        link(11, t).start()
        arrived(10, t)
        link(12, t).start()

    def multiply(t):
        arrived(11, t)
        arrived(12, t)
        panel = whole[t].reshape(weight_ref.shape[1], tile)
        part = pl.ds(pl.multiple_of(t * tile, tile), tile)
        product = jnp.dot(weight_ref[...], panel, preferred_element_type=jnp.float32)
        gf_ref[part, :] = product.T.astype(gf_ref.dtype)
        gw_ref[...] += jnp.dot(panel, feat_ref[part, :], preferred_element_type=jnp.float32)

    stages = (send_shares, merge, sum_over_z, sum_over_y, spread, forward, multiply)

    @pl.loop(0, chunks + len(stages) - 1)
    def _(step):
        for late, stage in enumerate(stages):
            t = step - late

            @pl.when((t >= 0) & (t < chunks))
            def _(stage=stage, t=t):
                stage(t)

    @pl.loop(0, chunks)
    def _(t):
        for kind in range(13):
            link(kind, t).wait_send()


def flow(part, weight, features):
    _, _, chunks, width, tile = part.shape
    nodes, whole = features.shape[0], weight.shape[1]
    piece = (width, tile)
    sixteen = jnp.bfloat16
    return pl.pallas_call(
        flow_kernel,
        out_shape=(
            jax.ShapeDtypeStruct((nodes, width), sixteen),
            jax.ShapeDtypeStruct((whole, width), jnp.float32),
        ),
        in_specs=[VMEM] * 3,
        out_specs=(VMEM, VMEM),
        scratch_shapes=[
            pltpu.VMEM((2, chunks, *piece), sixteen),
            pltpu.VMEM((2, chunks, 2, *piece), sixteen),
            pltpu.VMEM((2, chunks, *piece), sixteen),
            pltpu.VMEM((chunks, *piece), sixteen),
            pltpu.VMEM((chunks, *piece), sixteen),
            pltpu.VMEM((chunks, *piece), sixteen),
            pltpu.VMEM((chunks, RING, 2, *piece), sixteen),
            pltpu.SemaphoreType.DMA((13, chunks)),
            pltpu.SemaphoreType.DMA((13, chunks)),
        ],
        compiler_params=pltpu.CompilerParams(
            collective_id=1, has_side_effects=True, vmem_limit_bytes=40 << 20
        ),
        cost_estimate=pl.CostEstimate(
            flops=4 * nodes * width * whole, bytes_accessed=16 << 20, transcendentals=0
        ),
        name="flow",
    )(part, weight, features)


def weight_kernel(part_ref, out_ref, mate_in, mine, row_in, sems):
    row, col, fib = position()
    rows = out_ref.shape[0] // 16
    span = 8 * rows
    mate = (row, 1 - col, fib)
    peers = [(lax.rem(row + d, 8), col, fib) for d in range(1, 8)]
    greet([mate, *peers])

    def copy(kind, d, source, target, peer):
        return pltpu.make_async_remote_copy(
            source, target, sems.at[0, kind, d], sems.at[1, kind, d], device_id=peer, device_id_type=MESH
        )

    def at(ref, start, size):
        return ref.at[pl.ds(pl.multiple_of(start, rows), size)]

    swap = copy(0, 0, at(part_ref, (1 - col) * span, span), mate_in, mate)
    swap.start()
    swap.wait()
    mine[...] = part_ref[pl.ds(pl.multiple_of(col * span, span), span), :] + mate_in[...]
    sends = []
    for d in range(1, 8):
        to = lax.rem(row + d, 8)
        sends.append(copy(1, d, at(mine, to * rows, rows), row_in.at[d], peers[d - 1]))
        sends[-1].start()
    own = mine[pl.ds(pl.multiple_of(row * rows, rows), rows), :]
    for s, d in zip(sends, range(1, 8)):
        s.wait_recv()
        own += row_in[d]
    here = col * span + row * rows
    out_ref[pl.ds(pl.multiple_of(here, rows), rows), :] = own
    gives = []
    for d in range(1, 8):
        piece = at(out_ref, here, rows)
        gives.append(copy(2, d, piece, piece, peers[d - 1]))
        gives[-1].start()
    for d in range(1, 8):
        slot = at(out_ref, col * span + lax.rem(row + 8 - d, 8) * rows, rows)
        copy(2, d, slot, slot, peers[d - 1]).wait_recv()
    final = at(out_ref, col * span, span)
    last = copy(0, 1, final, final, mate)
    last.start()
    for s in (*sends, *gives):
        s.wait_send()
    last.wait_send()
    slot = at(out_ref, (1 - col) * span, span)
    copy(0, 1, slot, slot, mate).wait_recv()


def weight_sum(part):
    depth, width = part.shape
    return pl.pallas_call(
        weight_kernel,
        out_shape=jax.ShapeDtypeStruct(part.shape, part.dtype),
        in_specs=[VMEM],
        out_specs=VMEM,
        scratch_shapes=[
            pltpu.VMEM((depth // 2, width), part.dtype),
            pltpu.VMEM((depth // 2, width), part.dtype),
            pltpu.VMEM((8, depth // 16, width), part.dtype),
            pltpu.SemaphoreType.DMA((2, 3, 8)),
        ],
        compiler_params=pltpu.CompilerParams(
            collective_id=2, has_side_effects=True, vmem_limit_bytes=16 << 20
        ),
        cost_estimate=pl.CostEstimate(flops=1 << 20, bytes_accessed=2 << 20, transcendentals=0),
        name="weight_sum",
    )(part)


def on_device(features, pre_activation, out_grad, weight, tiles, rows, cols, counts):
    nodes, width = features.shape
    tile = tiles.shape[-1]
    own_tiles = nodes // tile
    grad = local_grads(pre_activation, out_grad, tile)
    part = tile_products(rows, cols, counts, grad, tiles[0, 0], 8 * own_tiles)
    part = part.reshape(2, RING, own_tiles, width, tile)
    mixed = weight.reshape(width, 2, RING, width).transpose(0, 2, 1, 3).reshape(width, -1)
    grad_features, share = flow(part, mixed, features)
    total = weight_sum(share)
    grad_weight = total.reshape(RING, 2, width, width).transpose(3, 1, 0, 2).reshape(width, -1)
    return grad_features, grad_weight


def solution(mesh):
    in_specs = (
        P(("row", "col"), "fib"),
        P(("row", "col"), "fib"),
        P(("row", "col"), "fib"),
        P("fib", None),
        P("row", "col", None, None, None),
        P("row", "col", None),
        P("row", "col", None),
        P("row", "col"),
    )
    out_specs = (P(("row", "col"), "fib"), P("fib", None))
    return jax.shard_map(
        on_device, mesh=mesh, in_specs=in_specs, out_specs=out_specs, check_vma=False
    )
```

```python
import functools

import jax
import jax.numpy as jnp
from jax import lax
from jax.experimental import pallas as pl
from jax.experimental.pallas import tpu as pltpu
from jax.sharding import PartitionSpec as P

GROUP = 8
RING = 4
LAGS = (0, 1, 2, 3, 4, 5, 6)
MESH = pl.DeviceIdType.MESH
VMEM = pl.BlockSpec(memory_space=pltpu.VMEM)
ANY = pl.BlockSpec(memory_space=pl.ANY)
CHUNK = 128


def greet(peers):
    barrier = pltpu.get_barrier_semaphore()
    for peer in peers:
        pl.semaphore_signal(barrier, inc=1, device_id=peer, device_id_type=MESH)
    pl.semaphore_wait(barrier, len(peers))


def position():
    return lax.axis_index("row"), lax.axis_index("col"), lax.axis_index("fib")


def grad_kernel(
    pre_hbm, out_grad_hbm, grad_ref, pre_ref, out_grad_ref, load_sems, send_sems, recv_sems
):
    row, col, fib = position()
    own_tiles = grad_ref.shape[0] // 2
    tile = grad_ref.shape[2]
    partner = (row, 1 - col, fib)

    def loads(t):
        part = pl.ds(pl.multiple_of(t * tile, tile), tile)
        return (
            pltpu.make_async_copy(pre_hbm.at[part], pre_ref.at[part], load_sems.at[0, t]),
            pltpu.make_async_copy(out_grad_hbm.at[part], out_grad_ref.at[part], load_sems.at[1, t]),
        )

    @pl.loop(0, own_tiles)
    def _(t):
        for load in loads(t):
            load.start()

    greet([partner])

    def copy(t, owner):
        slot = grad_ref.at[owner * own_tiles + t]
        return pltpu.make_async_remote_copy(
            slot, slot, send_sems.at[t], recv_sems.at[t], device_id=partner, device_id_type=MESH
        )

    @pl.loop(0, own_tiles)
    def _(t):
        for load in loads(t):
            load.wait()
        part = pl.ds(pl.multiple_of(t * tile, tile), tile)
        pre = pre_ref[part, :].astype(jnp.float32)
        sigmoid = jax.nn.sigmoid(pre)
        grad = out_grad_ref[part, :].astype(jnp.float32) * sigmoid * (1.0 + pre * (1.0 - sigmoid))
        grad_ref[col * own_tiles + t] = grad.T.astype(grad_ref.dtype)
        copy(t, col).start()

    @pl.loop(0, own_tiles)
    def _(t):
        copy(t, col).wait_send()
        copy(t, 1 - col).wait_recv()


def local_grads(pre, out_grad, tile):
    nodes, width = pre.shape
    own_tiles = nodes // tile
    return pl.pallas_call(
        grad_kernel,
        out_shape=jax.ShapeDtypeStruct((2 * own_tiles, width, tile), jnp.bfloat16),
        in_specs=[ANY, ANY],
        out_specs=VMEM,
        scratch_shapes=[
            pltpu.VMEM(pre.shape, pre.dtype),
            pltpu.VMEM(pre.shape, pre.dtype),
            pltpu.SemaphoreType.DMA((2, own_tiles)),
            pltpu.SemaphoreType.DMA((own_tiles,)),
            pltpu.SemaphoreType.DMA((own_tiles,)),
        ],
        compiler_params=pltpu.CompilerParams(
            collective_id=0, has_side_effects=True, vmem_limit_bytes=8 << 20
        ),
        cost_estimate=pl.CostEstimate(
            flops=10 * nodes * width, bytes_accessed=8 * nodes * width, transcendentals=nodes * width
        ),
        name="local_grads",
    )(pre, out_grad)


def tile_kernel(
    rows_hbm, cols_hbm, count_hbm, grad_ref, tiles_ref, out_ref,
    held, total, rows_ref, cols_ref, count_ref, sems, index_sems,
):
    slots, tile, _ = tiles_ref.shape
    cuts = tile // CHUNK
    out_tiles = out_ref.shape[0] // cuts
    row_tiles = grad_ref.shape[0]
    def copy(g):
        part = pl.ds(g * GROUP, GROUP)
        return pltpu.make_async_copy(tiles_ref.at[part], held.at[part], sems.at[g])

    indices = [
        pltpu.make_async_copy(source, target, index_sems.at[i])
        for i, (source, target) in enumerate(
            ((count_hbm, count_ref), (rows_hbm, rows_ref), (cols_hbm, cols_ref))
        )
    ]
    for load in indices:
        load.start()
    copy(0).start()
    indices[0].wait()
    count = jnp.clip(count_ref[0, 0], 1, slots)
    used = (count + GROUP - 1) // GROUP

    @pl.loop(1, used)
    def _(g):
        copy(g).start()

    @pl.loop(0, out_tiles + 1)
    def _(t):
        total[t] = jnp.zeros(total.shape[1:], total.dtype)

    for load in indices[1:]:
        load.wait()

    @pl.loop(0, used)
    def _(g):
        copy(g).wait()
        for j in range(GROUP):
            slot = g * GROUP + j
            row = jnp.clip(rows_ref[0, 0, slot], 0, row_tiles - 1)
            col = jnp.clip(cols_ref[0, 0, slot], 0, out_tiles - 1)
            target = jnp.where(slot < count, col, out_tiles)
            total[target] += jnp.dot(
                grad_ref[row], held[slot], preferred_element_type=jnp.float32
            )

    @pl.loop(0, out_tiles)
    def _(t):
        for cut in range(cuts):
            out_ref[t * cuts + cut] = total[t, :, cut * CHUNK : (cut + 1) * CHUNK].astype(out_ref.dtype)


def tile_products(rows, cols, count, grad, tiles, out_tiles):
    slots, tile, _ = tiles.shape
    width = grad.shape[1]
    return pl.pallas_call(
        tile_kernel,
        out_shape=jax.ShapeDtypeStruct((out_tiles * tile // CHUNK, width, CHUNK), jnp.bfloat16),
        in_specs=[ANY, ANY, ANY, VMEM, ANY],
        out_specs=VMEM,
        scratch_shapes=[
            pltpu.VMEM((slots, tile, tile), jnp.bfloat16),
            pltpu.VMEM((out_tiles + 1, width, tile), jnp.float32),
            pltpu.SMEM(rows.shape, rows.dtype),
            pltpu.SMEM(cols.shape, cols.dtype),
            pltpu.SMEM(count.shape, count.dtype),
            pltpu.SemaphoreType.DMA((slots // GROUP,)),
            pltpu.SemaphoreType.DMA((3,)),
        ],
        compiler_params=pltpu.CompilerParams(vmem_limit_bytes=28 << 20),
        cost_estimate=pl.CostEstimate(
            flops=2 * slots * width * tile * tile,
            bytes_accessed=2 * slots * tile * tile,
            transcendentals=0,
        ),
        name="tile_products",
    )(rows, cols, count, grad, tiles)


def flow_kernel(
    part_all, weight_hbm, feat_hbm, gf_ref, gw_out,
    first, second, merged, half, pair_in, total, whole, weight_raw, weight_ref, feat_ref, gw_ref, gw_send, gw_in,
    load_sems, send_sems, recv_sems, gw_sems,
):
    width = part_all.shape[1]
    chunks, nodes_t = whole.shape[0], part_all.shape[2]
    loads = [
        pltpu.make_async_copy(weight_hbm, weight_raw, load_sems.at[0]),
        pltpu.make_async_copy(feat_hbm, feat_ref, load_sems.at[1]),
    ]
    for load in loads:
        load.start()
    row, col, fib = position()
    l, z = row // RING, lax.rem(row, RING)
    h, x = fib // RING, lax.rem(fib, RING)
    z_up, z_down, z_far = (lax.rem(z + d, RING) for d in (1, RING - 1, 2))
    x_up, x_down, x_far = (lax.rem(x + d, RING) for d in (1, RING - 1, 2))
    to_z_up, to_z_down = (l * RING + z_up, col, fib), (l * RING + z_down, col, fib)
    to_x_up, to_x_down = (row, col, h * RING + x_up), (row, col, h * RING + x_down)
    to_pair = ((1 - l) * RING + z, col, fib)
    to_cross = ((1 - l) * RING + z, col, (1 - h) * RING + x)
    peers = [
        (lax.rem(row + d // 2, 8), lax.rem(col + d, 2), fib) for d in range(1, 16)
    ]
    greet([to_x_up, to_x_down, to_cross, *peers])

    def part_at(to_l, to_z, t):
        return part_all.at[(to_l * RING + to_z) * chunks + t]

    def copy(kind, t, source, target, peer):
        return pltpu.make_async_remote_copy(
            source,
            target,
            send_sems.at[kind, t],
            recv_sems.at[kind, t],
            device_id=peer,
            device_id_type=MESH,
        )

    def link(kind, t):
        if kind == 0:
            return copy(0, t, part_at(0, z_far, t), first.at[0, t], to_z_up)
        if kind == 1:
            return copy(1, t, part_at(1, z_far, t), first.at[1, t], to_z_down)
        if kind == 2:
            return copy(2, t, part_at(1, z_up, t), second.at[0, t, 1], to_z_up)
        if kind == 3:
            return copy(3, t, part_at(0, z_down, t), second.at[1, t, 0], to_z_down)
        if kind == 4:
            return copy(4, t, merged.at[0, t], second.at[0, t, 0], to_z_up)
        if kind == 5:
            return copy(5, t, merged.at[1, t], second.at[1, t, 1], to_z_down)
        if kind == 6:
            return copy(6, t, half.at[t], pair_in.at[t], to_pair)
        if kind == 7:
            return copy(7, t, total.at[t], whole.at[t, x, h], to_pair)
        if kind == 8:
            return copy(8, t, total.at[t], whole.at[t, x, h], to_cross)
        if kind == 9:
            return copy(9, t, whole.at[t, x], whole.at[t, x], to_x_up)
        if kind == 10:
            return copy(10, t, whole.at[t, x], whole.at[t, x], to_x_down)
        if kind == 11:
            return copy(11, t, whole.at[t, x_down, 0], whole.at[t, x_down, 0], to_x_up)
        return copy(12, t, whole.at[t, x_up, 1], whole.at[t, x_up, 1], to_x_down)

    def arrived(kind, t):
        if kind == 7:
            slot = whole.at[t, x, h]
        elif kind == 8:
            slot = whole.at[t, x, 1 - h]
        elif kind == 9:
            slot = whole.at[t, x_down]
        elif kind == 10:
            slot = whole.at[t, x_up]
        elif kind == 11:
            slot = whole.at[t, x_far, 0]
        elif kind == 12:
            slot = whole.at[t, x_far, 1]
        else:
            link(kind, t).wait_recv()
            return
        copy(kind, t, slot, slot, to_pair).wait_recv()

    def added(*refs):
        terms = [r[...].astype(jnp.float32) for r in refs]
        return functools.reduce(lambda a, b: a + b, terms)

    gw_ref[...] = jnp.zeros_like(gw_ref)

    def settle_loads():
        for load in loads:
            load.wait()
        for k in range(2 * RING):
            source = (k % 2) * RING + k // 2
            weight_ref[:, k * width : (k + 1) * width] = weight_raw[:, source * width : (source + 1) * width]

    def send_shares(t):
        for kind in range(4):
            link(kind, t).start()

    def merge(t):
        arrived(0, t)
        merged[0, t] = added(part_at(0, z_up, t), first.at[0, t]).astype(merged.dtype)
        link(4, t).start()
        arrived(1, t)
        merged[1, t] = added(part_at(1, z_down, t), first.at[1, t]).astype(merged.dtype)
        link(5, t).start()

    def sum_over_z(t):
        for kind in (2, 3, 4, 5):
            arrived(kind, t)
        half[t] = added(part_at(l, z, t), second.at[0, t, l], second.at[1, t, l]).astype(half.dtype)
        link(6, t).start()

    def sum_over_y(t):
        o = 1 - l
        arrived(6, t)
        total[t] = added(
            part_at(o, z, t), second.at[0, t, o], second.at[1, t, o], pair_in.at[t]
        ).astype(total.dtype)
        link(7, t).start()
        link(8, t).start()

    def spread(t):
        arrived(7, t)
        arrived(8, t)
        link(9, t).start()
        link(10, t).start()

    def forward(t):
        arrived(9, t)
        link(11, t).start()
        arrived(10, t)
        link(12, t).start()

    def multiply(t):
        arrived(11, t)
        arrived(12, t)

        @pl.when(lax.rem(t, 2) == 1)
        def _():
            depth = weight_ref.shape[1]
            panel = jnp.concatenate(
                [whole[t - 1].reshape(depth, nodes_t), whole[t].reshape(depth, nodes_t)], axis=1
            )
            part = pl.ds(pl.multiple_of((t - 1) * nodes_t, 2 * nodes_t), 2 * nodes_t)
            product = jnp.dot(weight_ref[...], panel, preferred_element_type=jnp.float32)
            gf_ref[part, :] = product.T.astype(gf_ref.dtype)
            gw_ref[...] += jnp.dot(panel, feat_ref[part, :], preferred_element_type=jnp.float32)

    stages = (send_shares, merge, sum_over_z, sum_over_y, spread, forward, multiply)

    settle_loads()

    @pl.loop(0, chunks + LAGS[-1])
    def _(step):
        for late, stage in zip(LAGS, stages):
            t = step - late

            @pl.when((t >= 0) & (t < chunks))
            def _(stage=stage, t=t):
                stage(t)

    rows = gw_ref.shape[0] // 16

    def place(of_row, of_col):
        return of_row * 2 + of_col

    def piece(ref, of):
        return ref.at[pl.ds(pl.multiple_of(of * rows, rows), rows)]

    def gw_copy(phase, d, source, target):
        return pltpu.make_async_remote_copy(
            source, target, gw_sems.at[phase, 0, d], gw_sems.at[phase, 1, d], device_id=peers[d - 1], device_id_type=MESH
        )

    here = place(row, col)
    gw_send[...] = gw_ref[...].astype(gw_send.dtype)
    gives = []
    for d, peer in enumerate(peers, 1):
        gives.append(gw_copy(0, d, piece(gw_send, place(peer[0], peer[1])), gw_in.at[d]))
        gives[-1].start()
    own = gw_ref[pl.ds(pl.multiple_of(here * rows, rows), rows), :]
    for d in range(1, 16):
        gives[d - 1].wait_recv()
        own += gw_in[d].astype(jnp.float32)
    gw_out[pl.ds(pl.multiple_of(here * rows, rows), rows), :] = own.astype(gw_out.dtype)
    for d in range(1, 16):
        gives.append(gw_copy(1, d, piece(gw_out, here), piece(gw_out, here)))
        gives[-1].start()

    @pl.loop(0, chunks)
    def _(t):
        for kind in range(13):
            link(kind, t).wait_send()

    for d in range(1, 16):
        slot = piece(gw_out, place(lax.rem(row + 8 - (d // 2), 8), lax.rem(col + d, 2)))
        gw_copy(1, d, slot, slot).wait_recv()
    for give in gives:
        give.wait_send()


def flow(part, weight, features):
    _, width, cut = part.shape
    nodes, whole = features.shape[0], weight.shape[1]
    chunks = nodes // cut
    piece = (width, cut)
    sixteen = jnp.bfloat16
    return pl.pallas_call(
        flow_kernel,
        out_shape=(
            jax.ShapeDtypeStruct((nodes, width), sixteen),
            jax.ShapeDtypeStruct((whole, width), sixteen),
        ),
        in_specs=[VMEM, ANY, ANY],
        out_specs=(VMEM, VMEM),
        scratch_shapes=[
            pltpu.VMEM((2, chunks, *piece), sixteen),
            pltpu.VMEM((2, chunks, 2, *piece), sixteen),
            pltpu.VMEM((2, chunks, *piece), sixteen),
            pltpu.VMEM((chunks, *piece), sixteen),
            pltpu.VMEM((chunks, *piece), sixteen),
            pltpu.VMEM((chunks, *piece), sixteen),
            pltpu.VMEM((chunks, RING, 2, *piece), sixteen),
            pltpu.VMEM(weight.shape, sixteen),
            pltpu.VMEM(weight.shape, sixteen),
            pltpu.VMEM(features.shape, sixteen),
            pltpu.VMEM((whole, width), jnp.float32),
            pltpu.VMEM((whole, width), sixteen),
            pltpu.VMEM((16, whole // 16, width), sixteen),
            pltpu.SemaphoreType.DMA((2,)),
            pltpu.SemaphoreType.DMA((13, chunks)),
            pltpu.SemaphoreType.DMA((13, chunks)),
            pltpu.SemaphoreType.DMA((2, 2, 16)),
        ],
        compiler_params=pltpu.CompilerParams(
            collective_id=1, has_side_effects=True, vmem_limit_bytes=20 << 20
        ),
        cost_estimate=pl.CostEstimate(
            flops=4 * nodes * width * whole, bytes_accessed=16 << 20, transcendentals=0
        ),
        name="flow",
    )(part, weight, features)


def finish_kernel(gf_ref, gw_ref, gf_hbm, gw_hbm, gw_turned, sems):
    width = gw_turned.shape[0]
    write_gf = pltpu.make_async_copy(gf_ref, gf_hbm, sems.at[0])
    write_gf.start()
    for k in range(2 * RING):
        target = (k % 2) * RING + k // 2
        block = gw_ref[k * width : (k + 1) * width, :].astype(jnp.float32)
        gw_turned[:, target * width : (target + 1) * width] = block.T
    write_gw = pltpu.make_async_copy(gw_turned, gw_hbm, sems.at[1])
    write_gw.start()
    write_gf.wait()
    write_gw.wait()


def finish(gf, gw):
    turned = gw.shape[::-1]
    return pl.pallas_call(
        finish_kernel,
        out_shape=(
            jax.ShapeDtypeStruct(gf.shape, gf.dtype),
            jax.ShapeDtypeStruct(turned, jnp.float32),
        ),
        in_specs=[VMEM, VMEM],
        out_specs=(ANY, ANY),
        scratch_shapes=[pltpu.VMEM(turned, jnp.float32), pltpu.SemaphoreType.DMA((2,))],
        compiler_params=pltpu.CompilerParams(vmem_limit_bytes=4 << 20),
        cost_estimate=pl.CostEstimate(flops=0, bytes_accessed=1 << 20, transcendentals=0),
        name="finish",
    )(gf, gw)


def on_device(features, pre_activation, out_grad, weight, tiles, rows, cols, counts):
    tile = tiles.shape[-1]
    grad = local_grads(pre_activation, out_grad, tile)
    part = tile_products(rows, cols, counts, grad, tiles[0, 0], 8 * (features.shape[0] // tile))
    return finish(*flow(part, weight, features))


def solution(mesh):
    in_specs = (
        P(("row", "col"), "fib"),
        P(("row", "col"), "fib"),
        P(("row", "col"), "fib"),
        P("fib", None),
        P("row", "col", None, None, None),
        P("row", "col", None),
        P("row", "col", None),
        P("row", "col"),
    )
    out_specs = (P(("row", "col"), "fib"), P("fib", None))
    return jax.shard_map(
        on_device, mesh=mesh, in_specs=in_specs, out_specs=out_specs, check_vma=False
    )
```

```python
import functools

import jax
import jax.numpy as jnp
from jax import lax
from jax.experimental import pallas as pl
from jax.experimental.pallas import tpu as pltpu
from jax.sharding import PartitionSpec as P

GROUP = 8
RING = 4
LAGS = (0, 2, 4, 6, 8, 10)
MESH = pl.DeviceIdType.MESH
VMEM = pl.BlockSpec(memory_space=pltpu.VMEM)
HBM = pl.BlockSpec(memory_space=pltpu.HBM)
CHUNK = 128
DIRECT = 2


def greet(peers):
    barrier = pltpu.get_barrier_semaphore()
    for peer in peers:
        pl.semaphore_signal(barrier, inc=1, device_id=peer, device_id_type=MESH)
    pl.semaphore_wait(barrier, len(peers))


def position():
    return lax.axis_index("row"), lax.axis_index("col"), lax.axis_index("fib")


def grad_kernel(
    pre_hbm, out_grad_hbm, grad_ref, pre_ref, out_grad_ref, load_sems, send_sems, recv_sems
):
    row, col, fib = position()
    own_tiles = grad_ref.shape[0] // 2
    tile = grad_ref.shape[2]
    partner = (row, 1 - col, fib)

    def loads(t):
        part = pl.ds(pl.multiple_of(t * tile, tile), tile)
        return (
            pltpu.make_async_copy(pre_hbm.at[part], pre_ref.at[part], load_sems.at[0, t]),
            pltpu.make_async_copy(out_grad_hbm.at[part], out_grad_ref.at[part], load_sems.at[1, t]),
        )

    @pl.loop(0, own_tiles)
    def _(t):
        for load in loads(t):
            load.start()

    greet([partner])

    def copy(t, owner):
        slot = grad_ref.at[owner * own_tiles + t]
        return pltpu.make_async_remote_copy(
            slot, slot, send_sems.at[t], recv_sems.at[t], device_id=partner, device_id_type=MESH
        )

    @pl.loop(0, own_tiles)
    def _(t):
        for load in loads(t):
            load.wait()
        part = pl.ds(pl.multiple_of(t * tile, tile), tile)
        pre = pre_ref[part, :].astype(jnp.float32)
        sigmoid = jax.nn.sigmoid(pre)
        grad = out_grad_ref[part, :].astype(jnp.float32) * sigmoid * (1.0 + pre * (1.0 - sigmoid))
        grad_ref[col * own_tiles + t] = grad.T.astype(grad_ref.dtype)
        copy(t, col).start()

    @pl.loop(0, own_tiles)
    def _(t):
        copy(t, col).wait_send()
        copy(t, 1 - col).wait_recv()


def local_grads(pre, out_grad, tile):
    nodes, width = pre.shape
    own_tiles = nodes // tile
    return pl.pallas_call(
        grad_kernel,
        out_shape=jax.ShapeDtypeStruct((2 * own_tiles, width, tile), jnp.bfloat16),
        in_specs=[HBM, HBM],
        out_specs=VMEM,
        scratch_shapes=[
            pltpu.VMEM(pre.shape, pre.dtype),
            pltpu.VMEM(pre.shape, pre.dtype),
            pltpu.SemaphoreType.DMA((2, own_tiles)),
            pltpu.SemaphoreType.DMA((own_tiles,)),
            pltpu.SemaphoreType.DMA((own_tiles,)),
        ],
        compiler_params=pltpu.CompilerParams(
            collective_id=0, has_side_effects=True, vmem_limit_bytes=8 << 20
        ),
        cost_estimate=pl.CostEstimate(
            flops=10 * nodes * width, bytes_accessed=8 * nodes * width, transcendentals=nodes * width
        ),
        name="local_grads",
    )(pre, out_grad)


def tile_kernel(
    rows_hbm, cols_hbm, count_ref, grad_ref, tiles_ref, out_ref,
    held, total, rows_ref, cols_ref, sems, index_sems,
):
    slots, tile, _ = tiles_ref.shape
    cuts = tile // CHUNK
    out_tiles = out_ref.shape[0] // cuts
    row_tiles = grad_ref.shape[0]
    def copy(g):
        part = pl.ds(g * GROUP, GROUP)
        return pltpu.make_async_copy(tiles_ref.at[part], held.at[part], sems.at[g])

    indices = [
        pltpu.make_async_copy(source, target, index_sems.at[i])
        for i, (source, target) in enumerate(
            ((rows_hbm, rows_ref), (cols_hbm, cols_ref))
        )
    ]
    for load in indices:
        load.start()
    count = jnp.clip(count_ref[0, 0], 1, slots)
    used = (count + GROUP - 1) // GROUP

    @pl.loop(0, used)
    def _(g):
        copy(g).start()

    @pl.loop(0, out_tiles + 1)
    def _(t):
        total[t] = jnp.zeros(total.shape[1:], total.dtype)

    for load in indices:
        load.wait()

    @pl.loop(0, used)
    def _(g):
        copy(g).wait()
        for j in range(GROUP):
            slot = g * GROUP + j
            row = jnp.clip(rows_ref[0, 0, slot], 0, row_tiles - 1)
            col = jnp.clip(cols_ref[0, 0, slot], 0, out_tiles - 1)
            target = jnp.where(slot < count, col, out_tiles)
            total[target] += jnp.dot(
                grad_ref[row], held[slot], preferred_element_type=jnp.float32
            )

    @pl.loop(0, out_tiles)
    def _(t):
        for cut in range(cuts):
            out_ref[t * cuts + cut] = total[t, :, cut * CHUNK : (cut + 1) * CHUNK].astype(out_ref.dtype)


def tile_products(rows, cols, count, grad, tiles, out_tiles):
    slots, tile, _ = tiles.shape
    width = grad.shape[1]
    return pl.pallas_call(
        tile_kernel,
        out_shape=jax.ShapeDtypeStruct((out_tiles * tile // CHUNK, width, CHUNK), jnp.bfloat16),
        in_specs=[HBM, HBM, pl.BlockSpec(memory_space=pltpu.SMEM), VMEM, HBM],
        out_specs=VMEM,
        scratch_shapes=[
            pltpu.VMEM((slots, tile, tile), jnp.bfloat16),
            pltpu.VMEM((out_tiles + 1, width, tile), jnp.float32),
            pltpu.SMEM(rows.shape, rows.dtype),
            pltpu.SMEM(cols.shape, cols.dtype),
            pltpu.SemaphoreType.DMA((slots // GROUP,)),
            pltpu.SemaphoreType.DMA((2,)),
        ],
        compiler_params=pltpu.CompilerParams(vmem_limit_bytes=28 << 20),
        cost_estimate=pl.CostEstimate(
            flops=2 * slots * width * tile * tile,
            bytes_accessed=2 * slots * tile * tile,
            transcendentals=0,
        ),
        name="tile_products",
    )(rows, cols, count, grad, tiles)


def flow_kernel(
    part_all, weight_hbm, feat_hbm, gf_ref, gw_out,
    first, second, merged, half, y_in, whole, weight_raw, weight_ref, feat_ref, gw_ref, gw_send, mate_in,
    half_send, gw_in,
    load_sems, send_sems, recv_sems, gw_sems,
):
    width = part_all.shape[1]
    chunks, nodes_t = whole.shape[0], part_all.shape[2]
    loads = [
        pltpu.make_async_copy(weight_hbm, weight_raw, load_sems.at[0]),
        pltpu.make_async_copy(feat_hbm, feat_ref, load_sems.at[1]),
    ]
    for load in loads:
        load.start()
    row, col, fib = position()
    l, z = row // RING, lax.rem(row, RING)
    h, x = fib // RING, lax.rem(fib, RING)
    z_up, z_down, z_far = (lax.rem(z + d, RING) for d in (1, RING - 1, 2))
    x_up, x_down, x_far = (lax.rem(x + d, RING) for d in (1, RING - 1, 2))
    to_z_up, to_z_down = (l * RING + z_up, col, fib), (l * RING + z_down, col, fib)
    to_x_up, to_x_down = (row, col, h * RING + x_up), (row, col, h * RING + x_down)
    to_x_far = (row, col, h * RING + x_far)
    to_pair = ((1 - l) * RING + z, col, fib)
    to_cross = ((1 - l) * RING + z, col, (1 - h) * RING + x)
    to_far = (row, col, (1 - h) * RING + x)
    mate = (row, 1 - col, fib)
    peers = [(lax.rem(row + d, 8), col, fib) for d in range(1, 8)]
    greet([to_x_up, to_x_down, to_x_far, to_cross, to_far, mate, *peers])

    forwarded = chunks - DIRECT

    def part_at(to_l, to_z, t):
        return part_all.at[(to_l * RING + to_z) * chunks + t]

    def copy(kind, t, source, target, peer):
        return pltpu.make_async_remote_copy(
            source,
            target,
            send_sems.at[kind, t],
            recv_sems.at[kind, t],
            device_id=peer,
            device_id_type=MESH,
        )

    def link(kind, t):
        if kind == 0:
            return copy(0, t, part_at(0, z_far, t), first.at[0, t], to_z_up)
        if kind == 1:
            return copy(1, t, part_at(1, z_far, t), first.at[1, t], to_z_down)
        if kind == 2:
            return copy(2, t, part_at(1, z_up, t), second.at[0, t, 1], to_z_up)
        if kind == 3:
            return copy(3, t, part_at(0, z_down, t), second.at[1, t, 0], to_z_down)
        if kind == 4:
            return copy(4, t, merged.at[0, t], second.at[0, t, 0], to_z_up)
        if kind == 5:
            return copy(5, t, merged.at[1, t], second.at[1, t, 1], to_z_down)
        if kind == 6:
            return copy(6, t, half.at[t, 1 - l], y_in.at[0, t], to_pair)
        if kind == 7:
            return copy(7, t, half.at[t, 1 - l], y_in.at[1, t], to_cross)
        if kind == 8:
            return copy(8, t, half.at[t, l], y_in.at[2, t], to_far)
        if kind == 9:
            return copy(9, t, whole.at[t, x], whole.at[t, x], to_x_up)
        if kind == 10:
            return copy(10, t, whole.at[t, x], whole.at[t, x], to_x_down)
        if kind == 11:
            return copy(11, t, whole.at[t, x_down, 0], whole.at[t, x_down, 0], to_x_up)
        return copy(12, t, whole.at[t, x_up, 1], whole.at[t, x_up, 1], to_x_down)

    def arrived(kind, t):
        if kind == 9:
            slot = whole.at[t, x_down]
        elif kind == 10:
            slot = whole.at[t, x_up]
        elif kind == 11:
            slot = whole.at[t, x_far, 0]
        elif kind == 12:
            slot = whole.at[t, x_far, 1]
        else:
            link(kind, t).wait_recv()
            return
        copy(kind, t, slot, slot, to_pair).wait_recv()

    def added(*refs):
        terms = [r[...].astype(jnp.float32) for r in refs]
        return functools.reduce(lambda a, b: a + b, terms)

    gw_ref[...] = jnp.zeros_like(gw_ref)

    def settle_loads():
        for load in loads:
            load.wait()
        for k in range(2 * RING):
            source = (k % 2) * RING + k // 2
            weight_ref[:, k * width : (k + 1) * width] = weight_raw[:, source * width : (source + 1) * width]

    def send_shares(t):
        for kind in range(4):
            link(kind, t).start()

    def merge(t):
        arrived(0, t)
        merged[0, t] = added(part_at(0, z_up, t), first.at[0, t]).astype(merged.dtype)
        link(4, t).start()
        arrived(1, t)
        merged[1, t] = added(part_at(1, z_down, t), first.at[1, t]).astype(merged.dtype)
        link(5, t).start()

    def sum_over_z(t):
        for kind in (2, 3, 4, 5):
            arrived(kind, t)
        for to_l in range(2):
            half[t, to_l] = added(
                part_at(to_l, z, t), second.at[0, t, to_l], second.at[1, t, to_l]
            ).astype(half.dtype)
        for kind in (6, 7, 8):
            link(kind, t).start()

    def sum_over_y(t):
        for kind in (6, 7, 8):
            arrived(kind, t)
        whole[t, x, h] = added(half.at[t, l], y_in.at[0, t]).astype(whole.dtype)
        whole[t, x, 1 - h] = added(y_in.at[1, t], y_in.at[2, t]).astype(whole.dtype)
        link(9, t).start()
        link(10, t).start()

        @pl.when(t >= forwarded)
        def _():
            for side in range(2):
                block = whole.at[t, x, side]
                copy(11 + side, t, block, block, to_x_far).start()

    def forward(t):
        for kind in (9, 10):
            arrived(kind, t)

            @pl.when(t < forwarded)
            def _(kind=kind):
                link(kind + 2, t).start()

        @pl.when(t >= forwarded)
        def _():
            multiply(t)

    def multiply(t):
        arrived(11, t)
        arrived(12, t)

        @pl.when(lax.rem(t, 2) == 1)
        def _():
            depth = weight_ref.shape[1]
            panel = jnp.concatenate(
                [whole[t - 1].reshape(depth, nodes_t), whole[t].reshape(depth, nodes_t)], axis=1
            )
            part = pl.ds(pl.multiple_of((t - 1) * nodes_t, 2 * nodes_t), 2 * nodes_t)
            product = jnp.dot(weight_ref[...], panel, preferred_element_type=jnp.float32)
            gf_ref[part, :] = product.T.astype(gf_ref.dtype)
            gw_ref[...] += jnp.dot(panel, feat_ref[part, :], preferred_element_type=jnp.float32)

    stages = (send_shares, merge, sum_over_z, sum_over_y, forward, multiply)

    settle_loads()

    @pl.loop(0, chunks + LAGS[-2])
    def _(step):
        for late, stage in zip(LAGS, stages):
            t = step - late

            @pl.when((t >= 0) & (t < (forwarded if stage is multiply else chunks)))
            def _(stage=stage, t=t):
                stage(t)

    span = gw_ref.shape[0] // 2
    rows = span // 8

    def piece(ref, of_row, size=rows):
        return ref.at[pl.ds(pl.multiple_of(of_row, size), size)]

    def gw_copy(phase, d, source, target, peer):
        return pltpu.make_async_remote_copy(
            source, target, gw_sems.at[phase, 0, d], gw_sems.at[phase, 1, d], device_id=peer, device_id_type=MESH
        )

    gw_send[...] = gw_ref[...].astype(gw_send.dtype)
    gives = [gw_copy(0, 0, piece(gw_send, (1 - col) * span, span), mate_in, mate)]
    gives[0].start()
    gives[0].wait_recv()
    mine = gw_ref[pl.ds(pl.multiple_of(col * span, span), span), :] + mate_in[...].astype(jnp.float32)
    gw_ref[0:span, :] = mine
    half_send[...] = mine.astype(half_send.dtype)
    for d in range(1, 8):
        to = lax.rem(row + d, 8)
        gives.append(gw_copy(1, d, piece(half_send, to * rows), gw_in.at[d], peers[d - 1]))
        gives[-1].start()
    own = gw_ref[pl.ds(pl.multiple_of(row * rows, rows), rows), :]
    for d in range(1, 8):
        gives[d].wait_recv()
        own += gw_in[d].astype(jnp.float32)
    here = col * span + row * rows
    gw_out[pl.ds(pl.multiple_of(here, rows), rows), :] = own.astype(gw_out.dtype)
    for d in range(1, 8):
        gives.append(gw_copy(2, d, piece(gw_out, here), piece(gw_out, here), peers[d - 1]))
        gives[-1].start()

    @pl.loop(0, chunks)
    def _(t):
        for kind in range(13):
            link(kind, t).wait_send()

    for d in range(1, 8):
        slot = piece(gw_out, col * span + lax.rem(row + 8 - d, 8) * rows)
        gw_copy(2, d, slot, slot, peers[d - 1]).wait_recv()
    final = piece(gw_out, col * span, span)
    gives.append(gw_copy(0, 1, final, final, mate))
    gives[-1].start()
    slot = piece(gw_out, (1 - col) * span, span)
    gw_copy(0, 1, slot, slot, mate).wait_recv()
    for give in gives:
        give.wait_send()


def flow(part, weight, features):
    _, width, cut = part.shape
    nodes, whole = features.shape[0], weight.shape[1]
    chunks = nodes // cut
    piece = (width, cut)
    sixteen = jnp.bfloat16
    return pl.pallas_call(
        flow_kernel,
        out_shape=(
            jax.ShapeDtypeStruct((nodes, width), sixteen),
            jax.ShapeDtypeStruct((whole, width), sixteen),
        ),
        in_specs=[VMEM, HBM, HBM],
        out_specs=(VMEM, VMEM),
        scratch_shapes=[
            pltpu.VMEM((2, chunks, *piece), sixteen),
            pltpu.VMEM((2, chunks, 2, *piece), sixteen),
            pltpu.VMEM((2, chunks, *piece), sixteen),
            pltpu.VMEM((chunks, 2, *piece), sixteen),
            pltpu.VMEM((3, chunks, *piece), sixteen),
            pltpu.VMEM((chunks, RING, 2, *piece), sixteen),
            pltpu.VMEM(weight.shape, sixteen),
            pltpu.VMEM(weight.shape, sixteen),
            pltpu.VMEM(features.shape, sixteen),
            pltpu.VMEM((whole, width), jnp.float32),
            pltpu.VMEM((whole, width), sixteen),
            pltpu.VMEM((whole // 2, width), sixteen),
            pltpu.VMEM((whole // 2, width), sixteen),
            pltpu.VMEM((8, whole // 16, width), sixteen),
            pltpu.SemaphoreType.DMA((2,)),
            pltpu.SemaphoreType.DMA((13, chunks)),
            pltpu.SemaphoreType.DMA((13, chunks)),
            pltpu.SemaphoreType.DMA((3, 2, 8)),
        ],
        compiler_params=pltpu.CompilerParams(
            collective_id=1, has_side_effects=True, vmem_limit_bytes=20 << 20
        ),
        cost_estimate=pl.CostEstimate(
            flops=4 * nodes * width * whole, bytes_accessed=16 << 20, transcendentals=0
        ),
        name="flow",
    )(part, weight, features)


def finish_kernel(gf_ref, gw_ref, gf_hbm, gw_hbm, gw_turned, sems):
    width = gw_turned.shape[0]
    write_gf = pltpu.make_async_copy(gf_ref, gf_hbm, sems.at[0])
    write_gf.start()
    for k in range(2 * RING):
        target = (k % 2) * RING + k // 2
        block = gw_ref[k * width : (k + 1) * width, :].astype(jnp.float32)
        gw_turned[:, target * width : (target + 1) * width] = block.T
    write_gw = pltpu.make_async_copy(gw_turned, gw_hbm, sems.at[1])
    write_gw.start()
    write_gf.wait()
    write_gw.wait()


def finish(gf, gw):
    turned = gw.shape[::-1]
    return pl.pallas_call(
        finish_kernel,
        out_shape=(
            jax.ShapeDtypeStruct(gf.shape, gf.dtype),
            jax.ShapeDtypeStruct(turned, jnp.float32),
        ),
        in_specs=[VMEM, VMEM],
        out_specs=(HBM, HBM),
        scratch_shapes=[pltpu.VMEM(turned, jnp.float32), pltpu.SemaphoreType.DMA((2,))],
        compiler_params=pltpu.CompilerParams(vmem_limit_bytes=4 << 20),
        cost_estimate=pl.CostEstimate(flops=0, bytes_accessed=1 << 20, transcendentals=0),
        name="finish",
    )(gf, gw)


def on_device(features, pre_activation, out_grad, weight, tiles, rows, cols, counts):
    tile = tiles.shape[-1]
    features, pre_activation, out_grad, weight, tiles, rows, cols = (
        pltpu.with_memory_space_constraint(a, pltpu.HBM)
        for a in (features, pre_activation, out_grad, weight, tiles[0, 0], rows, cols)
    )
    grad = local_grads(pre_activation, out_grad, tile)
    part = tile_products(rows, cols, counts, grad, tiles, 8 * (features.shape[0] // tile))
    return finish(*flow(part, weight, features))


def solution(mesh):
    in_specs = (
        P(("row", "col"), "fib"),
        P(("row", "col"), "fib"),
        P(("row", "col"), "fib"),
        P("fib", None),
        P("row", "col", None, None, None),
        P("row", "col", None),
        P("row", "col", None),
        P("row", "col"),
    )
    out_specs = (P(("row", "col"), "fib"), P("fib", None))
    return jax.shard_map(
        on_device, mesh=mesh, in_specs=in_specs, out_specs=out_specs, check_vma=False
    )
```

```python
import functools

import jax
import jax.numpy as jnp
from jax import lax
from jax.experimental import pallas as pl
from jax.experimental.pallas import tpu as pltpu
from jax.sharding import PartitionSpec as P

GROUP = 8
RING = 4
LAGS = (0, 2, 4, 6)
MESH = pl.DeviceIdType.MESH
VMEM = pl.BlockSpec(memory_space=pltpu.VMEM)
HBM = pl.BlockSpec(memory_space=pltpu.HBM)
CHUNK = 128


def greet(peers):
    barrier = pltpu.get_barrier_semaphore()
    for peer in peers:
        pl.semaphore_signal(barrier, inc=1, device_id=peer, device_id_type=MESH)
    pl.semaphore_wait(barrier, len(peers))


def position():
    return lax.axis_index("row"), lax.axis_index("col"), lax.axis_index("fib")


def grad_kernel(
    pre_hbm, out_grad_hbm, grad_ref, pre_ref, out_grad_ref, load_sems, send_sems, recv_sems
):
    row, col, fib = position()
    own_tiles = grad_ref.shape[0] // 2
    tile = grad_ref.shape[2]
    partner = (row, 1 - col, fib)

    def loads(t):
        part = pl.ds(pl.multiple_of(t * tile, tile), tile)
        return (
            pltpu.make_async_copy(pre_hbm.at[part], pre_ref.at[part], load_sems.at[0, t]),
            pltpu.make_async_copy(out_grad_hbm.at[part], out_grad_ref.at[part], load_sems.at[1, t]),
        )

    @pl.loop(0, own_tiles)
    def _(t):
        for load in loads(t):
            load.start()

    greet([partner])

    def copy(t, owner):
        slot = grad_ref.at[owner * own_tiles + t]
        return pltpu.make_async_remote_copy(
            slot, slot, send_sems.at[t], recv_sems.at[t], device_id=partner, device_id_type=MESH
        )

    @pl.loop(0, own_tiles)
    def _(t):
        for load in loads(t):
            load.wait()
        part = pl.ds(pl.multiple_of(t * tile, tile), tile)
        pre = pre_ref[part, :].astype(jnp.float32)
        sigmoid = jax.nn.sigmoid(pre)
        grad = out_grad_ref[part, :].astype(jnp.float32) * sigmoid * (1.0 + pre * (1.0 - sigmoid))
        grad_ref[col * own_tiles + t] = grad.T.astype(grad_ref.dtype)
        copy(t, col).start()

    @pl.loop(0, own_tiles)
    def _(t):
        copy(t, col).wait_send()
        copy(t, 1 - col).wait_recv()


def local_grads(pre, out_grad, tile):
    nodes, width = pre.shape
    own_tiles = nodes // tile
    return pl.pallas_call(
        grad_kernel,
        out_shape=jax.ShapeDtypeStruct((2 * own_tiles, width, tile), jnp.bfloat16),
        in_specs=[HBM, HBM],
        out_specs=VMEM,
        scratch_shapes=[
            pltpu.VMEM(pre.shape, pre.dtype),
            pltpu.VMEM(pre.shape, pre.dtype),
            pltpu.SemaphoreType.DMA((2, own_tiles)),
            pltpu.SemaphoreType.DMA((own_tiles,)),
            pltpu.SemaphoreType.DMA((own_tiles,)),
        ],
        compiler_params=pltpu.CompilerParams(
            collective_id=0, has_side_effects=True, vmem_limit_bytes=8 << 20
        ),
        cost_estimate=pl.CostEstimate(
            flops=10 * nodes * width, bytes_accessed=8 * nodes * width, transcendentals=nodes * width
        ),
        name="local_grads",
    )(pre, out_grad)


def tile_kernel(
    rows_hbm, cols_hbm, count_ref, grad_ref, tiles_ref, out_ref,
    held, total, rows_ref, cols_ref, sems, index_sems,
):
    slots, tile, _ = tiles_ref.shape
    cuts = tile // CHUNK
    out_tiles = out_ref.shape[0] // cuts
    row_tiles = grad_ref.shape[0]
    def copy(g):
        part = pl.ds(g * GROUP, GROUP)
        return pltpu.make_async_copy(tiles_ref.at[part], held.at[part], sems.at[g])

    indices = [
        pltpu.make_async_copy(source, target, index_sems.at[i])
        for i, (source, target) in enumerate(
            ((rows_hbm, rows_ref), (cols_hbm, cols_ref))
        )
    ]
    for load in indices:
        load.start()
    count = jnp.clip(count_ref[0, 0], 1, slots)
    used = (count + GROUP - 1) // GROUP

    @pl.loop(0, used)
    def _(g):
        copy(g).start()

    @pl.loop(0, out_tiles + 1)
    def _(t):
        total[t] = jnp.zeros(total.shape[1:], total.dtype)

    for load in indices:
        load.wait()

    @pl.loop(0, used)
    def _(g):
        copy(g).wait()
        for j in range(GROUP):
            slot = g * GROUP + j
            row = jnp.clip(rows_ref[0, 0, slot], 0, row_tiles - 1)
            col = jnp.clip(cols_ref[0, 0, slot], 0, out_tiles - 1)
            target = jnp.where(slot < count, col, out_tiles)
            total[target] += jnp.dot(
                grad_ref[row], held[slot], preferred_element_type=jnp.float32
            )

    @pl.loop(0, out_tiles)
    def _(t):
        for cut in range(cuts):
            out_ref[t * cuts + cut] = total[t, :, cut * CHUNK : (cut + 1) * CHUNK].astype(out_ref.dtype)


def tile_products(rows, cols, count, grad, tiles, out_tiles):
    slots, tile, _ = tiles.shape
    width = grad.shape[1]
    return pl.pallas_call(
        tile_kernel,
        out_shape=jax.ShapeDtypeStruct((out_tiles * tile // CHUNK, width, CHUNK), jnp.bfloat16),
        in_specs=[HBM, HBM, pl.BlockSpec(memory_space=pltpu.SMEM), VMEM, HBM],
        out_specs=VMEM,
        scratch_shapes=[
            pltpu.VMEM((slots, tile, tile), jnp.bfloat16),
            pltpu.VMEM((out_tiles + 1, width, tile), jnp.float32),
            pltpu.SMEM(rows.shape, rows.dtype),
            pltpu.SMEM(cols.shape, cols.dtype),
            pltpu.SemaphoreType.DMA((slots // GROUP,)),
            pltpu.SemaphoreType.DMA((2,)),
        ],
        compiler_params=pltpu.CompilerParams(vmem_limit_bytes=28 << 20),
        cost_estimate=pl.CostEstimate(
            flops=2 * slots * width * tile * tile,
            bytes_accessed=2 * slots * tile * tile,
            transcendentals=0,
        ),
        name="tile_products",
    )(rows, cols, count, grad, tiles)


def flow_kernel(
    part_all, weight_hbm, feat_hbm, gf_ref, gw_out,
    first, second, merged, half, y_in, whole, weight_raw, weight_send, weight_in, feat,
    gf_own, gf_send, gf_in, gw_ref, gw_send, mate_in, row_send, row_in, x_send,
    load_sems, send_sems, recv_sems, x_sems, gw_sems,
):
    row, col, fib = position()
    l, z = row // RING, lax.rem(row, RING)
    h, x = fib // RING, lax.rem(fib, RING)
    chunks, width, nodes_t = whole.shape[1:]
    pairs, span_t = chunks // 2, 2 * nodes_t
    z_up, z_down, z_far = (lax.rem(z + d, RING) for d in (1, RING - 1, 2))
    to_z_up, to_z_down = (l * RING + z_up, col, fib), (l * RING + z_down, col, fib)
    to_x = [(row, col, h * RING + lax.rem(x + d, RING)) for d in range(RING)]
    to_pair = ((1 - l) * RING + z, col, fib)
    to_cross = ((1 - l) * RING + z, col, (1 - h) * RING + x)
    to_far = (row, col, (1 - h) * RING + x)
    mate = (row, 1 - col, fib)
    peers = [(lax.rem(row + d, 8), col, fib) for d in range(1, 8)]

    def nodes_of(p):
        return pl.ds(pl.multiple_of(p * span_t, span_t), span_t)

    load_weight = [
        pltpu.make_async_copy(
            weight_hbm.at[:, k * width : (k + 1) * width], weight_raw.at[k], load_sems.at[1 + k]
        )
        for k in range(2 * RING)
    ]
    load_feat = pltpu.make_async_copy(feat_hbm, feat.at[0], load_sems.at[0])
    for load in load_weight:
        load.start()
    load_feat.start()
    greet([*to_x[1:], to_cross, to_far, mate, *peers])

    def part_at(to_l, to_z, t):
        return part_all.at[(to_l * RING + to_z) * chunks + t]

    def copy(kind, t, source, target, peer):
        return pltpu.make_async_remote_copy(
            source, target, send_sems.at[kind, t], recv_sems.at[kind, t], device_id=peer, device_id_type=MESH
        )

    def link(kind, t):
        if kind == 0:
            return copy(0, t, part_at(0, z_far, t), first.at[0, t], to_z_up)
        if kind == 1:
            return copy(1, t, part_at(1, z_far, t), first.at[1, t], to_z_down)
        if kind == 2:
            return copy(2, t, part_at(1, z_up, t), second.at[0, t, 1], to_z_up)
        if kind == 3:
            return copy(3, t, part_at(0, z_down, t), second.at[1, t, 0], to_z_down)
        if kind == 4:
            return copy(4, t, merged.at[0, t], second.at[0, t, 0], to_z_up)
        if kind == 5:
            return copy(5, t, merged.at[1, t], second.at[1, t, 1], to_z_down)
        if kind == 6:
            return copy(6, t, half.at[t, 1 - l], y_in.at[0, t], to_pair)
        if kind == 7:
            return copy(7, t, half.at[t, 1 - l], y_in.at[1, t], to_cross)
        return copy(8, t, half.at[t, l], y_in.at[2, t], to_far)

    def along_x(kind, d, p, source, target):
        return pltpu.make_async_remote_copy(
            source, target, x_sems.at[0, kind, d, p], x_sems.at[1, kind, d, p], device_id=to_x[d], device_id_type=MESH
        )

    def feat_copy(d, p):
        return along_x(0, d, p, feat.at[0, nodes_of(p)], feat.at[RING - d, nodes_of(p)])

    def gf_copy(d, p):
        return along_x(1, d, p, gf_send.at[d - 1, p], gf_in.at[d - 1, p])

    def weight_copy(d):
        return along_x(2, d, 0, weight_send.at[d - 1], weight_in.at[RING - d])

    def added(*refs):
        terms = [r[...].astype(jnp.float32) for r in refs]
        return functools.reduce(lambda a, b: a + b, terms)

    def send_shares(t):
        for kind in range(4):
            link(kind, t).start()

        @pl.when(t == 0)
        def _():
            for load in load_weight:
                load.wait()
            for d in range(RING):
                at = lax.rem(x + d, RING)
                block = jnp.concatenate([weight_raw[at], weight_raw[RING + at]], axis=1)
                if d == 0:
                    weight_in[0] = block
                else:
                    weight_send[d - 1] = block
                    weight_copy(d).start()
            gw_ref[...] = jnp.zeros_like(gw_ref)
            load_feat.wait()

        @pl.when(t < pairs)
        def _():
            for d in range(1, RING):
                feat_copy(d, t).start()

    def merge(t):
        link(0, t).wait_recv()
        merged[0, t] = added(part_at(0, z_up, t), first.at[0, t]).astype(merged.dtype)
        link(4, t).start()
        link(1, t).wait_recv()
        merged[1, t] = added(part_at(1, z_down, t), first.at[1, t]).astype(merged.dtype)
        link(5, t).start()

    def sum_over_z(t):
        for kind in (2, 3, 4, 5):
            link(kind, t).wait_recv()
        for to_l in range(2):
            half[t, to_l] = added(
                part_at(to_l, z, t), second.at[0, t, to_l], second.at[1, t, to_l]
            ).astype(half.dtype)
        for kind in (6, 7, 8):
            link(kind, t).start()

    def sum_over_y(t):
        for kind in (6, 7, 8):
            link(kind, t).wait_recv()
        whole[h, t] = added(half.at[t, l], y_in.at[0, t]).astype(whole.dtype)
        whole[1 - h, t] = added(y_in.at[1, t], y_in.at[2, t]).astype(whole.dtype)

        @pl.when(lax.rem(t, 2) == 1)
        def _():
            multiply(lax.div(t, 2))

    def multiply(p):
        @pl.when(p == 0)
        def _():
            for d in range(1, RING):
                weight_copy(d).wait_recv()

        panel = jnp.concatenate(
            [whole[:, 2 * p].reshape(2 * width, nodes_t), whole[:, 2 * p + 1].reshape(2 * width, nodes_t)], axis=1
        )
        for d in range(1, RING):
            feat_copy(d, p).wait_recv()
        beside = jnp.concatenate([feat[d, nodes_of(p), :] for d in range(RING)], axis=1)
        gw_ref[...] += jnp.dot(panel, beside, preferred_element_type=jnp.float32)
        for d in (2, 1, 3, 0):
            block = jnp.dot(weight_in[d], panel, preferred_element_type=jnp.float32)
            if d == 0:
                gf_own[p] = block
            else:
                gf_send[d - 1, p] = block.astype(gf_send.dtype)
                gf_copy(d, p).start()

    def collect(p):
        for d in range(1, RING):
            gf_copy(d, p).wait_recv()
        block = gf_own[p] + added(*[gf_in.at[d - 1, p] for d in range(1, RING)])
        gf_ref[nodes_of(p), :] = block.T.astype(gf_ref.dtype)

    stages = (send_shares, merge, sum_over_z, sum_over_y)

    @pl.loop(0, chunks + LAGS[-1])
    def _(step):
        for late, stage in zip(LAGS, stages):
            t = step - late

            @pl.when((t >= 0) & (t < chunks))
            def _(stage=stage, t=t):
                stage(t)

    rows = width // 8

    def gw_copy(phase, d, source, target, peer):
        return pltpu.make_async_remote_copy(
            source, target, gw_sems.at[phase, 0, d], gw_sems.at[phase, 1, d], device_id=peer, device_id_type=MESH
        )

    def piece(ref, of, size=rows):
        return ref.at[pl.ds(pl.multiple_of(of * size, size), size)]

    gw_send[...] = gw_ref[pl.ds(pl.multiple_of((1 - col) * width, width), width), :].astype(gw_send.dtype)
    gives = [gw_copy(0, 0, gw_send, mate_in, mate)]
    gives[0].start()
    gives[0].wait_recv()
    mine = gw_ref[pl.ds(pl.multiple_of(col * width, width), width), :] + mate_in[...].astype(jnp.float32)
    gw_ref[0:width, :] = mine
    row_send[...] = mine.astype(row_send.dtype)
    for d in range(1, 8):
        gives.append(gw_copy(1, d, piece(row_send, lax.rem(row + d, 8)), row_in.at[d], peers[d - 1]))
        gives[-1].start()

    @pl.loop(0, pairs // 2)
    def _(p):
        collect(p)

    own = gw_ref[pl.ds(pl.multiple_of(row * rows, rows), rows), :]
    for d in range(1, 8):
        gives[d].wait_recv()
        own += row_in[d].astype(jnp.float32)
    for d in range(RING):
        block = own[:, d * width : (d + 1) * width].astype(gw_out.dtype)
        if d == 0:
            gw_out[col, row, x] = block
        else:
            x_send[d] = block
            gives.append(gw_copy(2, d, x_send.at[d], gw_out.at[col, row, x], to_x[d]))
            gives[-1].start()

    @pl.loop(pairs // 2, pairs)
    def _(p):
        collect(p)

    for d in range(1, RING):
        slot = gw_out.at[col, row, lax.rem(x + RING - d, RING)]
        gw_copy(2, d, slot, slot, to_x[d]).wait_recv()
    for d in range(1, 8):
        gives.append(gw_copy(3, d, gw_out.at[col, row], gw_out.at[col, row], peers[d - 1]))
        gives[-1].start()

    @pl.loop(0, chunks)
    def _(t):
        for kind in range(9):
            link(kind, t).wait_send()

    @pl.loop(0, pairs)
    def _(p):
        for d in range(1, RING):
            feat_copy(d, p).wait_send()
            gf_copy(d, p).wait_send()

    for d in range(1, RING):
        weight_copy(d).wait_send()
    for d in range(1, 8):
        slot = gw_out.at[col, lax.rem(row + 8 - d, 8)]
        gw_copy(3, d, slot, slot, peers[d - 1]).wait_recv()
    gives.append(gw_copy(0, 1, gw_out.at[col], gw_out.at[col], mate))
    gives[-1].start()
    slot = gw_out.at[1 - col]
    gw_copy(0, 1, slot, slot, mate).wait_recv()
    for give in gives:
        give.wait_send()


def flow(part, weight, features):
    _, width, cut = part.shape
    nodes = features.shape[0]
    chunks = nodes // cut
    pairs = chunks // 2
    piece = (width, cut)
    block = (width, 2 * cut)
    sixteen = jnp.bfloat16
    rows = width // 8
    return pl.pallas_call(
        flow_kernel,
        out_shape=(
            jax.ShapeDtypeStruct((nodes, width), sixteen),
            jax.ShapeDtypeStruct((2, 8, RING, rows, width), sixteen),
        ),
        in_specs=[VMEM, HBM, HBM],
        out_specs=(VMEM, VMEM),
        scratch_shapes=[
            pltpu.VMEM((2, chunks, *piece), sixteen),
            pltpu.VMEM((2, chunks, 2, *piece), sixteen),
            pltpu.VMEM((2, chunks, *piece), sixteen),
            pltpu.VMEM((chunks, 2, *piece), sixteen),
            pltpu.VMEM((3, chunks, *piece), sixteen),
            pltpu.VMEM((2, chunks, *piece), sixteen),
            pltpu.VMEM((2 * RING, width, width), sixteen),
            pltpu.VMEM((RING - 1, width, 2 * width), sixteen),
            pltpu.VMEM((RING, width, 2 * width), sixteen),
            pltpu.VMEM((RING, nodes, width), sixteen),
            pltpu.VMEM((pairs, *block), jnp.float32),
            pltpu.VMEM((RING - 1, pairs, *block), sixteen),
            pltpu.VMEM((RING - 1, pairs, *block), sixteen),
            pltpu.VMEM((2 * width, RING * width), jnp.float32),
            pltpu.VMEM((width, RING * width), sixteen),
            pltpu.VMEM((width, RING * width), sixteen),
            pltpu.VMEM((width, RING * width), sixteen),
            pltpu.VMEM((8, rows, RING * width), sixteen),
            pltpu.VMEM((RING, rows, width), sixteen),
            pltpu.SemaphoreType.DMA((1 + 2 * RING,)),
            pltpu.SemaphoreType.DMA((9, chunks)),
            pltpu.SemaphoreType.DMA((9, chunks)),
            pltpu.SemaphoreType.DMA((2, 3, RING, pairs)),
            pltpu.SemaphoreType.DMA((4, 2, 8)),
        ],
        compiler_params=pltpu.CompilerParams(
            collective_id=1, has_side_effects=True, vmem_limit_bytes=24 << 20
        ),
        cost_estimate=pl.CostEstimate(
            flops=32 * nodes * width * width, bytes_accessed=16 << 20, transcendentals=0
        ),
        name="flow",
    )(part, weight, features)


def finish_kernel(gf_ref, gw_ref, gf_hbm, gw_hbm, gw_turned, sems):
    width = gw_turned.shape[0]
    write_gf = pltpu.make_async_copy(gf_ref, gf_hbm, sems.at[0])
    write_gf.start()
    for side in range(2):
        for x in range(RING):
            target = side * RING + x
            block = gw_ref[side, :, x].reshape(width, width).astype(jnp.float32)
            gw_turned[:, target * width : (target + 1) * width] = block.T
    write_gw = pltpu.make_async_copy(gw_turned, gw_hbm, sems.at[1])
    write_gw.start()
    write_gf.wait()
    write_gw.wait()


def finish(gf, gw):
    width = gf.shape[1]
    turned = (width, 2 * RING * width)
    return pl.pallas_call(
        finish_kernel,
        out_shape=(
            jax.ShapeDtypeStruct(gf.shape, gf.dtype),
            jax.ShapeDtypeStruct(turned, jnp.float32),
        ),
        in_specs=[VMEM, VMEM],
        out_specs=(HBM, HBM),
        scratch_shapes=[pltpu.VMEM(turned, jnp.float32), pltpu.SemaphoreType.DMA((2,))],
        compiler_params=pltpu.CompilerParams(vmem_limit_bytes=4 << 20),
        cost_estimate=pl.CostEstimate(flops=0, bytes_accessed=1 << 20, transcendentals=0),
        name="finish",
    )(gf, gw)


def on_device(features, pre_activation, out_grad, weight, tiles, rows, cols, counts):
    tile = tiles.shape[-1]
    features, pre_activation, out_grad, weight, tiles, rows, cols = (
        pltpu.with_memory_space_constraint(a, pltpu.HBM)
        for a in (features, pre_activation, out_grad, weight, tiles[0, 0], rows, cols)
    )
    grad = local_grads(pre_activation, out_grad, tile)
    part = tile_products(rows, cols, counts, grad, tiles, 8 * (features.shape[0] // tile))
    return finish(*flow(part, weight, features))


def solution(mesh):
    in_specs = (
        P(("row", "col"), "fib"),
        P(("row", "col"), "fib"),
        P(("row", "col"), "fib"),
        P("fib", None),
        P("row", "col", None, None, None),
        P("row", "col", None),
        P("row", "col", None),
        P("row", "col"),
    )
    out_specs = (P(("row", "col"), "fib"), P("fib", None))
    return jax.shard_map(
        on_device, mesh=mesh, in_specs=in_specs, out_specs=out_specs, check_vma=False
    )
```

```python
import functools

import jax
import jax.numpy as jnp
from jax import lax
from jax.experimental import pallas as pl
from jax.experimental.pallas import tpu as pltpu
from jax.sharding import PartitionSpec as P

GROUP = 8
EARLY = 64
RING = 4
LAGS = (0, 2, 4, 6)
MESH = pl.DeviceIdType.MESH
VMEM = pl.BlockSpec(memory_space=pltpu.VMEM)
HBM = pl.BlockSpec(memory_space=pltpu.HBM)
CHUNK = 128
LATE = 4


def greet(peers):
    barrier = pltpu.get_barrier_semaphore()
    for peer in peers:
        pl.semaphore_signal(barrier, inc=1, device_id=peer, device_id_type=MESH)
    pl.semaphore_wait(barrier, len(peers))


def position():
    return lax.axis_index("row"), lax.axis_index("col"), lax.axis_index("fib")


def grad_kernel(
    pre_hbm, out_grad_hbm, tiles_hbm, grad_ref, early_ref,
    pre_ref, out_grad_ref, load_sems, tile_sems, send_sems, recv_sems,
):
    row, col, fib = position()
    own_tiles = grad_ref.shape[0] // 2
    tile = grad_ref.shape[2]
    partner = (row, 1 - col, fib)

    def loads(t):
        part = pl.ds(pl.multiple_of(t * tile, tile), tile)
        return (
            pltpu.make_async_copy(pre_hbm.at[part], pre_ref.at[part], load_sems.at[0, t]),
            pltpu.make_async_copy(out_grad_hbm.at[part], out_grad_ref.at[part], load_sems.at[1, t]),
        )

    @pl.loop(0, own_tiles)
    def _(t):
        for load in loads(t):
            load.start()

    def early(g):
        group = pl.ds(g * GROUP, GROUP)
        return pltpu.make_async_copy(tiles_hbm.at[group], early_ref.at[group], tile_sems.at[g])

    @pl.loop(0, EARLY // GROUP)
    def _(g):
        early(g).start()

    greet([partner])

    def copy(t, owner):
        slot = grad_ref.at[owner * own_tiles + t]
        return pltpu.make_async_remote_copy(
            slot, slot, send_sems.at[t], recv_sems.at[t], device_id=partner, device_id_type=MESH
        )

    @pl.loop(0, own_tiles)
    def _(t):
        for load in loads(t):
            load.wait()
        part = pl.ds(pl.multiple_of(t * tile, tile), tile)
        pre = pre_ref[part, :].astype(jnp.float32)
        sigmoid = jax.nn.sigmoid(pre)
        grad = out_grad_ref[part, :].astype(jnp.float32) * sigmoid * (1.0 + pre * (1.0 - sigmoid))
        grad_ref[col * own_tiles + t] = grad.T.astype(grad_ref.dtype)
        copy(t, col).start()

    @pl.loop(0, own_tiles)
    def _(t):
        copy(t, col).wait_send()
        copy(t, 1 - col).wait_recv()

    @pl.loop(0, EARLY // GROUP)
    def _(g):
        early(g).wait()


def local_grads(pre, out_grad, tiles):
    nodes, width = pre.shape
    tile = tiles.shape[1]
    own_tiles = nodes // tile
    return pl.pallas_call(
        grad_kernel,
        out_shape=(
            jax.ShapeDtypeStruct((2 * own_tiles, width, tile), jnp.bfloat16),
            jax.ShapeDtypeStruct((EARLY, tile, tile), tiles.dtype),
        ),
        in_specs=[HBM, HBM, HBM],
        out_specs=(VMEM, VMEM),
        scratch_shapes=[
            pltpu.VMEM(pre.shape, pre.dtype),
            pltpu.VMEM(pre.shape, pre.dtype),
            pltpu.SemaphoreType.DMA((2, own_tiles)),
            pltpu.SemaphoreType.DMA((EARLY // GROUP,)),
            pltpu.SemaphoreType.DMA((own_tiles,)),
            pltpu.SemaphoreType.DMA((own_tiles,)),
        ],
        compiler_params=pltpu.CompilerParams(
            collective_id=0, has_side_effects=True, vmem_limit_bytes=16 << 20
        ),
        cost_estimate=pl.CostEstimate(
            flops=10 * nodes * width, bytes_accessed=8 * nodes * width, transcendentals=nodes * width
        ),
        name="local_grads",
    )(pre, out_grad, tiles)


def tile_kernel(
    rows_hbm, cols_hbm, count_ref, grad_ref, early_ref, tiles_ref, out_ref,
    held, total, rows_ref, cols_ref, sems, index_sems,
):
    slots, tile, _ = tiles_ref.shape
    cuts = tile // CHUNK
    out_tiles = out_ref.shape[0] // cuts
    row_tiles = grad_ref.shape[0]
    def copy(g):
        source = tiles_ref.at[pl.ds(g * GROUP, GROUP)]
        return pltpu.make_async_copy(
            source, held.at[pl.ds(g * GROUP - EARLY, GROUP)], sems.at[g - EARLY // GROUP]
        )

    indices = [
        pltpu.make_async_copy(source, target, index_sems.at[i])
        for i, (source, target) in enumerate(
            ((rows_hbm, rows_ref), (cols_hbm, cols_ref))
        )
    ]
    for load in indices:
        load.start()
    count = jnp.clip(count_ref[0, 0], 1, slots)
    used = (count + GROUP - 1) // GROUP

    @pl.loop(EARLY // GROUP, used)
    def _(g):
        copy(g).start()

    @pl.loop(0, out_tiles + 1)
    def _(t):
        total[t] = jnp.zeros(total.shape[1:], total.dtype)

    for load in indices:
        load.wait()

    def add_group(g, tile_at):
        for j in range(GROUP):
            slot = g * GROUP + j
            row = jnp.clip(rows_ref[0, 0, slot], 0, row_tiles - 1)
            col = jnp.clip(cols_ref[0, 0, slot], 0, out_tiles - 1)
            target = jnp.where(slot < count, col, out_tiles)
            total[target] += jnp.dot(grad_ref[row], tile_at(slot), preferred_element_type=jnp.float32)

    @pl.loop(0, jnp.minimum(used, EARLY // GROUP))
    def _(g):
        add_group(g, lambda slot: early_ref[slot])

    @pl.loop(EARLY // GROUP, used)
    def _(g):
        copy(g).wait()
        add_group(g, lambda slot: held[slot - EARLY])

    @pl.loop(0, out_tiles)
    def _(t):
        for cut in range(cuts):
            out_ref[t * cuts + cut] = total[t, :, cut * CHUNK : (cut + 1) * CHUNK].astype(out_ref.dtype)


def tile_products(rows, cols, count, grad, early, tiles, out_tiles):
    slots, tile, _ = tiles.shape
    width = grad.shape[1]
    return pl.pallas_call(
        tile_kernel,
        out_shape=jax.ShapeDtypeStruct((out_tiles * tile // CHUNK, width, CHUNK), jnp.bfloat16),
        in_specs=[HBM, HBM, pl.BlockSpec(memory_space=pltpu.SMEM), VMEM, VMEM, HBM],
        out_specs=VMEM,
        scratch_shapes=[
            pltpu.VMEM((slots - EARLY, tile, tile), jnp.bfloat16),
            pltpu.VMEM((out_tiles + 1, width, tile), jnp.float32),
            pltpu.SMEM(rows.shape, rows.dtype),
            pltpu.SMEM(cols.shape, cols.dtype),
            pltpu.SemaphoreType.DMA(((slots - EARLY) // GROUP,)),
            pltpu.SemaphoreType.DMA((2,)),
        ],
        compiler_params=pltpu.CompilerParams(vmem_limit_bytes=28 << 20),
        cost_estimate=pl.CostEstimate(
            flops=2 * slots * width * tile * tile,
            bytes_accessed=2 * slots * tile * tile,
            transcendentals=0,
        ),
        name="tile_products",
    )(rows, cols, count, grad, early, tiles)


def flow_kernel(
    part_all, weight_hbm, feat_hbm, gf_ref, gw_out,
    first, second, merged, half, y_in, late_in, late, whole, weight_raw, weight_send, weight_in, feat,
    gf_own, gf_send, gf_in, gw_ref, gw_send, mate_in, row_send, row_in, x_send,
    load_sems, send_sems, recv_sems, x_sems, late_sems, gw_sems,
):
    row, col, fib = position()
    l, z = row // RING, lax.rem(row, RING)
    h, x = fib // RING, lax.rem(fib, RING)
    chunks, width, nodes_t = whole.shape[1:]
    pairs, span_t = chunks // 2, 2 * nodes_t
    split = chunks - LATE
    units = split + LATE // 2
    z_up, z_down, z_far = (lax.rem(z + d, RING) for d in (1, RING - 1, 2))
    to_z_up, to_z_down = (l * RING + z_up, col, fib), (l * RING + z_down, col, fib)
    to_x = [(row, col, h * RING + lax.rem(x + d, RING)) for d in range(RING)]
    to_pair = ((1 - l) * RING + z, col, fib)
    to_cross = ((1 - l) * RING + z, col, (1 - h) * RING + x)
    to_far = (row, col, (1 - h) * RING + x)
    mate = (row, 1 - col, fib)
    peers = [(lax.rem(row + d, 8), col, fib) for d in range(1, 8)]

    def nodes_of(p):
        return pl.ds(pl.multiple_of(p * span_t, span_t), span_t)

    load_weight = [
        pltpu.make_async_copy(
            weight_hbm.at[:, k * width : (k + 1) * width], weight_raw.at[k], load_sems.at[1 + k]
        )
        for k in range(2 * RING)
    ]
    load_feat = pltpu.make_async_copy(feat_hbm, feat.at[0], load_sems.at[0])
    for load in load_weight:
        load.start()
    load_feat.start()
    greet([*to_x[1:], to_cross, to_far, mate, *peers])

    def part_at(to_l, to_z, t):
        return part_all.at[(to_l * RING + to_z) * chunks + t]

    def copy(kind, t, source, target, peer):
        return pltpu.make_async_remote_copy(
            source, target, send_sems.at[kind, t], recv_sems.at[kind, t], device_id=peer, device_id_type=MESH
        )

    def late_copy(to_z):
        source = part_all.at[pl.ds(((1 - l) * RING + to_z) * chunks + split, LATE)]
        return pltpu.make_async_remote_copy(
            source, late_in.at[to_z], late_sems.at[0, to_z], late_sems.at[1, to_z], device_id=to_pair, device_id_type=MESH
        )

    def early_share(i, to_z, t):
        return part_at(i, to_z, t)

    def late_share(i, to_z, t):
        return late.at[to_z, t - split, i]

    def link(kind, t, share=early_share):
        if kind == 0:
            return copy(0, t, share(0, z_far, t), first.at[0, t], to_z_up)
        if kind == 1:
            return copy(1, t, share(1, z_far, t), first.at[1, t], to_z_down)
        if kind == 2:
            return copy(2, t, share(1, z_up, t), second.at[0, t, 1], to_z_up)
        if kind == 3:
            return copy(3, t, share(0, z_down, t), second.at[1, t, 0], to_z_down)
        if kind == 4:
            return copy(4, t, merged.at[0, t], second.at[0, t, 0], to_z_up)
        if kind == 5:
            return copy(5, t, merged.at[1, t], second.at[1, t, 1], to_z_down)
        if kind == 6:
            return copy(6, t, half.at[t, 1 - l], y_in.at[0, t], to_pair)
        if kind == 7:
            return copy(7, t, half.at[t, 1 - l], y_in.at[1, t], to_cross)
        if share is late_share:
            both = whole.at[h, pl.ds(2 * t - split, 2)]
            return copy(8, t, both, both, to_far)
        return copy(8, t, half.at[t, l], y_in.at[2, t], to_far)

    def along_x(kind, d, p, source, target):
        return pltpu.make_async_remote_copy(
            source, target, x_sems.at[0, kind, d, p], x_sems.at[1, kind, d, p], device_id=to_x[d], device_id_type=MESH
        )

    def feat_copy(d, p):
        return along_x(0, d, p, feat.at[0, nodes_of(p)], feat.at[RING - d, nodes_of(p)])

    def gf_copy(d, p):
        return along_x(1, d, p, gf_send.at[d - 1, p], gf_in.at[d - 1, p])

    def weight_copy(d):
        return along_x(2, d, 0, weight_send.at[d - 1], weight_in.at[RING - d])

    def added(*refs):
        terms = [r[...].astype(jnp.float32) for r in refs]
        return functools.reduce(lambda a, b: a + b, terms)

    def send_shares(t):
        @pl.when(t < split)
        def _():
            for kind in range(4):
                link(kind, t).start()

        @pl.when(t == split)
        def _():
            for to_z in range(RING):
                late_copy(to_z).wait_recv()

        @pl.when(t >= split)
        def _():
            for to_z in (z_far, z_up, z_down, z):
                for i in range(2):
                    n = 2 * (t - split) + i
                    late[to_z, t - split, i] = added(
                        part_at(l, to_z, split + n), late_in.at[to_z, n]
                    ).astype(late.dtype)
            for kind in range(4):
                link(kind, t, late_share).start()

        @pl.when(t == 0)
        def _():
            for to_z in range(RING):
                late_copy(to_z).start()
            for load in load_weight:
                load.wait()
            for d in range(RING):
                at = lax.rem(x + d, RING)
                block = jnp.concatenate([weight_raw[at], weight_raw[RING + at]], axis=1)
                if d == 0:
                    weight_in[0] = block
                else:
                    weight_send[d - 1] = block
                    weight_copy(d).start()
            gw_ref[...] = jnp.zeros_like(gw_ref)
            load_feat.wait()

        @pl.when(t < pairs)
        def _():
            for d in range(1, RING):
                feat_copy(d, t).start()

    def merge(t):
        def run(share):
            link(0, t, share).wait_recv()
            merged[0, t] = added(share(0, z_up, t), first.at[0, t]).astype(merged.dtype)
            link(4, t, share).start()
            link(1, t, share).wait_recv()
            merged[1, t] = added(share(1, z_down, t), first.at[1, t]).astype(merged.dtype)
            link(5, t, share).start()

        pl.when(t < split)(lambda: run(early_share))
        pl.when(t >= split)(lambda: run(late_share))

    def sum_over_z(t):
        for kind in (2, 3, 4, 5):
            link(kind, t).wait_recv()

        @pl.when(t < split)
        def _():
            for i in range(2):
                half[t, i] = added(part_at(i, z, t), second.at[0, t, i], second.at[1, t, i]).astype(
                    half.dtype
                )
            for kind in (6, 7, 8):
                link(kind, t).start()

        @pl.when(t >= split)
        def _():
            for i in range(2):
                whole[h, 2 * t - split + i] = added(
                    late.at[z, t - split, i], second.at[0, t, i], second.at[1, t, i]
                ).astype(whole.dtype)
            link(8, t, late_share).start()

    def sum_over_y(t):
        @pl.when(t < split)
        def _():
            for kind in (6, 7, 8):
                link(kind, t).wait_recv()
            whole[h, t] = added(half.at[t, l], y_in.at[0, t]).astype(whole.dtype)
            whole[1 - h, t] = added(y_in.at[1, t], y_in.at[2, t]).astype(whole.dtype)

        @pl.when(t >= split)
        def _():
            link(8, t, late_share).wait_recv()

        @pl.when((lax.rem(t, 2) == 1) | (t >= split))
        def _():
            multiply(jnp.where(t < split, lax.div(t, 2), t - split // 2))

    def multiply(p):
        @pl.when(p == 0)
        def _():
            for d in range(1, RING):
                weight_copy(d).wait_recv()

        panel = jnp.concatenate(
            [whole[:, 2 * p].reshape(2 * width, nodes_t), whole[:, 2 * p + 1].reshape(2 * width, nodes_t)], axis=1
        )
        for d in range(1, RING):
            feat_copy(d, p).wait_recv()
        beside = jnp.concatenate([feat[d, nodes_of(p), :] for d in range(RING)], axis=1)
        gw_ref[...] += jnp.dot(panel, beside, preferred_element_type=jnp.float32)
        for d in (2, 1, 3, 0):
            block = jnp.dot(weight_in[d], panel, preferred_element_type=jnp.float32)
            if d == 0:
                gf_own[p] = block
            else:
                gf_send[d - 1, p] = block.astype(gf_send.dtype)
                gf_copy(d, p).start()

    def collect(p):
        for d in range(1, RING):
            gf_copy(d, p).wait_recv()
        block = gf_own[p] + added(*[gf_in.at[d - 1, p] for d in range(1, RING)])
        gf_ref[nodes_of(p), :] = block.T.astype(gf_ref.dtype)

    stages = (send_shares, merge, sum_over_z, sum_over_y)

    @pl.loop(0, units + LAGS[-1])
    def _(step):
        for late, stage in zip(LAGS, stages):
            t = step - late

            @pl.when((t >= 0) & (t < units))
            def _(stage=stage, t=t):
                stage(t)

    rows = width // 8

    def gw_copy(phase, d, source, target, peer):
        return pltpu.make_async_remote_copy(
            source, target, gw_sems.at[phase, 0, d], gw_sems.at[phase, 1, d], device_id=peer, device_id_type=MESH
        )

    def piece(ref, of, size=rows):
        return ref.at[pl.ds(pl.multiple_of(of * size, size), size)]

    gw_send[...] = gw_ref[pl.ds(pl.multiple_of((1 - col) * width, width), width), :].astype(gw_send.dtype)
    gives = [gw_copy(0, 0, gw_send, mate_in, mate)]
    gives[0].start()
    gives[0].wait_recv()
    mine = gw_ref[pl.ds(pl.multiple_of(col * width, width), width), :] + mate_in[...].astype(jnp.float32)
    gw_ref[0:width, :] = mine
    row_send[...] = mine.astype(row_send.dtype)
    for d in range(1, 8):
        gives.append(gw_copy(1, d, piece(row_send, lax.rem(row + d, 8)), row_in.at[d], peers[d - 1]))
        gives[-1].start()

    @pl.loop(0, pairs // 2)
    def _(p):
        collect(p)

    own = gw_ref[pl.ds(pl.multiple_of(row * rows, rows), rows), :]
    for d in range(1, 8):
        gives[d].wait_recv()
        own += row_in[d].astype(jnp.float32)
    for d in range(RING):
        block = own[:, d * width : (d + 1) * width].astype(gw_out.dtype)
        if d == 0:
            gw_out[col, row, x] = block
        else:
            x_send[d] = block
            gives.append(gw_copy(2, d, x_send.at[d], gw_out.at[col, row, x], to_x[d]))
            gives[-1].start()

    for d in range(1, RING):
        slot = gw_out.at[col, row, lax.rem(x + RING - d, RING)]
        gw_copy(2, d, slot, slot, to_x[d]).wait_recv()
    for d in range(1, 8):
        gives.append(gw_copy(3, d, gw_out.at[col, row], gw_out.at[col, row], peers[d - 1]))
        gives[-1].start()

    @pl.loop(pairs // 2, pairs)
    def _(p):
        collect(p)

    @pl.loop(0, split)
    def _(t):
        for kind in range(9):
            link(kind, t).wait_send()

    @pl.loop(split, units)
    def _(t):
        for kind in (0, 1, 2, 3, 4, 5, 8):
            link(kind, t, late_share).wait_send()

    for to_z in range(RING):
        late_copy(to_z).wait_send()

    @pl.loop(0, pairs)
    def _(p):
        for d in range(1, RING):
            feat_copy(d, p).wait_send()
            gf_copy(d, p).wait_send()

    for d in range(1, RING):
        weight_copy(d).wait_send()
    for d in range(1, 8):
        slot = gw_out.at[col, lax.rem(row + 8 - d, 8)]
        gw_copy(3, d, slot, slot, peers[d - 1]).wait_recv()
    gives.append(gw_copy(0, 1, gw_out.at[col], gw_out.at[col], mate))
    gives[-1].start()
    slot = gw_out.at[1 - col]
    gw_copy(0, 1, slot, slot, mate).wait_recv()
    for give in gives:
        give.wait_send()


def flow(part, weight, features):
    _, width, cut = part.shape
    nodes = features.shape[0]
    chunks = nodes // cut
    pairs = chunks // 2
    piece = (width, cut)
    block = (width, 2 * cut)
    sixteen = jnp.bfloat16
    rows = width // 8
    return pl.pallas_call(
        flow_kernel,
        out_shape=(
            jax.ShapeDtypeStruct((nodes, width), sixteen),
            jax.ShapeDtypeStruct((2, 8, RING, rows, width), sixteen),
        ),
        in_specs=[VMEM, HBM, HBM],
        out_specs=(VMEM, VMEM),
        scratch_shapes=[
            pltpu.VMEM((2, chunks, *piece), sixteen),
            pltpu.VMEM((2, chunks, 2, *piece), sixteen),
            pltpu.VMEM((2, chunks, *piece), sixteen),
            pltpu.VMEM((chunks, 2, *piece), sixteen),
            pltpu.VMEM((3, chunks, *piece), sixteen),
            pltpu.VMEM((RING, LATE, *piece), sixteen),
            pltpu.VMEM((RING, LATE // 2, 2, *piece), sixteen),
            pltpu.VMEM((2, chunks, *piece), sixteen),
            pltpu.VMEM((2 * RING, width, width), sixteen),
            pltpu.VMEM((RING - 1, width, 2 * width), sixteen),
            pltpu.VMEM((RING, width, 2 * width), sixteen),
            pltpu.VMEM((RING, nodes, width), sixteen),
            pltpu.VMEM((pairs, *block), jnp.float32),
            pltpu.VMEM((RING - 1, pairs, *block), sixteen),
            pltpu.VMEM((RING - 1, pairs, *block), sixteen),
            pltpu.VMEM((2 * width, RING * width), jnp.float32),
            pltpu.VMEM((width, RING * width), sixteen),
            pltpu.VMEM((width, RING * width), sixteen),
            pltpu.VMEM((width, RING * width), sixteen),
            pltpu.VMEM((8, rows, RING * width), sixteen),
            pltpu.VMEM((RING, rows, width), sixteen),
            pltpu.SemaphoreType.DMA((1 + 2 * RING,)),
            pltpu.SemaphoreType.DMA((9, chunks)),
            pltpu.SemaphoreType.DMA((9, chunks)),
            pltpu.SemaphoreType.DMA((2, 3, RING, pairs)),
            pltpu.SemaphoreType.DMA((2, RING)),
            pltpu.SemaphoreType.DMA((4, 2, 8)),
        ],
        compiler_params=pltpu.CompilerParams(
            collective_id=1, has_side_effects=True, vmem_limit_bytes=24 << 20
        ),
        cost_estimate=pl.CostEstimate(
            flops=32 * nodes * width * width, bytes_accessed=16 << 20, transcendentals=0
        ),
        name="flow",
    )(part, weight, features)


def finish_kernel(gf_ref, gw_ref, gf_hbm, gw_hbm, gw_turned, sems):
    width = gw_turned.shape[0]
    write_gf = pltpu.make_async_copy(gf_ref, gf_hbm, sems.at[0])
    write_gf.start()
    for side in range(2):
        for x in range(RING):
            target = side * RING + x
            block = gw_ref[side, :, x].reshape(width, width).astype(jnp.float32)
            gw_turned[:, target * width : (target + 1) * width] = block.T
    write_gw = pltpu.make_async_copy(gw_turned, gw_hbm, sems.at[1])
    write_gw.start()
    write_gf.wait()
    write_gw.wait()


def finish(gf, gw):
    width = gf.shape[1]
    turned = (width, 2 * RING * width)
    return pl.pallas_call(
        finish_kernel,
        out_shape=(
            jax.ShapeDtypeStruct(gf.shape, gf.dtype),
            jax.ShapeDtypeStruct(turned, jnp.float32),
        ),
        in_specs=[VMEM, VMEM],
        out_specs=(HBM, HBM),
        scratch_shapes=[pltpu.VMEM(turned, jnp.float32), pltpu.SemaphoreType.DMA((2,))],
        compiler_params=pltpu.CompilerParams(vmem_limit_bytes=4 << 20),
        cost_estimate=pl.CostEstimate(flops=0, bytes_accessed=1 << 20, transcendentals=0),
        name="finish",
    )(gf, gw)


def on_device(features, pre_activation, out_grad, weight, tiles, rows, cols, counts):
    features, pre_activation, out_grad, weight, tiles, rows, cols = (
        pltpu.with_memory_space_constraint(a, pltpu.HBM)
        for a in (features, pre_activation, out_grad, weight, tiles[0, 0], rows, cols)
    )
    grad, early = local_grads(pre_activation, out_grad, tiles)
    out_tiles = 8 * (features.shape[0] // tiles.shape[1])
    part = tile_products(rows, cols, counts, grad, early, tiles, out_tiles)
    return finish(*flow(part, weight, features))


def solution(mesh):
    in_specs = (
        P(("row", "col"), "fib"),
        P(("row", "col"), "fib"),
        P(("row", "col"), "fib"),
        P("fib", None),
        P("row", "col", None, None, None),
        P("row", "col", None),
        P("row", "col", None),
        P("row", "col"),
    )
    out_specs = (P(("row", "col"), "fib"), P("fib", None))
    return jax.shard_map(
        on_device, mesh=mesh, in_specs=in_specs, out_specs=out_specs, check_vma=False
    )
```

```python
import functools

import jax
import jax.numpy as jnp
from jax import lax
from jax.experimental import pallas as pl
from jax.experimental.pallas import tpu as pltpu
from jax.sharding import PartitionSpec as P

GROUP = 8
EARLY = 24
RING = 4
LAGS = (0, 2, 5, 8, 4)
MESH = pl.DeviceIdType.MESH
VMEM = pl.BlockSpec(memory_space=pltpu.VMEM)
HBM = pl.BlockSpec(memory_space=pltpu.HBM)
CHUNK = 128
LATE = 4


def greet(peers):
    barrier = pltpu.get_barrier_semaphore()
    for peer in peers:
        pl.semaphore_signal(barrier, inc=1, device_id=peer, device_id_type=MESH)
    pl.semaphore_wait(barrier, len(peers))


def position():
    return lax.axis_index("row"), lax.axis_index("col"), lax.axis_index("fib")


def grad_kernel(
    pre_hbm, out_grad_hbm, tiles_hbm, grad_ref, early_ref,
    pre_ref, out_grad_ref, load_sems, tile_sems, send_sems, recv_sems,
):
    row, col, fib = position()
    own_tiles = grad_ref.shape[0] // 2
    tile = grad_ref.shape[2]
    partner = (row, 1 - col, fib)

    def loads(t):
        part = pl.ds(pl.multiple_of(t * tile, tile), tile)
        return (
            pltpu.make_async_copy(pre_hbm.at[part], pre_ref.at[part], load_sems.at[0, t]),
            pltpu.make_async_copy(out_grad_hbm.at[part], out_grad_ref.at[part], load_sems.at[1, t]),
        )

    @pl.loop(0, own_tiles)
    def _(t):
        for load in loads(t):
            load.start()

    def early(g):
        group = pl.ds(g * GROUP, GROUP)
        return pltpu.make_async_copy(tiles_hbm.at[group], early_ref.at[group], tile_sems.at[g])

    @pl.loop(0, EARLY // GROUP)
    def _(g):
        early(g).start()

    greet([partner])

    def copy(t, owner):
        slot = grad_ref.at[owner * own_tiles + t]
        return pltpu.make_async_remote_copy(
            slot, slot, send_sems.at[t], recv_sems.at[t], device_id=partner, device_id_type=MESH
        )

    @pl.loop(0, own_tiles)
    def _(t):
        for load in loads(t):
            load.wait()
        part = pl.ds(pl.multiple_of(t * tile, tile), tile)
        pre = pre_ref[part, :].astype(jnp.float32)
        sigmoid = jax.nn.sigmoid(pre)
        grad = out_grad_ref[part, :].astype(jnp.float32) * sigmoid * (1.0 + pre * (1.0 - sigmoid))
        grad_ref[col * own_tiles + t] = grad.T.astype(grad_ref.dtype)
        copy(t, col).start()

    @pl.loop(0, own_tiles)
    def _(t):
        copy(t, col).wait_send()
        copy(t, 1 - col).wait_recv()

    @pl.loop(0, EARLY // GROUP)
    def _(g):
        early(g).wait()


def local_grads(pre, out_grad, tiles):
    nodes, width = pre.shape
    tile = tiles.shape[1]
    own_tiles = nodes // tile
    return pl.pallas_call(
        grad_kernel,
        out_shape=(
            jax.ShapeDtypeStruct((2 * own_tiles, width, tile), jnp.bfloat16),
            jax.ShapeDtypeStruct((EARLY, tile, tile), tiles.dtype),
        ),
        in_specs=[HBM, HBM, HBM],
        out_specs=(VMEM, VMEM),
        scratch_shapes=[
            pltpu.VMEM(pre.shape, pre.dtype),
            pltpu.VMEM(pre.shape, pre.dtype),
            pltpu.SemaphoreType.DMA((2, own_tiles)),
            pltpu.SemaphoreType.DMA((EARLY // GROUP,)),
            pltpu.SemaphoreType.DMA((own_tiles,)),
            pltpu.SemaphoreType.DMA((own_tiles,)),
        ],
        compiler_params=pltpu.CompilerParams(
            collective_id=0, has_side_effects=True, vmem_limit_bytes=16 << 20
        ),
        cost_estimate=pl.CostEstimate(
            flops=10 * nodes * width, bytes_accessed=8 * nodes * width, transcendentals=nodes * width
        ),
        name="local_grads",
    )(pre, out_grad, tiles)


def tile_kernel(
    rows_hbm, cols_hbm, count_ref, grad_ref, early_ref, tiles_ref, out_ref,
    held, total, rows_ref, cols_ref, sems, index_sems,
):
    slots, tile, _ = tiles_ref.shape
    cuts = tile // CHUNK
    out_tiles = out_ref.shape[0] // cuts
    row_tiles = grad_ref.shape[0]
    def copy(g):
        source = tiles_ref.at[pl.ds(g * GROUP, GROUP)]
        return pltpu.make_async_copy(
            source, held.at[pl.ds(g * GROUP - EARLY, GROUP)], sems.at[g - EARLY // GROUP]
        )

    indices = [
        pltpu.make_async_copy(source, target, index_sems.at[i])
        for i, (source, target) in enumerate(
            ((rows_hbm, rows_ref), (cols_hbm, cols_ref))
        )
    ]
    for load in indices:
        load.start()
    count = jnp.clip(count_ref[0, 0], 1, slots)
    used = (count + GROUP - 1) // GROUP

    @pl.loop(EARLY // GROUP, used)
    def _(g):
        copy(g).start()

    @pl.loop(0, out_tiles + 1, unroll=5)
    def _(t):
        total[t] = jnp.zeros(total.shape[1:], total.dtype)

    for load in indices:
        load.wait()

    def add_group(g, tile_at):
        for j in range(GROUP):
            slot = g * GROUP + j
            row = jnp.clip(rows_ref[0, 0, slot], 0, row_tiles - 1)
            col = jnp.clip(cols_ref[0, 0, slot], 0, out_tiles - 1)
            target = jnp.where(slot < count, col, out_tiles)
            total[target] += jnp.dot(grad_ref[row], tile_at(slot), preferred_element_type=jnp.float32)

    @pl.loop(0, jnp.minimum(used, EARLY // GROUP))
    def _(g):
        add_group(g, lambda slot: early_ref[slot])

    @pl.loop(EARLY // GROUP, used)
    def _(g):
        copy(g).wait()
        add_group(g, lambda slot: held[slot - EARLY])

    @pl.loop(0, out_tiles, unroll=4)
    def _(t):
        for cut in range(cuts):
            out_ref[t * cuts + cut] = total[t, :, cut * CHUNK : (cut + 1) * CHUNK].astype(out_ref.dtype)


def tile_products(rows, cols, count, grad, early, tiles, out_tiles):
    slots, tile, _ = tiles.shape
    width = grad.shape[1]
    return pl.pallas_call(
        tile_kernel,
        out_shape=jax.ShapeDtypeStruct((out_tiles * tile // CHUNK, width, CHUNK), jnp.bfloat16),
        in_specs=[HBM, HBM, pl.BlockSpec(memory_space=pltpu.SMEM), VMEM, VMEM, HBM],
        out_specs=VMEM,
        scratch_shapes=[
            pltpu.VMEM((slots - EARLY, tile, tile), jnp.bfloat16),
            pltpu.VMEM((out_tiles + 1, width, tile), jnp.float32),
            pltpu.SMEM(rows.shape, rows.dtype),
            pltpu.SMEM(cols.shape, cols.dtype),
            pltpu.SemaphoreType.DMA(((slots - EARLY) // GROUP,)),
            pltpu.SemaphoreType.DMA((2,)),
        ],
        compiler_params=pltpu.CompilerParams(vmem_limit_bytes=28 << 20),
        cost_estimate=pl.CostEstimate(
            flops=2 * slots * width * tile * tile,
            bytes_accessed=2 * slots * tile * tile,
            transcendentals=0,
        ),
        name="tile_products",
    )(rows, cols, count, grad, early, tiles)


def flow_kernel(
    part_all, weight_hbm, feat_hbm, gf_ref, gw_out,
    first, second, merged, half, y_in, late_in, late, whole, weight_raw, weight_send, weight_in, feat,
    gf_own, gf_send, gf_in, gw_ref, gw_send, mate_in, row_send, row_in, x_send,
    load_sems, send_sems, recv_sems, x_sems, late_sems, gw_sems,
):
    row, col, fib = position()
    l, z = row // RING, lax.rem(row, RING)
    h, x = fib // RING, lax.rem(fib, RING)
    chunks, width, nodes_t = whole.shape[1:]
    pairs, span_t = chunks // 2, 2 * nodes_t
    split = chunks - LATE
    units = split + LATE // 2
    z_up, z_down, z_far = (lax.rem(z + d, RING) for d in (1, RING - 1, 2))
    to_z_up, to_z_down = (l * RING + z_up, col, fib), (l * RING + z_down, col, fib)
    to_x = [(row, col, h * RING + lax.rem(x + d, RING)) for d in range(RING)]
    to_pair = ((1 - l) * RING + z, col, fib)
    to_cross = ((1 - l) * RING + z, col, (1 - h) * RING + x)
    to_far = (row, col, (1 - h) * RING + x)
    mate = (row, 1 - col, fib)
    peers = [(lax.rem(row + d, 8), col, fib) for d in range(1, 8)]

    def nodes_of(p):
        return pl.ds(pl.multiple_of(p * span_t, span_t), span_t)

    load_weight = [
        pltpu.make_async_copy(
            weight_hbm.at[:, k * width : (k + 1) * width], weight_raw.at[k], load_sems.at[1 + k]
        )
        for k in range(2 * RING)
    ]
    load_feat = pltpu.make_async_copy(feat_hbm, feat.at[0], load_sems.at[0])
    for load in load_weight:
        load.start()
    load_feat.start()
    greet([*to_x[1:], to_cross, to_far, mate, *peers])

    def part_at(to_l, to_z, t):
        return part_all.at[(to_l * RING + to_z) * chunks + t]

    def copy(kind, t, source, target, peer):
        return pltpu.make_async_remote_copy(
            source, target, send_sems.at[kind, t], recv_sems.at[kind, t], device_id=peer, device_id_type=MESH
        )

    def late_copy(to_z):
        source = part_all.at[pl.ds(((1 - l) * RING + to_z) * chunks + split, LATE)]
        return pltpu.make_async_remote_copy(
            source, late_in.at[to_z], late_sems.at[0, to_z], late_sems.at[1, to_z], device_id=to_pair, device_id_type=MESH
        )

    def early_share(i, to_z, t):
        return part_at(i, to_z, t)

    def late_share(i, to_z, t):
        return late.at[to_z, t - split, i]

    def link(kind, t, share=early_share):
        if kind == 0:
            return copy(0, t, share(0, z_far, t), first.at[0, t], to_z_up)
        if kind == 1:
            return copy(1, t, share(1, z_far, t), first.at[1, t], to_z_down)
        if kind == 2:
            return copy(2, t, share(1, z_up, t), second.at[0, t, 1], to_z_up)
        if kind == 3:
            return copy(3, t, share(0, z_down, t), second.at[1, t, 0], to_z_down)
        if kind == 4:
            return copy(4, t, merged.at[0, t], second.at[0, t, 0], to_z_up)
        if kind == 5:
            return copy(5, t, merged.at[1, t], second.at[1, t, 1], to_z_down)
        if kind == 6:
            return copy(6, t, half.at[t, 1 - l], y_in.at[0, t], to_pair)
        if kind == 7:
            return copy(7, t, half.at[t, 1 - l], y_in.at[1, t], to_cross)
        if share is late_share:
            both = whole.at[h, pl.ds(2 * t - split, 2)]
            return copy(8, t, both, both, to_far)
        return copy(8, t, half.at[t, l], y_in.at[2, t], to_far)

    def along_x(kind, d, p, source, target, peer=None):
        return pltpu.make_async_remote_copy(
            source,
            target,
            x_sems.at[0, kind, d, p],
            x_sems.at[1, kind, d, p],
            device_id=to_x[d] if peer is None else peer,
            device_id_type=MESH,
        )

    def feat_pass(up, p):
        part = pl.ds(pl.multiple_of(p * span_t + (0 if up else nodes_t), nodes_t), nodes_t)
        source = feat.at[RING - 1 if up else 1, part]
        return along_x(0, 2 if up else 0, p, source, feat.at[2, part], to_x[1 if up else RING - 1])

    def feat_copy(d, p):
        return along_x(0, d, p, feat.at[0, nodes_of(p)], feat.at[RING - d, nodes_of(p)])

    def gf_copy(d, p):
        return along_x(1, d, p, gf_send.at[d - 1, p], gf_in.at[d - 1, p])

    def weight_copy(d):
        return along_x(2, d, 0, weight_send.at[d - 1], weight_in.at[RING - d])

    def added(*refs):
        terms = [r[...].astype(jnp.float32) for r in refs]
        return functools.reduce(lambda a, b: a + b, terms)

    def send_shares(t):
        @pl.when(t < split)
        def _():
            for kind in range(4):
                link(kind, t).start()

        @pl.when(t == split)
        def _():
            for to_z in range(RING):
                late_copy(to_z).wait_recv()

        @pl.when(t >= split)
        def _():
            for to_z in (z_far, z_up, z_down, z):
                for i in range(2):
                    n = 2 * (t - split) + i
                    late[to_z, t - split, i] = added(
                        part_at(l, to_z, split + n), late_in.at[to_z, n]
                    ).astype(late.dtype)
            for kind in range(4):
                link(kind, t, late_share).start()

        @pl.when(t == 0)
        def _():
            for to_z in range(RING):
                late_copy(to_z).start()
            for load in load_weight:
                load.wait()
            for d in range(RING):
                at = lax.rem(x + d, RING)
                block = jnp.concatenate([weight_raw[at], weight_raw[RING + at]], axis=1)
                if d == 0:
                    weight_in[0] = block
                else:
                    weight_send[d - 1] = block
                    weight_copy(d).start()
            gw_ref[...] = jnp.zeros_like(gw_ref)
            load_feat.wait()

        @pl.when(t < pairs)
        def _():
            for d in (1, RING - 1):
                feat_copy(d, t).start()

    def pass_on(t):
        @pl.when(t < pairs)
        def _():
            feat_copy(1, t).wait_recv()
            feat_pass(True, t).start()
            feat_copy(RING - 1, t).wait_recv()
            feat_pass(False, t).start()

    def merge(t):
        def run(share):
            link(0, t, share).wait_recv()
            merged[0, t] = added(share(0, z_up, t), first.at[0, t]).astype(merged.dtype)
            link(4, t, share).start()
            link(1, t, share).wait_recv()
            merged[1, t] = added(share(1, z_down, t), first.at[1, t]).astype(merged.dtype)
            link(5, t, share).start()

        pl.when(t < split)(lambda: run(early_share))
        pl.when(t >= split)(lambda: run(late_share))

    def sum_over_z(t):
        for kind in (2, 3, 4, 5):
            link(kind, t).wait_recv()

        @pl.when(t < split)
        def _():
            for i in range(2):
                half[t, i] = added(part_at(i, z, t), second.at[0, t, i], second.at[1, t, i]).astype(
                    half.dtype
                )
            for kind in (6, 7, 8):
                link(kind, t).start()

        @pl.when(t >= split)
        def _():
            for i in range(2):
                whole[h, 2 * t - split + i] = added(
                    late.at[z, t - split, i], second.at[0, t, i], second.at[1, t, i]
                ).astype(whole.dtype)
            link(8, t, late_share).start()

    def sum_over_y(t):
        @pl.when(t < split)
        def _():
            for kind in (6, 7, 8):
                link(kind, t).wait_recv()
            whole[h, t] = added(half.at[t, l], y_in.at[0, t]).astype(whole.dtype)
            whole[1 - h, t] = added(y_in.at[1, t], y_in.at[2, t]).astype(whole.dtype)

        @pl.when(t >= split)
        def _():
            link(8, t, late_share).wait_recv()

        @pl.when((lax.rem(t, 2) == 1) | (t >= split))
        def _():
            multiply(jnp.where(t < split, lax.div(t, 2), t - split // 2))

    def multiply(p):
        @pl.when(p == 0)
        def _():
            for d in range(1, RING):
                weight_copy(d).wait_recv()

        panel = jnp.concatenate(
            [whole[:, 2 * p].reshape(2 * width, nodes_t), whole[:, 2 * p + 1].reshape(2 * width, nodes_t)], axis=1
        )
        for up in (True, False):
            feat_pass(up, p).wait_recv()
        beside = jnp.concatenate([feat[d, nodes_of(p), :] for d in range(RING)], axis=1)
        gw_ref[...] += jnp.dot(panel, beside, preferred_element_type=jnp.float32)
        for d in (2, 1, 3, 0):
            block = jnp.dot(weight_in[d], panel, preferred_element_type=jnp.float32)
            if d == 0:
                gf_own[p] = block
            else:
                gf_send[d - 1, p] = block.astype(gf_send.dtype)
                gf_copy(d, p).start()

    def collect(p):
        for d in range(1, RING):
            gf_copy(d, p).wait_recv()
        block = gf_own[p] + added(*[gf_in.at[d - 1, p] for d in range(1, RING)])
        gf_ref[nodes_of(p), :] = block.T.astype(gf_ref.dtype)

    stages = (send_shares, merge, sum_over_z, sum_over_y, pass_on)

    @pl.loop(0, units + max(LAGS))
    def _(step):
        for late, stage in zip(LAGS, stages):
            t = step - late

            @pl.when((t >= 0) & (t < units))
            def _(stage=stage, t=t):
                stage(t)

    rows = width // 8

    def gw_copy(phase, d, source, target, peer):
        return pltpu.make_async_remote_copy(
            source, target, gw_sems.at[phase, 0, d], gw_sems.at[phase, 1, d], device_id=peer, device_id_type=MESH
        )

    def piece(ref, of, size=rows):
        return ref.at[pl.ds(pl.multiple_of(of * size, size), size)]

    gw_send[...] = gw_ref[pl.ds(pl.multiple_of((1 - col) * width, width), width), :].astype(gw_send.dtype)
    gives = [gw_copy(0, 0, gw_send, mate_in, mate)]
    gives[0].start()
    gives[0].wait_recv()
    mine = gw_ref[pl.ds(pl.multiple_of(col * width, width), width), :] + mate_in[...].astype(jnp.float32)
    gw_ref[0:width, :] = mine
    row_send[...] = mine.astype(row_send.dtype)
    for d in range(1, 8):
        gives.append(gw_copy(1, d, piece(row_send, lax.rem(row + d, 8)), row_in.at[d], peers[d - 1]))
        gives[-1].start()

    @pl.loop(0, pairs // 2)
    def _(p):
        collect(p)

    @pl.loop(0, split)
    def _(t):
        for kind in range(9):
            link(kind, t).wait_send()

    @pl.loop(split, units)
    def _(t):
        for kind in (0, 1, 2, 3, 4, 5, 8):
            link(kind, t, late_share).wait_send()

    for to_z in range(RING):
        late_copy(to_z).wait_send()

    own = gw_ref[pl.ds(pl.multiple_of(row * rows, rows), rows), :]
    for d in range(1, 8):
        gives[d].wait_recv()
        own += row_in[d].astype(jnp.float32)
    for d in range(RING):
        block = own[:, d * width : (d + 1) * width].astype(gw_out.dtype)
        if d == 0:
            gw_out[col, row, x] = block
        else:
            x_send[d] = block
            gives.append(gw_copy(2, d, x_send.at[d], gw_out.at[col, row, x], to_x[d]))
            gives[-1].start()

    for d in range(1, RING):
        slot = gw_out.at[col, row, lax.rem(x + RING - d, RING)]
        gw_copy(2, d, slot, slot, to_x[d]).wait_recv()
    for d in range(1, 8):
        gives.append(gw_copy(3, d, gw_out.at[col, row], gw_out.at[col, row], peers[d - 1]))
        gives[-1].start()

    @pl.loop(pairs // 2, pairs)
    def _(p):
        collect(p)

    @pl.loop(0, pairs)
    def _(p):
        for up in (True, False):
            feat_pass(up, p).wait_send()
        for d in (1, RING - 1):
            feat_copy(d, p).wait_send()
        for d in range(1, RING):
            gf_copy(d, p).wait_send()

    for d in range(1, RING):
        weight_copy(d).wait_send()
    for d in range(1, 8):
        slot = gw_out.at[col, lax.rem(row + 8 - d, 8)]
        gw_copy(3, d, slot, slot, peers[d - 1]).wait_recv()
    gives.append(gw_copy(0, 1, gw_out.at[col], gw_out.at[col], mate))
    gives[-1].start()
    slot = gw_out.at[1 - col]
    gw_copy(0, 1, slot, slot, mate).wait_recv()
    for give in gives:
        give.wait_send()


def flow(part, weight, features):
    _, width, cut = part.shape
    nodes = features.shape[0]
    chunks = nodes // cut
    pairs = chunks // 2
    piece = (width, cut)
    block = (width, 2 * cut)
    sixteen = jnp.bfloat16
    rows = width // 8
    return pl.pallas_call(
        flow_kernel,
        out_shape=(
            jax.ShapeDtypeStruct((nodes, width), sixteen),
            jax.ShapeDtypeStruct((2, 8, RING, rows, width), sixteen),
        ),
        in_specs=[VMEM, HBM, HBM],
        out_specs=(VMEM, VMEM),
        scratch_shapes=[
            pltpu.VMEM((2, chunks, *piece), sixteen),
            pltpu.VMEM((2, chunks, 2, *piece), sixteen),
            pltpu.VMEM((2, chunks, *piece), sixteen),
            pltpu.VMEM((chunks, 2, *piece), sixteen),
            pltpu.VMEM((3, chunks, *piece), sixteen),
            pltpu.VMEM((RING, LATE, *piece), sixteen),
            pltpu.VMEM((RING, LATE // 2, 2, *piece), sixteen),
            pltpu.VMEM((2, chunks, *piece), sixteen),
            pltpu.VMEM((2 * RING, width, width), sixteen),
            pltpu.VMEM((RING - 1, width, 2 * width), sixteen),
            pltpu.VMEM((RING, width, 2 * width), sixteen),
            pltpu.VMEM((RING, nodes, width), sixteen),
            pltpu.VMEM((pairs, *block), jnp.float32),
            pltpu.VMEM((RING - 1, pairs, *block), sixteen),
            pltpu.VMEM((RING - 1, pairs, *block), sixteen),
            pltpu.VMEM((2 * width, RING * width), jnp.float32),
            pltpu.VMEM((width, RING * width), sixteen),
            pltpu.VMEM((width, RING * width), sixteen),
            pltpu.VMEM((width, RING * width), sixteen),
            pltpu.VMEM((8, rows, RING * width), sixteen),
            pltpu.VMEM((RING, rows, width), sixteen),
            pltpu.SemaphoreType.DMA((1 + 2 * RING,)),
            pltpu.SemaphoreType.DMA((9, chunks)),
            pltpu.SemaphoreType.DMA((9, chunks)),
            pltpu.SemaphoreType.DMA((2, 3, RING, pairs)),
            pltpu.SemaphoreType.DMA((2, RING)),
            pltpu.SemaphoreType.DMA((4, 2, 8)),
        ],
        compiler_params=pltpu.CompilerParams(
            collective_id=1, has_side_effects=True, vmem_limit_bytes=24 << 20
        ),
        cost_estimate=pl.CostEstimate(
            flops=32 * nodes * width * width, bytes_accessed=16 << 20, transcendentals=0
        ),
        name="flow",
    )(part, weight, features)


def finish_kernel(gf_ref, gw_ref, gf_hbm, gw_hbm, gw_turned, sems):
    width = gw_turned.shape[0]
    write_gf = pltpu.make_async_copy(gf_ref, gf_hbm, sems.at[0])
    write_gf.start()
    for side in range(2):
        for x in range(RING):
            target = side * RING + x
            block = gw_ref[side, :, x].reshape(width, width).astype(jnp.float32)
            gw_turned[:, target * width : (target + 1) * width] = block.T
    write_gw = pltpu.make_async_copy(gw_turned, gw_hbm, sems.at[1])
    write_gw.start()
    write_gf.wait()
    write_gw.wait()


def finish(gf, gw):
    width = gf.shape[1]
    turned = (width, 2 * RING * width)
    return pl.pallas_call(
        finish_kernel,
        out_shape=(
            jax.ShapeDtypeStruct(gf.shape, gf.dtype),
            jax.ShapeDtypeStruct(turned, jnp.float32),
        ),
        in_specs=[VMEM, VMEM],
        out_specs=(HBM, HBM),
        scratch_shapes=[pltpu.VMEM(turned, jnp.float32), pltpu.SemaphoreType.DMA((2,))],
        compiler_params=pltpu.CompilerParams(vmem_limit_bytes=4 << 20),
        cost_estimate=pl.CostEstimate(flops=0, bytes_accessed=1 << 20, transcendentals=0),
        name="finish",
    )(gf, gw)


def on_device(features, pre_activation, out_grad, weight, tiles, rows, cols, counts):
    features, pre_activation, out_grad, weight, tiles, rows, cols = (
        pltpu.with_memory_space_constraint(a, pltpu.HBM)
        for a in (features, pre_activation, out_grad, weight, tiles[0, 0], rows, cols)
    )
    grad, early = local_grads(pre_activation, out_grad, tiles)
    out_tiles = 8 * (features.shape[0] // tiles.shape[1])
    part = tile_products(rows, cols, counts, grad, early, tiles, out_tiles)
    return finish(*flow(part, weight, features))


def solution(mesh):
    in_specs = (
        P(("row", "col"), "fib"),
        P(("row", "col"), "fib"),
        P(("row", "col"), "fib"),
        P("fib", None),
        P("row", "col", None, None, None),
        P("row", "col", None),
        P("row", "col", None),
        P("row", "col"),
    )
    out_specs = (P(("row", "col"), "fib"), P("fib", None))
    return jax.shard_map(
        on_device, mesh=mesh, in_specs=in_specs, out_specs=out_specs, check_vma=False
    )
```

```python
import functools

import jax
import jax.numpy as jnp
from jax import lax
from jax.experimental import pallas as pl
from jax.experimental.pallas import tpu as pltpu
from jax.sharding import PartitionSpec as P

GROUP = 16
EARLY = 48
RING = 4
LAGS = (0, 2, 5, 8, 4)
MESH = pl.DeviceIdType.MESH
VMEM = pl.BlockSpec(memory_space=pltpu.VMEM)
HBM = pl.BlockSpec(memory_space=pltpu.HBM)
CHUNK = 128
LATE = 4


def greet(peers):
    barrier = pltpu.get_barrier_semaphore()
    for peer in peers:
        pl.semaphore_signal(barrier, inc=1, device_id=peer, device_id_type=MESH)
    pl.semaphore_wait(barrier, len(peers))


def position():
    return lax.axis_index("row"), lax.axis_index("col"), lax.axis_index("fib")


def grad_kernel(
    pre_hbm, out_grad_hbm, tiles_hbm, grad_ref, early_ref,
    pre_ref, out_grad_ref, load_sems, tile_sems, send_sems, recv_sems,
):
    row, col, fib = position()
    own_tiles = grad_ref.shape[0] // 2
    tile = grad_ref.shape[2]
    partner = (row, 1 - col, fib)

    def loads(t):
        part = pl.ds(pl.multiple_of(t * tile, tile), tile)
        return (
            pltpu.make_async_copy(pre_hbm.at[part], pre_ref.at[part], load_sems.at[0, t]),
            pltpu.make_async_copy(out_grad_hbm.at[part], out_grad_ref.at[part], load_sems.at[1, t]),
        )

    @pl.loop(0, own_tiles)
    def _(t):
        for load in loads(t):
            load.start()

    def early(g):
        group = pl.ds(g * GROUP, GROUP)
        return pltpu.make_async_copy(tiles_hbm.at[group], early_ref.at[group], tile_sems.at[g])

    @pl.loop(0, EARLY // GROUP)
    def _(g):
        early(g).start()

    greet([partner])

    def copy(t, owner):
        slot = grad_ref.at[owner * own_tiles + t]
        return pltpu.make_async_remote_copy(
            slot, slot, send_sems.at[t], recv_sems.at[t], device_id=partner, device_id_type=MESH
        )

    @pl.loop(0, own_tiles)
    def _(t):
        for load in loads(t):
            load.wait()
        part = pl.ds(pl.multiple_of(t * tile, tile), tile)
        pre = pre_ref[part, :].astype(jnp.float32)
        sigmoid = jax.nn.sigmoid(pre)
        grad = out_grad_ref[part, :].astype(jnp.float32) * sigmoid * (1.0 + pre * (1.0 - sigmoid))
        grad_ref[col * own_tiles + t] = grad.T.astype(grad_ref.dtype)
        copy(t, col).start()

    @pl.loop(0, own_tiles)
    def _(t):
        copy(t, col).wait_send()
        copy(t, 1 - col).wait_recv()

    @pl.loop(0, EARLY // GROUP)
    def _(g):
        early(g).wait()


def local_grads(pre, out_grad, tiles):
    nodes, width = pre.shape
    tile = tiles.shape[1]
    own_tiles = nodes // tile
    return pl.pallas_call(
        grad_kernel,
        out_shape=(
            jax.ShapeDtypeStruct((2 * own_tiles, width, tile), jnp.bfloat16),
            jax.ShapeDtypeStruct((EARLY, tile, tile), tiles.dtype),
        ),
        in_specs=[HBM, HBM, HBM],
        out_specs=(VMEM, VMEM),
        scratch_shapes=[
            pltpu.VMEM(pre.shape, pre.dtype),
            pltpu.VMEM(pre.shape, pre.dtype),
            pltpu.SemaphoreType.DMA((2, own_tiles)),
            pltpu.SemaphoreType.DMA((EARLY // GROUP,)),
            pltpu.SemaphoreType.DMA((own_tiles,)),
            pltpu.SemaphoreType.DMA((own_tiles,)),
        ],
        compiler_params=pltpu.CompilerParams(
            collective_id=0, has_side_effects=True, vmem_limit_bytes=16 << 20
        ),
        cost_estimate=pl.CostEstimate(
            flops=10 * nodes * width, bytes_accessed=8 * nodes * width, transcendentals=nodes * width
        ),
        name="local_grads",
    )(pre, out_grad, tiles)


def tile_kernel(
    rows_hbm, cols_hbm, count_ref, grad_ref, early_ref, tiles_ref, out_ref,
    held, total, rows_ref, cols_ref, sems, index_sems,
):
    slots, tile, _ = tiles_ref.shape
    cuts = tile // CHUNK
    out_tiles = out_ref.shape[0] // cuts
    row_tiles = grad_ref.shape[0]
    def copy(g):
        source = tiles_ref.at[pl.ds(g * GROUP, GROUP)]
        return pltpu.make_async_copy(
            source, held.at[pl.ds(g * GROUP - EARLY, GROUP)], sems.at[g - EARLY // GROUP]
        )

    indices = [
        pltpu.make_async_copy(source, target, index_sems.at[i])
        for i, (source, target) in enumerate(
            ((rows_hbm, rows_ref), (cols_hbm, cols_ref))
        )
    ]
    for load in indices:
        load.start()
    count = jnp.clip(count_ref[0, 0], 1, slots)
    used = (count + GROUP - 1) // GROUP

    @pl.loop(EARLY // GROUP, used)
    def _(g):
        copy(g).start()

    @pl.loop(0, out_tiles + 1, unroll=5)
    def _(t):
        total[t] = jnp.zeros(total.shape[1:], total.dtype)

    for load in indices:
        load.wait()

    def add_group(g, tile_at):
        for j in range(GROUP):
            slot = g * GROUP + j
            row = jnp.clip(rows_ref[0, 0, slot], 0, row_tiles - 1)
            col = jnp.clip(cols_ref[0, 0, slot], 0, out_tiles - 1)
            target = jnp.where(slot < count, col, out_tiles)
            total[target] += jnp.dot(grad_ref[row], tile_at(slot), preferred_element_type=jnp.float32)

    @pl.loop(0, jnp.minimum(used, EARLY // GROUP))
    def _(g):
        add_group(g, lambda slot: early_ref[slot])

    @pl.loop(EARLY // GROUP, used)
    def _(g):
        copy(g).wait()
        add_group(g, lambda slot: held[slot - EARLY])

    @pl.loop(0, out_tiles, unroll=4)
    def _(t):
        for cut in range(cuts):
            out_ref[t * cuts + cut] = total[t, :, cut * CHUNK : (cut + 1) * CHUNK].astype(out_ref.dtype)


def tile_products(rows, cols, count, grad, early, tiles, out_tiles):
    slots, tile, _ = tiles.shape
    width = grad.shape[1]
    return pl.pallas_call(
        tile_kernel,
        out_shape=jax.ShapeDtypeStruct((out_tiles * tile // CHUNK, width, CHUNK), jnp.bfloat16),
        in_specs=[HBM, HBM, pl.BlockSpec(memory_space=pltpu.SMEM), VMEM, VMEM, HBM],
        out_specs=VMEM,
        scratch_shapes=[
            pltpu.VMEM((slots - EARLY, tile, tile), jnp.bfloat16),
            pltpu.VMEM((out_tiles + 1, width, tile), jnp.float32),
            pltpu.SMEM(rows.shape, rows.dtype),
            pltpu.SMEM(cols.shape, cols.dtype),
            pltpu.SemaphoreType.DMA(((slots - EARLY) // GROUP,)),
            pltpu.SemaphoreType.DMA((2,)),
        ],
        compiler_params=pltpu.CompilerParams(vmem_limit_bytes=28 << 20),
        cost_estimate=pl.CostEstimate(
            flops=2 * slots * width * tile * tile,
            bytes_accessed=2 * slots * tile * tile,
            transcendentals=0,
        ),
        name="tile_products",
    )(rows, cols, count, grad, early, tiles)


def flow_kernel(
    part_all, weight_hbm, feat_hbm, gf_ref, gw_out,
    first, second, merged, half, y_in, late_in, late, whole, weight_raw, weight_send, weight_in, feat,
    gf_own, gf_send, gf_in, gw_ref, gw_send, mate_in, row_send, row_in, x_send,
    load_sems, send_sems, recv_sems, x_sems, late_sems, gw_sems,
):
    row, col, fib = position()
    l, z = row // RING, lax.rem(row, RING)
    h, x = fib // RING, lax.rem(fib, RING)
    chunks, width, nodes_t = whole.shape[1:]
    pairs, span_t = chunks // 2, 2 * nodes_t
    split = chunks - LATE
    units = split + LATE // 2
    z_up, z_down, z_far = (lax.rem(z + d, RING) for d in (1, RING - 1, 2))
    to_z_up, to_z_down = (l * RING + z_up, col, fib), (l * RING + z_down, col, fib)
    to_x = [(row, col, h * RING + lax.rem(x + d, RING)) for d in range(RING)]
    to_pair = ((1 - l) * RING + z, col, fib)
    to_cross = ((1 - l) * RING + z, col, (1 - h) * RING + x)
    to_far = (row, col, (1 - h) * RING + x)
    mate = (row, 1 - col, fib)
    peers = [(lax.rem(row + d, 8), col, fib) for d in range(1, 8)]

    def nodes_of(p):
        return pl.ds(pl.multiple_of(p * span_t, span_t), span_t)

    load_weight = [
        pltpu.make_async_copy(
            weight_hbm.at[:, k * width : (k + 1) * width], weight_raw.at[k], load_sems.at[1 + k]
        )
        for k in range(2 * RING)
    ]
    load_feat = pltpu.make_async_copy(feat_hbm, feat.at[0], load_sems.at[0])
    for load in load_weight:
        load.start()
    load_feat.start()
    greet([*to_x[1:], to_cross, to_far, mate, *peers])

    def part_at(to_l, to_z, t):
        return part_all.at[(to_l * RING + to_z) * chunks + t]

    def copy(kind, t, source, target, peer):
        return pltpu.make_async_remote_copy(
            source, target, send_sems.at[kind, t], recv_sems.at[kind, t], device_id=peer, device_id_type=MESH
        )

    def late_copy(to_z):
        source = part_all.at[pl.ds(((1 - l) * RING + to_z) * chunks + split, LATE)]
        return pltpu.make_async_remote_copy(
            source, late_in.at[to_z], late_sems.at[0, to_z], late_sems.at[1, to_z], device_id=to_pair, device_id_type=MESH
        )

    def early_share(i, to_z, t):
        return part_at(i, to_z, t)

    def late_share(i, to_z, t):
        return late.at[to_z, t - split, i]

    def link(kind, t, share=early_share):
        if kind == 0:
            return copy(0, t, share(0, z_far, t), first.at[0, t], to_z_up)
        if kind == 1:
            return copy(1, t, share(1, z_far, t), first.at[1, t], to_z_down)
        if kind == 2:
            return copy(2, t, share(1, z_up, t), second.at[0, t, 1], to_z_up)
        if kind == 3:
            return copy(3, t, share(0, z_down, t), second.at[1, t, 0], to_z_down)
        if kind == 4:
            return copy(4, t, merged.at[0, t], second.at[0, t, 0], to_z_up)
        if kind == 5:
            return copy(5, t, merged.at[1, t], second.at[1, t, 1], to_z_down)
        if kind == 6:
            return copy(6, t, half.at[t, 1 - l], y_in.at[0, t], to_pair)
        if kind == 7:
            return copy(7, t, half.at[t, 1 - l], y_in.at[1, t], to_cross)
        if share is late_share:
            both = whole.at[h, pl.ds(2 * t - split, 2)]
            return copy(8, t, both, both, to_far)
        return copy(8, t, half.at[t, l], y_in.at[2, t], to_far)

    def along_x(kind, d, p, source, target, peer=None):
        return pltpu.make_async_remote_copy(
            source,
            target,
            x_sems.at[0, kind, d, p],
            x_sems.at[1, kind, d, p],
            device_id=to_x[d] if peer is None else peer,
            device_id_type=MESH,
        )

    def feat_pass(up, p):
        part = pl.ds(pl.multiple_of(p * span_t + (0 if up else nodes_t), nodes_t), nodes_t)
        source = feat.at[RING - 1 if up else 1, part]
        return along_x(0, 2 if up else 0, p, source, feat.at[2, part], to_x[1 if up else RING - 1])

    def feat_copy(d, p):
        return along_x(0, d, p, feat.at[0, nodes_of(p)], feat.at[RING - d, nodes_of(p)])

    def gf_copy(d, p):
        return along_x(1, d, p, gf_send.at[d - 1, p], gf_in.at[d - 1, p])

    def weight_copy(d):
        return along_x(2, d, 0, weight_send.at[d - 1], weight_in.at[RING - d])

    def added(*refs):
        terms = [r[...].astype(jnp.float32) for r in refs]
        return functools.reduce(lambda a, b: a + b, terms)

    def send_shares(t):
        @pl.when(t < split)
        def _():
            for kind in range(4):
                link(kind, t).start()

        @pl.when(t == split)
        def _():
            for to_z in range(RING):
                late_copy(to_z).wait_recv()

        @pl.when(t >= split)
        def _():
            for to_z in (z_far, z_up, z_down, z):
                for i in range(2):
                    n = 2 * (t - split) + i
                    late[to_z, t - split, i] = added(
                        part_at(l, to_z, split + n), late_in.at[to_z, n]
                    ).astype(late.dtype)
            for kind in range(4):
                link(kind, t, late_share).start()

        @pl.when(t == 0)
        def _():
            for to_z in range(RING):
                late_copy(to_z).start()
            for load in load_weight:
                load.wait()
            for d in range(RING):
                at = lax.rem(x + d, RING)
                block = jnp.concatenate([weight_raw[at], weight_raw[RING + at]], axis=1)
                if d == 0:
                    weight_in[0] = block
                else:
                    weight_send[d - 1] = block
                    weight_copy(d).start()
            gw_ref[...] = jnp.zeros_like(gw_ref)
            load_feat.wait()

        @pl.when(t < pairs)
        def _():
            for d in (1, RING - 1):
                feat_copy(d, t).start()

    def pass_on(t):
        @pl.when(t < pairs)
        def _():
            feat_copy(1, t).wait_recv()
            feat_pass(True, t).start()
            feat_copy(RING - 1, t).wait_recv()
            feat_pass(False, t).start()

    def merge(t):
        def run(share):
            link(0, t, share).wait_recv()
            merged[0, t] = added(share(0, z_up, t), first.at[0, t]).astype(merged.dtype)
            link(4, t, share).start()
            link(1, t, share).wait_recv()
            merged[1, t] = added(share(1, z_down, t), first.at[1, t]).astype(merged.dtype)
            link(5, t, share).start()

        pl.when(t < split)(lambda: run(early_share))
        pl.when(t >= split)(lambda: run(late_share))

    def sum_over_z(t):
        for kind in (2, 3, 4, 5):
            link(kind, t).wait_recv()

        @pl.when(t < split)
        def _():
            for i in range(2):
                half[t, i] = added(part_at(i, z, t), second.at[0, t, i], second.at[1, t, i]).astype(
                    half.dtype
                )
            for kind in (6, 7, 8):
                link(kind, t).start()

        @pl.when(t >= split)
        def _():
            for i in range(2):
                whole[h, 2 * t - split + i] = added(
                    late.at[z, t - split, i], second.at[0, t, i], second.at[1, t, i]
                ).astype(whole.dtype)
            link(8, t, late_share).start()

    def sum_over_y(t):
        @pl.when(t < split)
        def _():
            for kind in (6, 7, 8):
                link(kind, t).wait_recv()
            whole[h, t] = added(half.at[t, l], y_in.at[0, t]).astype(whole.dtype)
            whole[1 - h, t] = added(y_in.at[1, t], y_in.at[2, t]).astype(whole.dtype)

        @pl.when(t >= split)
        def _():
            link(8, t, late_share).wait_recv()

        @pl.when((lax.rem(t, 2) == 1) | (t >= split))
        def _():
            p = jnp.where(t < split, lax.div(t, 2), t - split // 2)
            multiply_features(p)

            @pl.when(p < pairs - 1)
            def _():
                multiply_weight(p)

    def panel_of(p):
        return jnp.concatenate(
            [whole[:, 2 * p + i].reshape(2 * width, nodes_t) for i in range(2)], axis=1
        )

    def multiply_features(p):
        for up in (True, False):
            feat_pass(up, p).wait_recv()
        beside = jnp.concatenate([feat[d, nodes_of(p), :] for d in range(RING)], axis=1)
        gw_ref[...] += jnp.dot(panel_of(p), beside, preferred_element_type=jnp.float32)

    def multiply_weight(p):
        @pl.when(p == 0)
        def _():
            for d in range(1, RING):
                weight_copy(d).wait_recv()

        panel = panel_of(p)
        for d in (2, 1, 3, 0):
            block = jnp.dot(weight_in[d], panel, preferred_element_type=jnp.float32)
            if d == 0:
                gf_own[p] = block
            else:
                gf_send[d - 1, p] = block.astype(gf_send.dtype)
                gf_copy(d, p).start()

    def collect(p):
        for d in range(1, RING):
            gf_copy(d, p).wait_recv()
        block = gf_own[p] + added(*[gf_in.at[d - 1, p] for d in range(1, RING)])
        gf_ref[nodes_of(p), :] = block.T.astype(gf_ref.dtype)

    stages = (send_shares, merge, sum_over_z, sum_over_y, pass_on)

    @pl.loop(0, units + max(LAGS))
    def _(step):
        for late, stage in zip(LAGS, stages):
            t = step - late

            @pl.when((t >= 0) & (t < units))
            def _(stage=stage, t=t):
                stage(t)

    rows = width // 8

    def gw_copy(phase, d, source, target, peer):
        return pltpu.make_async_remote_copy(
            source, target, gw_sems.at[phase, 0, d], gw_sems.at[phase, 1, d], device_id=peer, device_id_type=MESH
        )

    def piece(ref, of, size=rows):
        return ref.at[pl.ds(pl.multiple_of(of * size, size), size)]

    gw_send[...] = gw_ref[pl.ds(pl.multiple_of((1 - col) * width, width), width), :].astype(gw_send.dtype)
    gives = [gw_copy(0, 0, gw_send, mate_in, mate)]
    gives[0].start()
    multiply_weight(pairs - 1)
    gives[0].wait_recv()
    mine = gw_ref[pl.ds(pl.multiple_of(col * width, width), width), :] + mate_in[...].astype(jnp.float32)
    gw_ref[0:width, :] = mine
    row_send[...] = mine.astype(row_send.dtype)
    for d in range(1, 8):
        gives.append(gw_copy(1, d, piece(row_send, lax.rem(row + d, 8)), row_in.at[d], peers[d - 1]))
        gives[-1].start()

    @pl.loop(0, pairs // 2)
    def _(p):
        collect(p)

    @pl.loop(0, split)
    def _(t):
        for kind in range(9):
            link(kind, t).wait_send()

    @pl.loop(split, units)
    def _(t):
        for kind in (0, 1, 2, 3, 4, 5, 8):
            link(kind, t, late_share).wait_send()

    for to_z in range(RING):
        late_copy(to_z).wait_send()

    own = gw_ref[pl.ds(pl.multiple_of(row * rows, rows), rows), :]
    for d in range(1, 8):
        gives[d].wait_recv()
        own += row_in[d].astype(jnp.float32)
    for d in range(RING):
        block = own[:, d * width : (d + 1) * width].astype(gw_out.dtype)
        if d == 0:
            gw_out[col, row, x] = block
        else:
            x_send[d] = block
            gives.append(gw_copy(2, d, x_send.at[d], gw_out.at[col, row, x], to_x[d]))
            gives[-1].start()

    for d in range(1, RING):
        slot = gw_out.at[col, row, lax.rem(x + RING - d, RING)]
        gw_copy(2, d, slot, slot, to_x[d]).wait_recv()
    for d in range(1, 8):
        gives.append(gw_copy(3, d, gw_out.at[col, row], gw_out.at[col, row], peers[d - 1]))
        gives[-1].start()

    @pl.loop(pairs // 2, pairs)
    def _(p):
        collect(p)

    @pl.loop(0, pairs)
    def _(p):
        for up in (True, False):
            feat_pass(up, p).wait_send()
        for d in (1, RING - 1):
            feat_copy(d, p).wait_send()
        for d in range(1, RING):
            gf_copy(d, p).wait_send()

    for d in range(1, RING):
        weight_copy(d).wait_send()
    for d in range(1, 8):
        slot = gw_out.at[col, lax.rem(row + 8 - d, 8)]
        gw_copy(3, d, slot, slot, peers[d - 1]).wait_recv()
    gives.append(gw_copy(0, 1, gw_out.at[col], gw_out.at[col], mate))
    gives[-1].start()
    slot = gw_out.at[1 - col]
    gw_copy(0, 1, slot, slot, mate).wait_recv()
    for give in gives:
        give.wait_send()


def flow(part, weight, features):
    _, width, cut = part.shape
    nodes = features.shape[0]
    chunks = nodes // cut
    pairs = chunks // 2
    piece = (width, cut)
    block = (width, 2 * cut)
    sixteen = jnp.bfloat16
    rows = width // 8
    return pl.pallas_call(
        flow_kernel,
        out_shape=(
            jax.ShapeDtypeStruct((nodes, width), sixteen),
            jax.ShapeDtypeStruct((2, 8, RING, rows, width), sixteen),
        ),
        in_specs=[VMEM, HBM, HBM],
        out_specs=(VMEM, VMEM),
        scratch_shapes=[
            pltpu.VMEM((2, chunks, *piece), sixteen),
            pltpu.VMEM((2, chunks, 2, *piece), sixteen),
            pltpu.VMEM((2, chunks, *piece), sixteen),
            pltpu.VMEM((chunks, 2, *piece), sixteen),
            pltpu.VMEM((3, chunks, *piece), sixteen),
            pltpu.VMEM((RING, LATE, *piece), sixteen),
            pltpu.VMEM((RING, LATE // 2, 2, *piece), sixteen),
            pltpu.VMEM((2, chunks, *piece), sixteen),
            pltpu.VMEM((2 * RING, width, width), sixteen),
            pltpu.VMEM((RING - 1, width, 2 * width), sixteen),
            pltpu.VMEM((RING, width, 2 * width), sixteen),
            pltpu.VMEM((RING, nodes, width), sixteen),
            pltpu.VMEM((pairs, *block), jnp.float32),
            pltpu.VMEM((RING - 1, pairs, *block), sixteen),
            pltpu.VMEM((RING - 1, pairs, *block), sixteen),
            pltpu.VMEM((2 * width, RING * width), jnp.float32),
            pltpu.VMEM((width, RING * width), sixteen),
            pltpu.VMEM((width, RING * width), sixteen),
            pltpu.VMEM((width, RING * width), sixteen),
            pltpu.VMEM((8, rows, RING * width), sixteen),
            pltpu.VMEM((RING, rows, width), sixteen),
            pltpu.SemaphoreType.DMA((1 + 2 * RING,)),
            pltpu.SemaphoreType.DMA((9, chunks)),
            pltpu.SemaphoreType.DMA((9, chunks)),
            pltpu.SemaphoreType.DMA((2, 3, RING, pairs)),
            pltpu.SemaphoreType.DMA((2, RING)),
            pltpu.SemaphoreType.DMA((4, 2, 8)),
        ],
        compiler_params=pltpu.CompilerParams(
            collective_id=1, has_side_effects=True, vmem_limit_bytes=24 << 20
        ),
        cost_estimate=pl.CostEstimate(
            flops=32 * nodes * width * width, bytes_accessed=16 << 20, transcendentals=0
        ),
        name="flow",
    )(part, weight, features)


def finish_kernel(gf_ref, gw_ref, gf_hbm, gw_hbm, gw_turned, sems):
    width = gw_turned.shape[0]
    write_gf = pltpu.make_async_copy(gf_ref, gf_hbm, sems.at[0])
    write_gf.start()
    for side in range(2):
        for x in range(RING):
            target = side * RING + x
            block = gw_ref[side, :, x].reshape(width, width).astype(jnp.float32)
            gw_turned[:, target * width : (target + 1) * width] = block.T
    write_gw = pltpu.make_async_copy(gw_turned, gw_hbm, sems.at[1])
    write_gw.start()
    write_gf.wait()
    write_gw.wait()


def finish(gf, gw):
    width = gf.shape[1]
    turned = (width, 2 * RING * width)
    return pl.pallas_call(
        finish_kernel,
        out_shape=(
            jax.ShapeDtypeStruct(gf.shape, gf.dtype),
            jax.ShapeDtypeStruct(turned, jnp.float32),
        ),
        in_specs=[VMEM, VMEM],
        out_specs=(HBM, HBM),
        scratch_shapes=[pltpu.VMEM(turned, jnp.float32), pltpu.SemaphoreType.DMA((2,))],
        compiler_params=pltpu.CompilerParams(vmem_limit_bytes=4 << 20),
        cost_estimate=pl.CostEstimate(flops=0, bytes_accessed=1 << 20, transcendentals=0),
        name="finish",
    )(gf, gw)


def on_device(features, pre_activation, out_grad, weight, tiles, rows, cols, counts):
    features, pre_activation, out_grad, weight, tiles, rows, cols = (
        pltpu.with_memory_space_constraint(a, pltpu.HBM)
        for a in (features, pre_activation, out_grad, weight, tiles[0, 0], rows, cols)
    )
    grad, early = local_grads(pre_activation, out_grad, tiles)
    out_tiles = 8 * (features.shape[0] // tiles.shape[1])
    part = tile_products(rows, cols, counts, grad, early, tiles, out_tiles)
    return finish(*flow(part, weight, features))


def solution(mesh):
    in_specs = (
        P(("row", "col"), "fib"),
        P(("row", "col"), "fib"),
        P(("row", "col"), "fib"),
        P("fib", None),
        P("row", "col", None, None, None),
        P("row", "col", None),
        P("row", "col", None),
        P("row", "col"),
    )
    out_specs = (P(("row", "col"), "fib"), P("fib", None))
    return jax.shard_map(
        on_device, mesh=mesh, in_specs=in_specs, out_specs=out_specs, check_vma=False
    )
```

```python
import functools

import jax
import jax.numpy as jnp
from jax import lax
from jax.experimental import pallas as pl
from jax.experimental.pallas import tpu as pltpu
from jax.sharding import PartitionSpec as P

GROUP = 16
EARLY = 48
RING = 4
LAGS = (0, 2, 5, 8, 4)
MESH = pl.DeviceIdType.MESH
VMEM = pl.BlockSpec(memory_space=pltpu.VMEM)
HBM = pl.BlockSpec(memory_space=pltpu.HBM)
CHUNK = 128
LATE = 4


def greet(peers):
    barrier = pltpu.get_barrier_semaphore()
    for peer in peers:
        pl.semaphore_signal(barrier, inc=1, device_id=peer, device_id_type=MESH)
    pl.semaphore_wait(barrier, len(peers))


def position():
    return lax.axis_index("row"), lax.axis_index("col"), lax.axis_index("fib")


def grad_kernel(
    pre_hbm, out_grad_hbm, tiles_hbm, grad_ref, early_ref, sums_ref,
    pre_ref, out_grad_ref, load_sems, tile_sems, send_sems, recv_sems,
):
    row, col, fib = position()
    own_tiles = grad_ref.shape[0] // 2
    tile = grad_ref.shape[2]
    partner = (row, 1 - col, fib)

    def loads(t):
        part = pl.ds(pl.multiple_of(t * tile, tile), tile)
        return (
            pltpu.make_async_copy(pre_hbm.at[part], pre_ref.at[part], load_sems.at[0, t]),
            pltpu.make_async_copy(out_grad_hbm.at[part], out_grad_ref.at[part], load_sems.at[1, t]),
        )

    @pl.loop(0, own_tiles)
    def _(t):
        for load in loads(t):
            load.start()

    def early(g):
        group = pl.ds(g * GROUP, GROUP)
        return pltpu.make_async_copy(tiles_hbm.at[group], early_ref.at[group], tile_sems.at[g])

    @pl.loop(0, EARLY // GROUP)
    def _(g):
        early(g).start()

    greet([partner])

    def copy(t, owner):
        slot = grad_ref.at[owner * own_tiles + t]
        return pltpu.make_async_remote_copy(
            slot, slot, send_sems.at[t], recv_sems.at[t], device_id=partner, device_id_type=MESH
        )

    @pl.loop(0, own_tiles)
    def _(t):
        for load in loads(t):
            load.wait()
        part = pl.ds(pl.multiple_of(t * tile, tile), tile)
        pre = pre_ref[part, :].astype(jnp.float32)
        sigmoid = jax.nn.sigmoid(pre)
        grad = out_grad_ref[part, :].astype(jnp.float32) * sigmoid * (1.0 + pre * (1.0 - sigmoid))
        grad_ref[col * own_tiles + t] = grad.T.astype(grad_ref.dtype)
        copy(t, col).start()

    @pl.loop(0, sums_ref.shape[0], unroll=5)
    def _(t):
        sums_ref[t] = jnp.zeros(sums_ref.shape[1:], sums_ref.dtype)

    @pl.loop(0, own_tiles)
    def _(t):
        copy(t, col).wait_send()
        copy(t, 1 - col).wait_recv()

    @pl.loop(0, EARLY // GROUP)
    def _(g):
        early(g).wait()


def local_grads(pre, out_grad, tiles, out_tiles):
    nodes, width = pre.shape
    tile = tiles.shape[1]
    own_tiles = nodes // tile
    return pl.pallas_call(
        grad_kernel,
        out_shape=(
            jax.ShapeDtypeStruct((2 * own_tiles, width, tile), jnp.bfloat16),
            jax.ShapeDtypeStruct((EARLY, tile, tile), tiles.dtype),
            jax.ShapeDtypeStruct((out_tiles + 1, width, tile), jnp.float32),
        ),
        in_specs=[HBM, HBM, HBM],
        out_specs=(VMEM, VMEM, VMEM),
        scratch_shapes=[
            pltpu.VMEM(pre.shape, pre.dtype),
            pltpu.VMEM(pre.shape, pre.dtype),
            pltpu.SemaphoreType.DMA((2, own_tiles)),
            pltpu.SemaphoreType.DMA((EARLY // GROUP,)),
            pltpu.SemaphoreType.DMA((own_tiles,)),
            pltpu.SemaphoreType.DMA((own_tiles,)),
        ],
        compiler_params=pltpu.CompilerParams(
            collective_id=0, has_side_effects=True, vmem_limit_bytes=16 << 20
        ),
        cost_estimate=pl.CostEstimate(
            flops=10 * nodes * width, bytes_accessed=8 * nodes * width, transcendentals=nodes * width
        ),
        name="local_grads",
    )(pre, out_grad, tiles)


def tile_kernel(
    rows_hbm, cols_hbm, count_ref, grad_ref, early_ref, sums_ref, tiles_ref, out_ref, total,
    held, rows_ref, cols_ref, sems, index_sems,
):
    slots, tile, _ = tiles_ref.shape
    cuts = tile // CHUNK
    out_tiles = out_ref.shape[0] // cuts
    row_tiles = grad_ref.shape[0]
    def copy(g):
        source = tiles_ref.at[pl.ds(g * GROUP, GROUP)]
        return pltpu.make_async_copy(
            source, held.at[pl.ds(g * GROUP - EARLY, GROUP)], sems.at[g - EARLY // GROUP]
        )

    indices = [
        pltpu.make_async_copy(source, target, index_sems.at[i])
        for i, (source, target) in enumerate(
            ((rows_hbm, rows_ref), (cols_hbm, cols_ref))
        )
    ]
    for load in indices:
        load.start()
    count = jnp.clip(count_ref[0, 0], 1, slots)
    used = (count + GROUP - 1) // GROUP

    @pl.loop(EARLY // GROUP, used)
    def _(g):
        copy(g).start()

    for load in indices:
        load.wait()

    def add_group(g, tile_at):
        for j in range(GROUP):
            slot = g * GROUP + j
            row = jnp.clip(rows_ref[0, 0, slot], 0, row_tiles - 1)
            col = jnp.clip(cols_ref[0, 0, slot], 0, out_tiles - 1)
            target = jnp.where(slot < count, col, out_tiles)
            total[target] += jnp.dot(grad_ref[row], tile_at(slot), preferred_element_type=jnp.float32)

    @pl.loop(0, jnp.minimum(used, EARLY // GROUP))
    def _(g):
        add_group(g, lambda slot: early_ref[slot])

    @pl.loop(EARLY // GROUP, used)
    def _(g):
        copy(g).wait()
        add_group(g, lambda slot: held[slot - EARLY])

    @pl.loop(0, out_tiles, unroll=4)
    def _(t):
        for cut in range(cuts):
            out_ref[t * cuts + cut] = total[t, :, cut * CHUNK : (cut + 1) * CHUNK].astype(out_ref.dtype)


def tile_products(rows, cols, count, grad, early, sums, tiles, out_tiles):
    slots, tile, _ = tiles.shape
    width = grad.shape[1]
    return pl.pallas_call(
        tile_kernel,
        out_shape=(
            jax.ShapeDtypeStruct((out_tiles * tile // CHUNK, width, CHUNK), jnp.bfloat16),
            jax.ShapeDtypeStruct(sums.shape, sums.dtype),
        ),
        input_output_aliases={5: 1},
        in_specs=[HBM, HBM, pl.BlockSpec(memory_space=pltpu.SMEM), VMEM, VMEM, VMEM, HBM],
        out_specs=(VMEM, VMEM),
        scratch_shapes=[
            pltpu.VMEM((slots - EARLY, tile, tile), jnp.bfloat16),
            pltpu.SMEM(rows.shape, rows.dtype),
            pltpu.SMEM(cols.shape, cols.dtype),
            pltpu.SemaphoreType.DMA(((slots - EARLY) // GROUP,)),
            pltpu.SemaphoreType.DMA((2,)),
        ],
        compiler_params=pltpu.CompilerParams(vmem_limit_bytes=28 << 20),
        cost_estimate=pl.CostEstimate(
            flops=2 * slots * width * tile * tile,
            bytes_accessed=2 * slots * tile * tile,
            transcendentals=0,
        ),
        name="tile_products",
    )(rows, cols, count, grad, early, sums, tiles)[0]


def flow_kernel(
    part_all, weight_hbm, feat_hbm, gf_ref, gw_out,
    first, second, merged, half, y_in, late_in, late, whole, weight_raw, weight_send, weight_in, feat,
    gf_own, gf_send, gf_in, gw_ref, gw_send, mate_in, row_send, row_in, x_send,
    load_sems, send_sems, recv_sems, x_sems, late_sems, gw_sems,
):
    row, col, fib = position()
    l, z = row // RING, lax.rem(row, RING)
    h, x = fib // RING, lax.rem(fib, RING)
    chunks, width, nodes_t = whole.shape[1:]
    pairs, span_t = chunks // 2, 2 * nodes_t
    split = chunks - LATE
    units = split + LATE // 2
    z_up, z_down, z_far = (lax.rem(z + d, RING) for d in (1, RING - 1, 2))
    to_z_up, to_z_down = (l * RING + z_up, col, fib), (l * RING + z_down, col, fib)
    to_x = [(row, col, h * RING + lax.rem(x + d, RING)) for d in range(RING)]
    to_pair = ((1 - l) * RING + z, col, fib)
    to_cross = ((1 - l) * RING + z, col, (1 - h) * RING + x)
    to_far = (row, col, (1 - h) * RING + x)
    mate = (row, 1 - col, fib)
    peers = [(lax.rem(row + d, 8), col, fib) for d in range(1, 8)]

    def nodes_of(p):
        return pl.ds(pl.multiple_of(p * span_t, span_t), span_t)

    load_weight = [
        pltpu.make_async_copy(
            weight_hbm.at[:, k * width : (k + 1) * width], weight_raw.at[k], load_sems.at[1 + k]
        )
        for k in range(2 * RING)
    ]
    load_feat = pltpu.make_async_copy(feat_hbm, feat.at[0], load_sems.at[0])
    for load in load_weight:
        load.start()
    load_feat.start()
    greet([*to_x[1:], to_cross, to_far, mate, *peers])

    def part_at(to_l, to_z, t):
        return part_all.at[(to_l * RING + to_z) * chunks + t]

    def copy(kind, t, source, target, peer):
        return pltpu.make_async_remote_copy(
            source, target, send_sems.at[kind, t], recv_sems.at[kind, t], device_id=peer, device_id_type=MESH
        )

    def late_copy(to_z):
        source = part_all.at[pl.ds(((1 - l) * RING + to_z) * chunks + split, LATE)]
        return pltpu.make_async_remote_copy(
            source, late_in.at[to_z], late_sems.at[0, to_z], late_sems.at[1, to_z], device_id=to_pair, device_id_type=MESH
        )

    def early_share(i, to_z, t):
        return part_at(i, to_z, t)

    def late_share(i, to_z, t):
        return late.at[to_z, t - split, i]

    def link(kind, t, share=early_share):
        if kind == 0:
            return copy(0, t, share(0, z_far, t), first.at[0, t], to_z_up)
        if kind == 1:
            return copy(1, t, share(1, z_far, t), first.at[1, t], to_z_down)
        if kind == 2:
            return copy(2, t, share(1, z_up, t), second.at[0, t, 1], to_z_up)
        if kind == 3:
            return copy(3, t, share(0, z_down, t), second.at[1, t, 0], to_z_down)
        if kind == 4:
            return copy(4, t, merged.at[0, t], second.at[0, t, 0], to_z_up)
        if kind == 5:
            return copy(5, t, merged.at[1, t], second.at[1, t, 1], to_z_down)
        if kind == 6:
            return copy(6, t, half.at[t, 1 - l], y_in.at[0, t], to_pair)
        if kind == 7:
            return copy(7, t, half.at[t, 1 - l], y_in.at[1, t], to_cross)
        if share is late_share:
            both = whole.at[h, pl.ds(2 * t - split, 2)]
            return copy(8, t, both, both, to_far)
        return copy(8, t, half.at[t, l], y_in.at[2, t], to_far)

    def along_x(kind, d, p, source, target, peer=None):
        return pltpu.make_async_remote_copy(
            source,
            target,
            x_sems.at[0, kind, d, p],
            x_sems.at[1, kind, d, p],
            device_id=to_x[d] if peer is None else peer,
            device_id_type=MESH,
        )

    def feat_pass(up, p):
        part = pl.ds(pl.multiple_of(p * span_t + (0 if up else nodes_t), nodes_t), nodes_t)
        source = feat.at[RING - 1 if up else 1, part]
        return along_x(0, 2 if up else 0, p, source, feat.at[2, part], to_x[1 if up else RING - 1])

    def feat_copy(d, p):
        return along_x(0, d, p, feat.at[0, nodes_of(p)], feat.at[RING - d, nodes_of(p)])

    def gf_copy(d, p):
        return along_x(1, d, p, gf_send.at[d - 1, p], gf_in.at[d - 1, p])

    def weight_copy(d):
        return along_x(2, d, 0, weight_send.at[d - 1], weight_in.at[RING - d])

    def added(*refs):
        terms = [r[...].astype(jnp.float32) for r in refs]
        return functools.reduce(lambda a, b: a + b, terms)

    def send_shares(t):
        @pl.when(t < split)
        def _():
            for kind in range(4):
                link(kind, t).start()

        @pl.when(t == split)
        def _():
            for to_z in range(RING):
                late_copy(to_z).wait_recv()

        @pl.when(t >= split)
        def _():
            for to_z in (z_far, z_up, z_down, z):
                for i in range(2):
                    n = 2 * (t - split) + i
                    late[to_z, t - split, i] = added(
                        part_at(l, to_z, split + n), late_in.at[to_z, n]
                    ).astype(late.dtype)
            for kind in range(4):
                link(kind, t, late_share).start()

        @pl.when(t == 0)
        def _():
            for to_z in range(RING):
                late_copy(to_z).start()
            for load in load_weight:
                load.wait()
            for d in range(RING):
                at = lax.rem(x + d, RING)
                block = jnp.concatenate([weight_raw[at], weight_raw[RING + at]], axis=1)
                if d == 0:
                    weight_in[0] = block
                else:
                    weight_send[d - 1] = block
                    weight_copy(d).start()
            gw_ref[...] = jnp.zeros_like(gw_ref)
            load_feat.wait()

        @pl.when(t < pairs)
        def _():
            for d in (1, RING - 1):
                feat_copy(d, t).start()

    def pass_on(t):
        @pl.when(t < pairs)
        def _():
            feat_copy(1, t).wait_recv()
            feat_pass(True, t).start()
            feat_copy(RING - 1, t).wait_recv()
            feat_pass(False, t).start()

    def merge(t):
        def run(share):
            link(0, t, share).wait_recv()
            merged[0, t] = added(share(0, z_up, t), first.at[0, t]).astype(merged.dtype)
            link(4, t, share).start()
            link(1, t, share).wait_recv()
            merged[1, t] = added(share(1, z_down, t), first.at[1, t]).astype(merged.dtype)
            link(5, t, share).start()

        pl.when(t < split)(lambda: run(early_share))
        pl.when(t >= split)(lambda: run(late_share))

    def sum_over_z(t):
        for kind in (2, 3, 4, 5):
            link(kind, t).wait_recv()

        @pl.when(t < split)
        def _():
            for i in range(2):
                half[t, i] = added(part_at(i, z, t), second.at[0, t, i], second.at[1, t, i]).astype(
                    half.dtype
                )
            for kind in (6, 7, 8):
                link(kind, t).start()

        @pl.when(t >= split)
        def _():
            for i in range(2):
                whole[h, 2 * t - split + i] = added(
                    late.at[z, t - split, i], second.at[0, t, i], second.at[1, t, i]
                ).astype(whole.dtype)
            link(8, t, late_share).start()

    def sum_over_y(t):
        @pl.when(t < split)
        def _():
            for kind in (6, 7, 8):
                link(kind, t).wait_recv()
            whole[h, t] = added(half.at[t, l], y_in.at[0, t]).astype(whole.dtype)
            whole[1 - h, t] = added(y_in.at[1, t], y_in.at[2, t]).astype(whole.dtype)
            for kind in range(9):
                link(kind, t).wait_send()

        @pl.when(t >= split)
        def _():
            link(8, t, late_share).wait_recv()

        @pl.when((lax.rem(t, 2) == 1) | (t >= split))
        def _():
            p = jnp.where(t < split, lax.div(t, 2), t - split // 2)
            multiply_features(p)

            @pl.when(p < pairs - 1)
            def _():
                multiply_weight(p)

    def panel_of(p):
        return jnp.concatenate(
            [whole[:, 2 * p + i].reshape(2 * width, nodes_t) for i in range(2)], axis=1
        )

    def multiply_features(p):
        for up in (True, False):
            feat_pass(up, p).wait_recv()
        beside = jnp.concatenate([feat[d, nodes_of(p), :] for d in range(RING)], axis=1)
        gw_ref[...] += jnp.dot(panel_of(p), beside, preferred_element_type=jnp.float32)

    def multiply_weight(p):
        @pl.when(p == 0)
        def _():
            for d in range(1, RING):
                weight_copy(d).wait_recv()

        panel = panel_of(p)
        for d in (2, 1, 3, 0):
            block = jnp.dot(weight_in[d], panel, preferred_element_type=jnp.float32)
            if d == 0:
                gf_own[p] = block
            else:
                gf_send[d - 1, p] = block.astype(gf_send.dtype)
                gf_copy(d, p).start()

    def collect(p):
        for d in range(1, RING):
            gf_copy(d, p).wait_recv()
        block = gf_own[p] + added(*[gf_in.at[d - 1, p] for d in range(1, RING)])
        gf_ref[nodes_of(p), :] = block.T.astype(gf_ref.dtype)

    stages = (send_shares, merge, sum_over_z, sum_over_y, pass_on)

    @pl.loop(0, units + max(LAGS))
    def _(step):
        for late, stage in zip(LAGS, stages):
            t = step - late

            @pl.when((t >= 0) & (t < units))
            def _(stage=stage, t=t):
                stage(t)

    rows = width // 8

    def gw_copy(phase, d, source, target, peer):
        return pltpu.make_async_remote_copy(
            source, target, gw_sems.at[phase, 0, d], gw_sems.at[phase, 1, d], device_id=peer, device_id_type=MESH
        )

    def piece(ref, of, size=rows):
        return ref.at[pl.ds(pl.multiple_of(of * size, size), size)]

    gw_send[...] = gw_ref[pl.ds(pl.multiple_of((1 - col) * width, width), width), :].astype(gw_send.dtype)
    gives = [gw_copy(0, 0, gw_send, mate_in, mate)]
    gives[0].start()
    multiply_weight(pairs - 1)
    gives[0].wait_recv()
    mine = gw_ref[pl.ds(pl.multiple_of(col * width, width), width), :] + mate_in[...].astype(jnp.float32)
    gw_ref[0:width, :] = mine
    row_send[...] = mine.astype(row_send.dtype)
    for d in range(1, 8):
        gives.append(gw_copy(1, d, piece(row_send, lax.rem(row + d, 8)), row_in.at[d], peers[d - 1]))
        gives[-1].start()

    @pl.loop(0, pairs // 2)
    def _(p):
        collect(p)

    for to_z in range(RING):
        late_copy(to_z).wait_send()

    @pl.loop(split, units)
    def _(t):
        for kind in (0, 1, 2, 3, 4, 5, 8):
            link(kind, t, late_share).wait_send()

    own = gw_ref[pl.ds(pl.multiple_of(row * rows, rows), rows), :]
    for d in range(1, 8):
        gives[d].wait_recv()
        own += row_in[d].astype(jnp.float32)
    for d in range(RING):
        block = own[:, d * width : (d + 1) * width].astype(gw_out.dtype)
        if d == 0:
            gw_out[col, row, x] = block
        else:
            x_send[d] = block
            gives.append(gw_copy(2, d, x_send.at[d], gw_out.at[col, row, x], to_x[d]))
            gives[-1].start()

    for d in range(1, RING):
        slot = gw_out.at[col, row, lax.rem(x + RING - d, RING)]
        gw_copy(2, d, slot, slot, to_x[d]).wait_recv()
    for d in range(1, 8):
        gives.append(gw_copy(3, d, gw_out.at[col, row], gw_out.at[col, row], peers[d - 1]))
        gives[-1].start()

    @pl.loop(pairs // 2, pairs)
    def _(p):
        collect(p)

    @pl.loop(0, pairs)
    def _(p):
        for up in (True, False):
            feat_pass(up, p).wait_send()
        for d in (1, RING - 1):
            feat_copy(d, p).wait_send()
        for d in range(1, RING):
            gf_copy(d, p).wait_send()

    for d in range(1, RING):
        weight_copy(d).wait_send()
    def hand_on(d, of_col):
        slot = gw_out.at[of_col, lax.rem(row + 8 - d, 8)]
        return gw_copy(4, d, slot, slot, mate)

    gives.append(hand_on(0, col))
    gives[-1].start()
    for d in range(1, 8):
        slot = gw_out.at[col, lax.rem(row + 8 - d, 8)]
        gw_copy(3, d, slot, slot, peers[d - 1]).wait_recv()
        gives.append(hand_on(d, col))
        gives[-1].start()
    for d in range(8):
        hand_on(d, 1 - col).wait_recv()
    for give in gives:
        give.wait_send()


def flow(part, weight, features):
    _, width, cut = part.shape
    nodes = features.shape[0]
    chunks = nodes // cut
    pairs = chunks // 2
    piece = (width, cut)
    block = (width, 2 * cut)
    sixteen = jnp.bfloat16
    rows = width // 8
    return pl.pallas_call(
        flow_kernel,
        out_shape=(
            jax.ShapeDtypeStruct((nodes, width), sixteen),
            jax.ShapeDtypeStruct((2, 8, RING, rows, width), sixteen),
        ),
        in_specs=[VMEM, HBM, HBM],
        out_specs=(VMEM, VMEM),
        scratch_shapes=[
            pltpu.VMEM((2, chunks, *piece), sixteen),
            pltpu.VMEM((2, chunks, 2, *piece), sixteen),
            pltpu.VMEM((2, chunks, *piece), sixteen),
            pltpu.VMEM((chunks, 2, *piece), sixteen),
            pltpu.VMEM((3, chunks, *piece), sixteen),
            pltpu.VMEM((RING, LATE, *piece), sixteen),
            pltpu.VMEM((RING, LATE // 2, 2, *piece), sixteen),
            pltpu.VMEM((2, chunks, *piece), sixteen),
            pltpu.VMEM((2 * RING, width, width), sixteen),
            pltpu.VMEM((RING - 1, width, 2 * width), sixteen),
            pltpu.VMEM((RING, width, 2 * width), sixteen),
            pltpu.VMEM((RING, nodes, width), sixteen),
            pltpu.VMEM((pairs, *block), jnp.float32),
            pltpu.VMEM((RING - 1, pairs, *block), sixteen),
            pltpu.VMEM((RING - 1, pairs, *block), sixteen),
            pltpu.VMEM((2 * width, RING * width), jnp.float32),
            pltpu.VMEM((width, RING * width), sixteen),
            pltpu.VMEM((width, RING * width), sixteen),
            pltpu.VMEM((width, RING * width), sixteen),
            pltpu.VMEM((8, rows, RING * width), sixteen),
            pltpu.VMEM((RING, rows, width), sixteen),
            pltpu.SemaphoreType.DMA((1 + 2 * RING,)),
            pltpu.SemaphoreType.DMA((9, chunks)),
            pltpu.SemaphoreType.DMA((9, chunks)),
            pltpu.SemaphoreType.DMA((2, 3, RING, pairs)),
            pltpu.SemaphoreType.DMA((2, RING)),
            pltpu.SemaphoreType.DMA((5, 2, 8)),
        ],
        compiler_params=pltpu.CompilerParams(
            collective_id=1, has_side_effects=True, vmem_limit_bytes=24 << 20
        ),
        cost_estimate=pl.CostEstimate(
            flops=32 * nodes * width * width, bytes_accessed=16 << 20, transcendentals=0
        ),
        name="flow",
    )(part, weight, features)


def finish_kernel(gf_ref, gw_ref, gf_hbm, gw_hbm, gw_turned, sems):
    width = gw_turned.shape[0]
    write_gf = pltpu.make_async_copy(gf_ref, gf_hbm, sems.at[0])
    write_gf.start()
    for side in range(2):
        for x in range(RING):
            target = side * RING + x
            block = gw_ref[side, :, x].reshape(width, width).astype(jnp.float32)
            gw_turned[:, target * width : (target + 1) * width] = block.T
    write_gw = pltpu.make_async_copy(gw_turned, gw_hbm, sems.at[1])
    write_gw.start()
    write_gf.wait()
    write_gw.wait()


def finish(gf, gw):
    width = gf.shape[1]
    turned = (width, 2 * RING * width)
    return pl.pallas_call(
        finish_kernel,
        out_shape=(
            jax.ShapeDtypeStruct(gf.shape, gf.dtype),
            jax.ShapeDtypeStruct(turned, jnp.float32),
        ),
        in_specs=[VMEM, VMEM],
        out_specs=(HBM, HBM),
        scratch_shapes=[pltpu.VMEM(turned, jnp.float32), pltpu.SemaphoreType.DMA((2,))],
        compiler_params=pltpu.CompilerParams(vmem_limit_bytes=4 << 20),
        cost_estimate=pl.CostEstimate(flops=0, bytes_accessed=1 << 20, transcendentals=0),
        name="finish",
    )(gf, gw)


def on_device(features, pre_activation, out_grad, weight, tiles, rows, cols, counts):
    features, pre_activation, out_grad, weight, tiles, rows, cols = (
        pltpu.with_memory_space_constraint(a, pltpu.HBM)
        for a in (features, pre_activation, out_grad, weight, tiles[0, 0], rows, cols)
    )
    out_tiles = 8 * (features.shape[0] // tiles.shape[1])
    grad, early, sums = local_grads(pre_activation, out_grad, tiles, out_tiles)
    part = tile_products(rows, cols, counts, grad, early, sums, tiles, out_tiles)
    return finish(*flow(part, weight, features))


def solution(mesh):
    in_specs = (
        P(("row", "col"), "fib"),
        P(("row", "col"), "fib"),
        P(("row", "col"), "fib"),
        P("fib", None),
        P("row", "col", None, None, None),
        P("row", "col", None),
        P("row", "col", None),
        P("row", "col"),
    )
    out_specs = (P(("row", "col"), "fib"), P("fib", None))
    return jax.shard_map(
        on_device, mesh=mesh, in_specs=in_specs, out_specs=out_specs, check_vma=False
    )
```

```python
import functools

import jax
import jax.numpy as jnp
from jax import lax
from jax.experimental import pallas as pl
from jax.experimental.pallas import tpu as pltpu
from jax.sharding import PartitionSpec as P

GROUP = 16
EARLY = 48
RING = 4
LAGS = (0, 2, 5, 8, 4)
MESH = pl.DeviceIdType.MESH
VMEM = pl.BlockSpec(memory_space=pltpu.VMEM)
HBM = pl.BlockSpec(memory_space=pltpu.HBM)
SMEM = pl.BlockSpec(memory_space=pltpu.SMEM)
CHUNK = 128
LATE = 4


def greet(peers):
    barrier = pltpu.get_barrier_semaphore()
    for peer in peers:
        pl.semaphore_signal(barrier, inc=1, device_id=peer, device_id_type=MESH)
    pl.semaphore_wait(barrier, len(peers))


def position():
    return lax.axis_index("row"), lax.axis_index("col"), lax.axis_index("fib")


def grad_kernel(
    pre_hbm, out_grad_hbm, tiles_hbm, rows_hbm, cols_hbm,
    grad_ref, early_ref, sums_ref, rows_ref, cols_ref,
    pre_ref, out_grad_ref, load_sems, tile_sems, index_sems, send_sems, recv_sems,
):
    row, col, fib = position()
    own_tiles = grad_ref.shape[0] // 2
    tile = grad_ref.shape[2]
    partner = (row, 1 - col, fib)

    def loads(t):
        part = pl.ds(pl.multiple_of(t * tile, tile), tile)
        return (
            pltpu.make_async_copy(pre_hbm.at[part], pre_ref.at[part], load_sems.at[0, t]),
            pltpu.make_async_copy(out_grad_hbm.at[part], out_grad_ref.at[part], load_sems.at[1, t]),
        )

    @pl.loop(0, own_tiles)
    def _(t):
        for load in loads(t):
            load.start()

    def early(g):
        group = pl.ds(g * GROUP, GROUP)
        return pltpu.make_async_copy(tiles_hbm.at[group], early_ref.at[group], tile_sems.at[g])

    @pl.loop(0, EARLY // GROUP)
    def _(g):
        early(g).start()

    indices = [
        pltpu.make_async_copy(source, target, index_sems.at[i])
        for i, (source, target) in enumerate(((rows_hbm, rows_ref), (cols_hbm, cols_ref)))
    ]
    for load in indices:
        load.start()
    greet([partner])

    def copy(t, owner):
        slot = grad_ref.at[owner * own_tiles + t]
        return pltpu.make_async_remote_copy(
            slot, slot, send_sems.at[t], recv_sems.at[t], device_id=partner, device_id_type=MESH
        )

    @pl.loop(0, own_tiles)
    def _(t):
        for load in loads(t):
            load.wait()
        part = pl.ds(pl.multiple_of(t * tile, tile), tile)
        pre = pre_ref[part, :].astype(jnp.float32)
        sigmoid = jax.nn.sigmoid(pre)
        grad = out_grad_ref[part, :].astype(jnp.float32) * sigmoid * (1.0 + pre * (1.0 - sigmoid))
        grad_ref[col * own_tiles + t] = grad.T.astype(grad_ref.dtype)
        copy(t, col).start()

    @pl.loop(0, sums_ref.shape[0], unroll=5)
    def _(t):
        sums_ref[t] = jnp.zeros(sums_ref.shape[1:], sums_ref.dtype)

    @pl.loop(0, own_tiles)
    def _(t):
        copy(t, col).wait_send()
        copy(t, 1 - col).wait_recv()

    @pl.loop(0, EARLY // GROUP)
    def _(g):
        early(g).wait()

    for load in indices:
        load.wait()


def local_grads(pre, out_grad, tiles, rows, cols, out_tiles):
    nodes, width = pre.shape
    tile = tiles.shape[1]
    own_tiles = nodes // tile
    return pl.pallas_call(
        grad_kernel,
        out_shape=(
            jax.ShapeDtypeStruct((2 * own_tiles, width, tile), jnp.bfloat16),
            jax.ShapeDtypeStruct((EARLY, tile, tile), tiles.dtype),
            jax.ShapeDtypeStruct((out_tiles + 1, width, tile), jnp.float32),
            jax.ShapeDtypeStruct(rows.shape, rows.dtype),
            jax.ShapeDtypeStruct(cols.shape, cols.dtype),
        ),
        in_specs=[HBM] * 5,
        out_specs=(VMEM, VMEM, VMEM, SMEM, SMEM),
        scratch_shapes=[
            pltpu.VMEM(pre.shape, pre.dtype),
            pltpu.VMEM(pre.shape, pre.dtype),
            pltpu.SemaphoreType.DMA((2, own_tiles)),
            pltpu.SemaphoreType.DMA((EARLY // GROUP,)),
            pltpu.SemaphoreType.DMA((2,)),
            pltpu.SemaphoreType.DMA((own_tiles,)),
            pltpu.SemaphoreType.DMA((own_tiles,)),
        ],
        compiler_params=pltpu.CompilerParams(
            collective_id=0, has_side_effects=True, vmem_limit_bytes=16 << 20
        ),
        cost_estimate=pl.CostEstimate(
            flops=10 * nodes * width, bytes_accessed=8 * nodes * width, transcendentals=nodes * width
        ),
        name="local_grads",
    )(pre, out_grad, tiles, rows, cols)


def tile_kernel(
    rows_ref, cols_ref, count_ref, grad_ref, early_ref, sums_ref, tiles_ref, out_ref, total,
    held, sems,
):
    slots, tile, _ = tiles_ref.shape
    cuts = tile // CHUNK
    out_tiles = out_ref.shape[0] // cuts
    row_tiles = grad_ref.shape[0]
    def copy(g):
        source = tiles_ref.at[pl.ds(g * GROUP, GROUP)]
        return pltpu.make_async_copy(
            source, held.at[pl.ds(g * GROUP - EARLY, GROUP)], sems.at[g - EARLY // GROUP]
        )

    count = jnp.clip(count_ref[0, 0], 1, slots)
    used = (count + GROUP - 1) // GROUP

    @pl.loop(EARLY // GROUP, used)
    def _(g):
        copy(g).start()

    def add_group(g, tile_at):
        for j in range(GROUP):
            slot = g * GROUP + j
            row = jnp.clip(rows_ref[0, 0, slot], 0, row_tiles - 1)
            col = jnp.clip(cols_ref[0, 0, slot], 0, out_tiles - 1)
            target = jnp.where(slot < count, col, out_tiles)
            total[target] += jnp.dot(grad_ref[row], tile_at(slot), preferred_element_type=jnp.float32)

    @pl.loop(0, jnp.minimum(used, EARLY // GROUP))
    def _(g):
        add_group(g, lambda slot: early_ref[slot])

    @pl.loop(EARLY // GROUP, used)
    def _(g):
        copy(g).wait()
        add_group(g, lambda slot: held[slot - EARLY])

    @pl.loop(0, out_tiles, unroll=4)
    def _(t):
        for cut in range(cuts):
            out_ref[t * cuts + cut] = total[t, :, cut * CHUNK : (cut + 1) * CHUNK].astype(out_ref.dtype)


def tile_products(rows, cols, count, grad, early, sums, tiles, out_tiles):
    slots, tile, _ = tiles.shape
    width = grad.shape[1]
    return pl.pallas_call(
        tile_kernel,
        out_shape=(
            jax.ShapeDtypeStruct((out_tiles * tile // CHUNK, width, CHUNK), jnp.bfloat16),
            jax.ShapeDtypeStruct(sums.shape, sums.dtype),
        ),
        input_output_aliases={5: 1},
        in_specs=[SMEM, SMEM, SMEM, VMEM, VMEM, VMEM, HBM],
        out_specs=(VMEM, VMEM),
        scratch_shapes=[
            pltpu.VMEM((slots - EARLY, tile, tile), jnp.bfloat16),
            pltpu.SemaphoreType.DMA(((slots - EARLY) // GROUP,)),
        ],
        compiler_params=pltpu.CompilerParams(vmem_limit_bytes=28 << 20),
        cost_estimate=pl.CostEstimate(
            flops=2 * slots * width * tile * tile,
            bytes_accessed=2 * slots * tile * tile,
            transcendentals=0,
        ),
        name="tile_products",
    )(rows, cols, count, grad, early, sums, tiles)[0]


def flow_kernel(
    part_all, weight_hbm, feat_hbm, gf_ref, gw_out,
    first, second, merged, half, y_in, late_in, late, whole, weight_raw, weight_send, weight_in, feat,
    gf_own, gf_send, gf_in, gw_ref, gw_send, mate_in, row_send, row_in, x_send,
    load_sems, send_sems, recv_sems, x_sems, late_sems, gw_sems,
):
    row, col, fib = position()
    l, z = row // RING, lax.rem(row, RING)
    h, x = fib // RING, lax.rem(fib, RING)
    chunks, width, nodes_t = whole.shape[1:]
    pairs, span_t = chunks // 2, 2 * nodes_t
    split = chunks - LATE
    units = split + LATE // 2
    z_up, z_down, z_far = (lax.rem(z + d, RING) for d in (1, RING - 1, 2))
    to_z_up, to_z_down = (l * RING + z_up, col, fib), (l * RING + z_down, col, fib)
    to_x = [(row, col, h * RING + lax.rem(x + d, RING)) for d in range(RING)]
    to_pair = ((1 - l) * RING + z, col, fib)
    to_cross = ((1 - l) * RING + z, col, (1 - h) * RING + x)
    to_far = (row, col, (1 - h) * RING + x)
    mate = (row, 1 - col, fib)
    peers = [(lax.rem(row + d, 8), col, fib) for d in range(1, 8)]

    def nodes_of(p):
        return pl.ds(pl.multiple_of(p * span_t, span_t), span_t)

    load_weight = [
        pltpu.make_async_copy(
            weight_hbm.at[:, k * width : (k + 1) * width], weight_raw.at[k], load_sems.at[1 + k]
        )
        for k in range(2 * RING)
    ]
    load_feat = pltpu.make_async_copy(feat_hbm, feat.at[0], load_sems.at[0])
    for load in load_weight:
        load.start()
    load_feat.start()
    greet([*to_x[1:], to_cross, to_far, mate, *peers])

    def part_at(to_l, to_z, t):
        return part_all.at[(to_l * RING + to_z) * chunks + t]

    def copy(kind, t, source, target, peer):
        return pltpu.make_async_remote_copy(
            source, target, send_sems.at[kind, t], recv_sems.at[kind, t], device_id=peer, device_id_type=MESH
        )

    def late_copy(to_z):
        source = part_all.at[pl.ds(((1 - l) * RING + to_z) * chunks + split, LATE)]
        return pltpu.make_async_remote_copy(
            source, late_in.at[to_z], late_sems.at[0, to_z], late_sems.at[1, to_z], device_id=to_pair, device_id_type=MESH
        )

    def early_share(i, to_z, t):
        return part_at(i, to_z, t)

    def late_share(i, to_z, t):
        return late.at[to_z, t - split, i]

    def link(kind, t, share=early_share):
        if kind == 0:
            return copy(0, t, share(0, z_far, t), first.at[0, t], to_z_up)
        if kind == 1:
            return copy(1, t, share(1, z_far, t), first.at[1, t], to_z_down)
        if kind == 2:
            return copy(2, t, share(1, z_up, t), second.at[0, t, 1], to_z_up)
        if kind == 3:
            return copy(3, t, share(0, z_down, t), second.at[1, t, 0], to_z_down)
        if kind == 4:
            return copy(4, t, merged.at[0, t], second.at[0, t, 0], to_z_up)
        if kind == 5:
            return copy(5, t, merged.at[1, t], second.at[1, t, 1], to_z_down)
        if kind == 6:
            return copy(6, t, half.at[t, 1 - l], y_in.at[0, t], to_pair)
        if kind == 7:
            return copy(7, t, half.at[t, 1 - l], y_in.at[1, t], to_cross)
        if share is late_share:
            both = whole.at[h, pl.ds(2 * t - split, 2)]
            return copy(8, t, both, both, to_far)
        return copy(8, t, half.at[t, l], y_in.at[2, t], to_far)

    def along_x(kind, d, p, source, target, peer=None):
        return pltpu.make_async_remote_copy(
            source,
            target,
            x_sems.at[0, kind, d, p],
            x_sems.at[1, kind, d, p],
            device_id=to_x[d] if peer is None else peer,
            device_id_type=MESH,
        )

    def feat_pass(up, p):
        part = pl.ds(pl.multiple_of(p * span_t + (0 if up else nodes_t), nodes_t), nodes_t)
        source = feat.at[RING - 1 if up else 1, part]
        return along_x(0, 2 if up else 0, p, source, feat.at[2, part], to_x[1 if up else RING - 1])

    def feat_copy(d, p):
        return along_x(0, d, p, feat.at[0, nodes_of(p)], feat.at[RING - d, nodes_of(p)])

    def gf_copy(d, p):
        return along_x(1, d, p, gf_send.at[d - 1, p], gf_in.at[d - 1, p])

    def weight_copy(d):
        return along_x(2, d, 0, weight_send.at[d - 1], weight_in.at[RING - d])

    def added(*refs):
        terms = [r[...].astype(jnp.float32) for r in refs]
        return functools.reduce(lambda a, b: a + b, terms)

    def send_shares(t):
        @pl.when(t < split)
        def _():
            for kind in range(4):
                link(kind, t).start()

        @pl.when(t == split)
        def _():
            for to_z in range(RING):
                late_copy(to_z).wait_recv()

        @pl.when(t >= split)
        def _():
            for to_z in (z_far, z_up, z_down, z):
                for i in range(2):
                    n = 2 * (t - split) + i
                    late[to_z, t - split, i] = added(
                        part_at(l, to_z, split + n), late_in.at[to_z, n]
                    ).astype(late.dtype)
            for kind in range(4):
                link(kind, t, late_share).start()

        @pl.when(t == 0)
        def _():
            for to_z in range(RING):
                late_copy(to_z).start()
            for load in load_weight:
                load.wait()
            for d in range(RING):
                at = lax.rem(x + d, RING)
                block = jnp.concatenate([weight_raw[at], weight_raw[RING + at]], axis=1)
                if d == 0:
                    weight_in[0] = block
                else:
                    weight_send[d - 1] = block
                    weight_copy(d).start()
            gw_ref[...] = jnp.zeros_like(gw_ref)
            load_feat.wait()

        @pl.when(t < pairs)
        def _():
            for d in (1, RING - 1):
                feat_copy(d, t).start()

    def pass_on(t):
        @pl.when(t < pairs)
        def _():
            feat_copy(1, t).wait_recv()
            feat_pass(True, t).start()
            feat_copy(RING - 1, t).wait_recv()
            feat_pass(False, t).start()

    def merge(t):
        def run(share):
            link(0, t, share).wait_recv()
            merged[0, t] = added(share(0, z_up, t), first.at[0, t]).astype(merged.dtype)
            link(4, t, share).start()
            link(1, t, share).wait_recv()
            merged[1, t] = added(share(1, z_down, t), first.at[1, t]).astype(merged.dtype)
            link(5, t, share).start()

        pl.when(t < split)(lambda: run(early_share))
        pl.when(t >= split)(lambda: run(late_share))

    def sum_over_z(t):
        for kind in (2, 3, 4, 5):
            link(kind, t).wait_recv()

        @pl.when(t < split)
        def _():
            for i in range(2):
                half[t, i] = added(part_at(i, z, t), second.at[0, t, i], second.at[1, t, i]).astype(
                    half.dtype
                )
            for kind in (6, 7, 8):
                link(kind, t).start()

        @pl.when(t >= split)
        def _():
            for i in range(2):
                whole[h, 2 * t - split + i] = added(
                    late.at[z, t - split, i], second.at[0, t, i], second.at[1, t, i]
                ).astype(whole.dtype)
            link(8, t, late_share).start()

    def sum_over_y(t):
        @pl.when(t < split)
        def _():
            for kind in (6, 7, 8):
                link(kind, t).wait_recv()
            whole[h, t] = added(half.at[t, l], y_in.at[0, t]).astype(whole.dtype)
            whole[1 - h, t] = added(y_in.at[1, t], y_in.at[2, t]).astype(whole.dtype)
            for kind in range(9):
                link(kind, t).wait_send()

        @pl.when(t >= split)
        def _():
            link(8, t, late_share).wait_recv()

        @pl.when((lax.rem(t, 2) == 1) | (t >= split))
        def _():
            p = jnp.where(t < split, lax.div(t, 2), t - split // 2)
            multiply_features(p)

            @pl.when(p < pairs - 1)
            def _():
                multiply_weight(p)

    def panel_of(p):
        return jnp.concatenate(
            [whole[:, 2 * p + i].reshape(2 * width, nodes_t) for i in range(2)], axis=1
        )

    def multiply_features(p):
        for up in (True, False):
            feat_pass(up, p).wait_recv()
        beside = jnp.concatenate([feat[d, nodes_of(p), :] for d in range(RING)], axis=1)
        gw_ref[...] += jnp.dot(panel_of(p), beside, preferred_element_type=jnp.float32)

    def multiply_weight(p):
        @pl.when(p == 0)
        def _():
            for d in range(1, RING):
                weight_copy(d).wait_recv()

        panel = panel_of(p)
        for d in (2, 1, 3, 0):
            block = jnp.dot(weight_in[d], panel, preferred_element_type=jnp.float32)
            if d == 0:
                gf_own[p] = block
            else:
                gf_send[d - 1, p] = block.astype(gf_send.dtype)
                gf_copy(d, p).start()

    def collect(p):
        for d in range(1, RING):
            gf_copy(d, p).wait_recv()
        block = gf_own[p] + added(*[gf_in.at[d - 1, p] for d in range(1, RING)])
        gf_ref[nodes_of(p), :] = block.T.astype(gf_ref.dtype)

    stages = (send_shares, merge, sum_over_z, sum_over_y, pass_on)

    @pl.loop(0, units + max(LAGS))
    def _(step):
        for late, stage in zip(LAGS, stages):
            t = step - late

            @pl.when((t >= 0) & (t < units))
            def _(stage=stage, t=t):
                stage(t)

    rows = width // 8

    def gw_copy(phase, d, source, target, peer):
        return pltpu.make_async_remote_copy(
            source, target, gw_sems.at[phase, 0, d], gw_sems.at[phase, 1, d], device_id=peer, device_id_type=MESH
        )

    def piece(ref, of, size=rows):
        return ref.at[pl.ds(pl.multiple_of(of * size, size), size)]

    gw_send[...] = gw_ref[pl.ds(pl.multiple_of((1 - col) * width, width), width), :].astype(gw_send.dtype)
    gives = [gw_copy(0, 0, gw_send, mate_in, mate)]
    gives[0].start()
    multiply_weight(pairs - 1)
    gives[0].wait_recv()
    mine = gw_ref[pl.ds(pl.multiple_of(col * width, width), width), :] + mate_in[...].astype(jnp.float32)
    gw_ref[0:width, :] = mine
    row_send[...] = mine.astype(row_send.dtype)
    for d in range(1, 8):
        gives.append(gw_copy(1, d, piece(row_send, lax.rem(row + d, 8)), row_in.at[d], peers[d - 1]))
        gives[-1].start()

    @pl.loop(0, pairs // 2)
    def _(p):
        collect(p)

    for to_z in range(RING):
        late_copy(to_z).wait_send()

    @pl.loop(split, units)
    def _(t):
        for kind in (0, 1, 2, 3, 4, 5, 8):
            link(kind, t, late_share).wait_send()

    own = gw_ref[pl.ds(pl.multiple_of(row * rows, rows), rows), :]
    for d in range(1, 8):
        gives[d].wait_recv()
        own += row_in[d].astype(jnp.float32)
    for d in range(RING):
        block = own[:, d * width : (d + 1) * width].astype(gw_out.dtype)
        if d == 0:
            gw_out[col, row, x] = block
        else:
            x_send[d] = block
            gives.append(gw_copy(2, d, x_send.at[d], gw_out.at[col, row, x], to_x[d]))
            gives[-1].start()

    for d in range(1, RING):
        slot = gw_out.at[col, row, lax.rem(x + RING - d, RING)]
        gw_copy(2, d, slot, slot, to_x[d]).wait_recv()
    for d in range(1, 8):
        gives.append(gw_copy(3, d, gw_out.at[col, row], gw_out.at[col, row], peers[d - 1]))
        gives[-1].start()

    @pl.loop(pairs // 2, pairs)
    def _(p):
        collect(p)

    @pl.loop(0, pairs)
    def _(p):
        for up in (True, False):
            feat_pass(up, p).wait_send()
        for d in (1, RING - 1):
            feat_copy(d, p).wait_send()
        for d in range(1, RING):
            gf_copy(d, p).wait_send()

    for d in range(1, RING):
        weight_copy(d).wait_send()
    def hand_on(d, of_col):
        slot = gw_out.at[of_col, lax.rem(row + 8 - d, 8)]
        return gw_copy(4, d, slot, slot, mate)

    gives.append(hand_on(0, col))
    gives[-1].start()
    for d in range(1, 8):
        slot = gw_out.at[col, lax.rem(row + 8 - d, 8)]
        gw_copy(3, d, slot, slot, peers[d - 1]).wait_recv()
        gives.append(hand_on(d, col))
        gives[-1].start()
    for d in range(8):
        hand_on(d, 1 - col).wait_recv()
    for give in gives:
        give.wait_send()


def flow(part, weight, features):
    _, width, cut = part.shape
    nodes = features.shape[0]
    chunks = nodes // cut
    pairs = chunks // 2
    piece = (width, cut)
    block = (width, 2 * cut)
    sixteen = jnp.bfloat16
    rows = width // 8
    return pl.pallas_call(
        flow_kernel,
        out_shape=(
            jax.ShapeDtypeStruct((nodes, width), sixteen),
            jax.ShapeDtypeStruct((2, 8, RING, rows, width), sixteen),
        ),
        in_specs=[VMEM, HBM, HBM],
        out_specs=(VMEM, VMEM),
        scratch_shapes=[
            pltpu.VMEM((2, chunks, *piece), sixteen),
            pltpu.VMEM((2, chunks, 2, *piece), sixteen),
            pltpu.VMEM((2, chunks, *piece), sixteen),
            pltpu.VMEM((chunks, 2, *piece), sixteen),
            pltpu.VMEM((3, chunks, *piece), sixteen),
            pltpu.VMEM((RING, LATE, *piece), sixteen),
            pltpu.VMEM((RING, LATE // 2, 2, *piece), sixteen),
            pltpu.VMEM((2, chunks, *piece), sixteen),
            pltpu.VMEM((2 * RING, width, width), sixteen),
            pltpu.VMEM((RING - 1, width, 2 * width), sixteen),
            pltpu.VMEM((RING, width, 2 * width), sixteen),
            pltpu.VMEM((RING, nodes, width), sixteen),
            pltpu.VMEM((pairs, *block), jnp.float32),
            pltpu.VMEM((RING - 1, pairs, *block), sixteen),
            pltpu.VMEM((RING - 1, pairs, *block), sixteen),
            pltpu.VMEM((2 * width, RING * width), jnp.float32),
            pltpu.VMEM((width, RING * width), sixteen),
            pltpu.VMEM((width, RING * width), sixteen),
            pltpu.VMEM((width, RING * width), sixteen),
            pltpu.VMEM((8, rows, RING * width), sixteen),
            pltpu.VMEM((RING, rows, width), sixteen),
            pltpu.SemaphoreType.DMA((1 + 2 * RING,)),
            pltpu.SemaphoreType.DMA((9, chunks)),
            pltpu.SemaphoreType.DMA((9, chunks)),
            pltpu.SemaphoreType.DMA((2, 3, RING, pairs)),
            pltpu.SemaphoreType.DMA((2, RING)),
            pltpu.SemaphoreType.DMA((5, 2, 8)),
        ],
        compiler_params=pltpu.CompilerParams(
            collective_id=1, has_side_effects=True, vmem_limit_bytes=24 << 20
        ),
        cost_estimate=pl.CostEstimate(
            flops=32 * nodes * width * width, bytes_accessed=16 << 20, transcendentals=0
        ),
        name="flow",
    )(part, weight, features)


def finish_kernel(gf_ref, gw_ref, gf_hbm, gw_hbm, gw_turned, sems):
    width = gw_turned.shape[0]
    write_gf = pltpu.make_async_copy(gf_ref, gf_hbm, sems.at[0])
    write_gf.start()
    for side in range(2):
        for x in range(RING):
            target = side * RING + x
            block = gw_ref[side, :, x].reshape(width, width).astype(jnp.float32)
            gw_turned[:, target * width : (target + 1) * width] = block.T
    write_gw = pltpu.make_async_copy(gw_turned, gw_hbm, sems.at[1])
    write_gw.start()
    write_gf.wait()
    write_gw.wait()


def finish(gf, gw):
    width = gf.shape[1]
    turned = (width, 2 * RING * width)
    return pl.pallas_call(
        finish_kernel,
        out_shape=(
            jax.ShapeDtypeStruct(gf.shape, gf.dtype),
            jax.ShapeDtypeStruct(turned, jnp.float32),
        ),
        in_specs=[VMEM, VMEM],
        out_specs=(HBM, HBM),
        scratch_shapes=[pltpu.VMEM(turned, jnp.float32), pltpu.SemaphoreType.DMA((2,))],
        compiler_params=pltpu.CompilerParams(vmem_limit_bytes=4 << 20),
        cost_estimate=pl.CostEstimate(flops=0, bytes_accessed=1 << 20, transcendentals=0),
        name="finish",
    )(gf, gw)


def on_device(features, pre_activation, out_grad, weight, tiles, rows, cols, counts):
    features, pre_activation, out_grad, weight, tiles, rows, cols = (
        pltpu.with_memory_space_constraint(a, pltpu.HBM)
        for a in (features, pre_activation, out_grad, weight, tiles[0, 0], rows, cols)
    )
    out_tiles = 8 * (features.shape[0] // tiles.shape[1])
    grad, early, sums, rows, cols = local_grads(
        pre_activation, out_grad, tiles, rows, cols, out_tiles
    )
    part = tile_products(rows, cols, counts, grad, early, sums, tiles, out_tiles)
    return finish(*flow(part, weight, features))


def solution(mesh):
    in_specs = (
        P(("row", "col"), "fib"),
        P(("row", "col"), "fib"),
        P(("row", "col"), "fib"),
        P("fib", None),
        P("row", "col", None, None, None),
        P("row", "col", None),
        P("row", "col", None),
        P("row", "col"),
    )
    out_specs = (P(("row", "col"), "fib"), P("fib", None))
    return jax.shard_map(
        on_device, mesh=mesh, in_specs=in_specs, out_specs=out_specs, check_vma=False
    )
```

```python
import functools

import jax
import jax.numpy as jnp
from jax import lax
from jax.experimental import pallas as pl
from jax.experimental.pallas import tpu as pltpu
from jax.sharding import PartitionSpec as P

GROUP = 16
EARLY = 48
RING = 4
LAGS = (0, 2, 5, 8, 4)
MESH = pl.DeviceIdType.MESH
VMEM = pl.BlockSpec(memory_space=pltpu.VMEM)
HBM = pl.BlockSpec(memory_space=pltpu.HBM)
SMEM = pl.BlockSpec(memory_space=pltpu.SMEM)
CHUNK = 128
LATE = 4


def greet(peers):
    barrier = pltpu.get_barrier_semaphore()
    for peer in peers:
        pl.semaphore_signal(barrier, inc=1, device_id=peer, device_id_type=MESH)
    pl.semaphore_wait(barrier, len(peers))


def position():
    return lax.axis_index("row"), lax.axis_index("col"), lax.axis_index("fib")


def grad_kernel(
    pre_hbm, out_grad_hbm, tiles_hbm, rows_hbm, cols_hbm,
    grad_ref, early_ref, sums_ref, rows_ref, cols_ref,
    pre_ref, out_grad_ref, load_sems, tile_sems, index_sems, send_sems, recv_sems,
):
    row, col, fib = position()
    own_tiles = grad_ref.shape[0] // 2
    tile = grad_ref.shape[2]
    partner = (row, 1 - col, fib)

    def loads(t):
        part = pl.ds(pl.multiple_of(t * tile, tile), tile)
        return (
            pltpu.make_async_copy(pre_hbm.at[part], pre_ref.at[part], load_sems.at[0, t]),
            pltpu.make_async_copy(out_grad_hbm.at[part], out_grad_ref.at[part], load_sems.at[1, t]),
        )

    @pl.loop(0, own_tiles)
    def _(t):
        for load in loads(t):
            load.start()

    def early(g):
        group = pl.ds(g * GROUP, GROUP)
        return pltpu.make_async_copy(tiles_hbm.at[group], early_ref.at[group], tile_sems.at[g])

    @pl.loop(0, EARLY // GROUP)
    def _(g):
        early(g).start()

    indices = [
        pltpu.make_async_copy(source, target, index_sems.at[i])
        for i, (source, target) in enumerate(((rows_hbm, rows_ref), (cols_hbm, cols_ref)))
    ]
    for load in indices:
        load.start()
    greet([partner])

    def copy(t, owner):
        slot = grad_ref.at[owner * own_tiles + t]
        return pltpu.make_async_remote_copy(
            slot, slot, send_sems.at[t], recv_sems.at[t], device_id=partner, device_id_type=MESH
        )

    @pl.loop(0, own_tiles)
    def _(t):
        for load in loads(t):
            load.wait()
        part = pl.ds(pl.multiple_of(t * tile, tile), tile)
        pre = pre_ref[part, :].astype(jnp.float32)
        sigmoid = jax.nn.sigmoid(pre)
        grad = out_grad_ref[part, :].astype(jnp.float32) * sigmoid * (1.0 + pre * (1.0 - sigmoid))
        grad_ref[col * own_tiles + t] = grad.T.astype(grad_ref.dtype)
        copy(t, col).start()

    @pl.loop(0, sums_ref.shape[0], unroll=5)
    def _(t):
        sums_ref[t] = jnp.zeros(sums_ref.shape[1:], sums_ref.dtype)

    @pl.loop(0, own_tiles)
    def _(t):
        copy(t, col).wait_send()
        copy(t, 1 - col).wait_recv()

    @pl.loop(0, EARLY // GROUP)
    def _(g):
        early(g).wait()

    for load in indices:
        load.wait()


def local_grads(pre, out_grad, tiles, rows, cols, out_tiles):
    nodes, width = pre.shape
    tile = tiles.shape[1]
    own_tiles = nodes // tile
    return pl.pallas_call(
        grad_kernel,
        out_shape=(
            jax.ShapeDtypeStruct((2 * own_tiles, width, tile), jnp.bfloat16),
            jax.ShapeDtypeStruct((EARLY, tile, tile), tiles.dtype),
            jax.ShapeDtypeStruct((out_tiles + 1, width, tile), jnp.float32),
            jax.ShapeDtypeStruct(rows.shape, rows.dtype),
            jax.ShapeDtypeStruct(cols.shape, cols.dtype),
        ),
        in_specs=[HBM] * 5,
        out_specs=(VMEM,) * 5,
        scratch_shapes=[
            pltpu.VMEM(pre.shape, pre.dtype),
            pltpu.VMEM(pre.shape, pre.dtype),
            pltpu.SemaphoreType.DMA((2, own_tiles)),
            pltpu.SemaphoreType.DMA((EARLY // GROUP,)),
            pltpu.SemaphoreType.DMA((2,)),
            pltpu.SemaphoreType.DMA((own_tiles,)),
            pltpu.SemaphoreType.DMA((own_tiles,)),
        ],
        compiler_params=pltpu.CompilerParams(
            collective_id=0, has_side_effects=True, vmem_limit_bytes=16 << 20
        ),
        cost_estimate=pl.CostEstimate(
            flops=10 * nodes * width, bytes_accessed=8 * nodes * width, transcendentals=nodes * width
        ),
        name="local_grads",
    )(pre, out_grad, tiles, rows, cols)


def tile_kernel(
    rows_ref, cols_ref, count_ref, grad_ref, early_ref, sums_ref, tiles_ref, out_ref, total,
    held, sems,
):
    slots, tile, _ = tiles_ref.shape
    cuts = tile // CHUNK
    out_tiles = out_ref.shape[0] // cuts
    row_tiles = grad_ref.shape[0]
    def copy(g):
        source = tiles_ref.at[pl.ds(g * GROUP, GROUP)]
        return pltpu.make_async_copy(
            source, held.at[pl.ds(g * GROUP - EARLY, GROUP)], sems.at[g - EARLY // GROUP]
        )

    count = jnp.clip(count_ref[0, 0], 1, slots)
    used = (count + GROUP - 1) // GROUP

    @pl.loop(EARLY // GROUP, used)
    def _(g):
        copy(g).start()

    def add_group(g, tile_at):
        for j in range(GROUP):
            slot = g * GROUP + j
            row = jnp.clip(rows_ref[0, 0, slot], 0, row_tiles - 1)
            col = jnp.clip(cols_ref[0, 0, slot], 0, out_tiles - 1)
            target = jnp.where(slot < count, col, out_tiles)
            total[target] += jnp.dot(grad_ref[row], tile_at(slot), preferred_element_type=jnp.float32)

    @pl.loop(0, jnp.minimum(used, EARLY // GROUP))
    def _(g):
        add_group(g, lambda slot: early_ref[slot])

    @pl.loop(EARLY // GROUP, used)
    def _(g):
        copy(g).wait()
        add_group(g, lambda slot: held[slot - EARLY])

    @pl.loop(0, out_tiles, unroll=4)
    def _(t):
        for cut in range(cuts):
            out_ref[t * cuts + cut] = total[t, :, cut * CHUNK : (cut + 1) * CHUNK].astype(out_ref.dtype)


def tile_products(rows, cols, count, grad, early, sums, tiles, out_tiles):
    slots, tile, _ = tiles.shape
    width = grad.shape[1]
    return pl.pallas_call(
        tile_kernel,
        out_shape=(
            jax.ShapeDtypeStruct((out_tiles * tile // CHUNK, width, CHUNK), jnp.bfloat16),
            jax.ShapeDtypeStruct(sums.shape, sums.dtype),
        ),
        input_output_aliases={5: 1},
        in_specs=[SMEM, SMEM, SMEM, VMEM, VMEM, VMEM, HBM],
        out_specs=(VMEM, VMEM),
        scratch_shapes=[
            pltpu.VMEM((slots - EARLY, tile, tile), jnp.bfloat16),
            pltpu.SemaphoreType.DMA(((slots - EARLY) // GROUP,)),
        ],
        compiler_params=pltpu.CompilerParams(vmem_limit_bytes=28 << 20),
        cost_estimate=pl.CostEstimate(
            flops=2 * slots * width * tile * tile,
            bytes_accessed=2 * slots * tile * tile,
            transcendentals=0,
        ),
        name="tile_products",
    )(rows, cols, count, grad, early, sums, tiles)[0]


def flow_kernel(
    part_all, weight_hbm, feat_hbm, gf_ref, gw_out,
    first, second, merged, half, y_in, late_in, late, whole, weight_raw, weight_send, weight_in, feat,
    gf_own, gf_send, gf_in, gw_ref, gw_send, mate_in, row_send, row_in, x_send,
    load_sems, send_sems, recv_sems, x_sems, late_sems, gw_sems,
):
    row, col, fib = position()
    l, z = row // RING, lax.rem(row, RING)
    h, x = fib // RING, lax.rem(fib, RING)
    chunks, width, nodes_t = whole.shape[1:]
    pairs, span_t = chunks // 2, 2 * nodes_t
    split = chunks - LATE
    units = split + LATE // 2
    z_up, z_down, z_far = (lax.rem(z + d, RING) for d in (1, RING - 1, 2))
    to_z_up, to_z_down = (l * RING + z_up, col, fib), (l * RING + z_down, col, fib)
    to_x = [(row, col, h * RING + lax.rem(x + d, RING)) for d in range(RING)]
    to_pair = ((1 - l) * RING + z, col, fib)
    to_cross = ((1 - l) * RING + z, col, (1 - h) * RING + x)
    to_far = (row, col, (1 - h) * RING + x)
    mate = (row, 1 - col, fib)
    peers = [(lax.rem(row + d, 8), col, fib) for d in range(1, 8)]

    def nodes_of(p):
        return pl.ds(pl.multiple_of(p * span_t, span_t), span_t)

    load_weight = [
        pltpu.make_async_copy(
            weight_hbm.at[:, k * width : (k + 1) * width], weight_raw.at[k], load_sems.at[1 + k]
        )
        for k in range(2 * RING)
    ]
    load_feat = pltpu.make_async_copy(feat_hbm, feat.at[0], load_sems.at[0])
    for load in load_weight:
        load.start()
    load_feat.start()
    greet([*to_x[1:], to_cross, to_far, mate, *peers])

    def part_at(to_l, to_z, t):
        return part_all.at[(to_l * RING + to_z) * chunks + t]

    def copy(kind, t, source, target, peer):
        return pltpu.make_async_remote_copy(
            source, target, send_sems.at[kind, t], recv_sems.at[kind, t], device_id=peer, device_id_type=MESH
        )

    def late_copy(to_z):
        source = part_all.at[pl.ds(((1 - l) * RING + to_z) * chunks + split, LATE)]
        return pltpu.make_async_remote_copy(
            source, late_in.at[to_z], late_sems.at[0, to_z], late_sems.at[1, to_z], device_id=to_pair, device_id_type=MESH
        )

    def early_share(i, to_z, t):
        return part_at(i, to_z, t)

    def late_share(i, to_z, t):
        return late.at[to_z, t - split, i]

    def link(kind, t, share=early_share):
        if kind == 0:
            return copy(0, t, share(0, z_far, t), first.at[0, t], to_z_up)
        if kind == 1:
            return copy(1, t, share(1, z_far, t), first.at[1, t], to_z_down)
        if kind == 2:
            return copy(2, t, share(1, z_up, t), second.at[0, t, 1], to_z_up)
        if kind == 3:
            return copy(3, t, share(0, z_down, t), second.at[1, t, 0], to_z_down)
        if kind == 4:
            return copy(4, t, merged.at[0, t], second.at[0, t, 0], to_z_up)
        if kind == 5:
            return copy(5, t, merged.at[1, t], second.at[1, t, 1], to_z_down)
        if kind == 6:
            return copy(6, t, half.at[t, 1 - l], y_in.at[0, t], to_pair)
        if kind == 7:
            return copy(7, t, half.at[t, 1 - l], y_in.at[1, t], to_cross)
        if share is late_share:
            both = whole.at[h, pl.ds(2 * t - split, 2)]
            return copy(8, t, both, both, to_far)
        return copy(8, t, half.at[t, l], y_in.at[2, t], to_far)

    def along_x(kind, d, p, source, target, peer=None):
        return pltpu.make_async_remote_copy(
            source,
            target,
            x_sems.at[0, kind, d, p],
            x_sems.at[1, kind, d, p],
            device_id=to_x[d] if peer is None else peer,
            device_id_type=MESH,
        )

    def feat_pass(up, p):
        part = pl.ds(pl.multiple_of(p * span_t + (0 if up else nodes_t), nodes_t), nodes_t)
        source = feat.at[RING - 1 if up else 1, part]
        return along_x(0, 2 if up else 0, p, source, feat.at[2, part], to_x[1 if up else RING - 1])

    def feat_copy(d, p):
        return along_x(0, d, p, feat.at[0, nodes_of(p)], feat.at[RING - d, nodes_of(p)])

    def gf_copy(d, p):
        return along_x(1, d, p, gf_send.at[d - 1, p], gf_in.at[d - 1, p])

    def weight_copy(d):
        return along_x(2, d, 0, weight_send.at[d - 1], weight_in.at[RING - d])

    def added(*refs):
        terms = [r[...].astype(jnp.float32) for r in refs]
        return functools.reduce(lambda a, b: a + b, terms)

    def send_shares(t):
        @pl.when(t < split)
        def _():
            for kind in range(4):
                link(kind, t).start()

        @pl.when(t == split)
        def _():
            for to_z in range(RING):
                late_copy(to_z).wait_recv()

        @pl.when(t >= split)
        def _():
            for to_z in (z_far, z_up, z_down, z):
                for i in range(2):
                    n = 2 * (t - split) + i
                    late[to_z, t - split, i] = added(
                        part_at(l, to_z, split + n), late_in.at[to_z, n]
                    ).astype(late.dtype)
            for kind in range(4):
                link(kind, t, late_share).start()

        @pl.when(t == 0)
        def _():
            for to_z in range(RING):
                late_copy(to_z).start()
            for load in load_weight:
                load.wait()
            for d in range(RING):
                at = lax.rem(x + d, RING)
                block = jnp.concatenate([weight_raw[at], weight_raw[RING + at]], axis=1)
                if d == 0:
                    weight_in[0] = block
                else:
                    weight_send[d - 1] = block
                    weight_copy(d).start()
            gw_ref[...] = jnp.zeros_like(gw_ref)
            load_feat.wait()

        @pl.when(t < pairs)
        def _():
            for d in (1, RING - 1):
                feat_copy(d, t).start()

    def pass_on(t):
        @pl.when(t < pairs)
        def _():
            feat_copy(1, t).wait_recv()
            feat_pass(True, t).start()
            feat_copy(RING - 1, t).wait_recv()
            feat_pass(False, t).start()

    def merge(t):
        def run(share):
            link(0, t, share).wait_recv()
            merged[0, t] = added(share(0, z_up, t), first.at[0, t]).astype(merged.dtype)
            link(4, t, share).start()
            link(1, t, share).wait_recv()
            merged[1, t] = added(share(1, z_down, t), first.at[1, t]).astype(merged.dtype)
            link(5, t, share).start()

        pl.when(t < split)(lambda: run(early_share))
        pl.when(t >= split)(lambda: run(late_share))

    def sum_over_z(t):
        for kind in (2, 3, 4, 5):
            link(kind, t).wait_recv()

        @pl.when(t < split)
        def _():
            for i in range(2):
                half[t, i] = added(part_at(i, z, t), second.at[0, t, i], second.at[1, t, i]).astype(
                    half.dtype
                )
            for kind in (6, 7, 8):
                link(kind, t).start()

        @pl.when(t >= split)
        def _():
            for i in range(2):
                whole[h, 2 * t - split + i] = added(
                    late.at[z, t - split, i], second.at[0, t, i], second.at[1, t, i]
                ).astype(whole.dtype)
            link(8, t, late_share).start()

    def sum_over_y(t):
        @pl.when(t < split)
        def _():
            for kind in (6, 7, 8):
                link(kind, t).wait_recv()
            whole[h, t] = added(half.at[t, l], y_in.at[0, t]).astype(whole.dtype)
            whole[1 - h, t] = added(y_in.at[1, t], y_in.at[2, t]).astype(whole.dtype)
            for kind in range(9):
                link(kind, t).wait_send()

        @pl.when(t >= split)
        def _():
            link(8, t, late_share).wait_recv()

        @pl.when((lax.rem(t, 2) == 1) | (t >= split))
        def _():
            p = jnp.where(t < split, lax.div(t, 2), t - split // 2)
            multiply_features(p)

            @pl.when(p < pairs - 1)
            def _():
                multiply_weight(p)

    def panel_of(p):
        return jnp.concatenate(
            [whole[:, 2 * p + i].reshape(2 * width, nodes_t) for i in range(2)], axis=1
        )

    def multiply_features(p):
        for up in (True, False):
            feat_pass(up, p).wait_recv()
        beside = jnp.concatenate([feat[d, nodes_of(p), :] for d in range(RING)], axis=1)
        gw_ref[...] += jnp.dot(panel_of(p), beside, preferred_element_type=jnp.float32)

    def multiply_weight(p):
        @pl.when(p == 0)
        def _():
            for d in range(1, RING):
                weight_copy(d).wait_recv()

        panel = panel_of(p)
        for d in (2, 1, 3, 0):
            block = jnp.dot(weight_in[d], panel, preferred_element_type=jnp.float32)
            if d == 0:
                gf_own[p] = block
            else:
                gf_send[d - 1, p] = block.astype(gf_send.dtype)
                gf_copy(d, p).start()

    def collect(p):
        for d in range(1, RING):
            gf_copy(d, p).wait_recv()
        block = gf_own[p] + added(*[gf_in.at[d - 1, p] for d in range(1, RING)])
        gf_ref[nodes_of(p), :] = block.T.astype(gf_ref.dtype)

    stages = (send_shares, merge, sum_over_z, sum_over_y, pass_on)

    @pl.loop(0, units + max(LAGS))
    def _(step):
        for late, stage in zip(LAGS, stages):
            t = step - late

            @pl.when((t >= 0) & (t < units))
            def _(stage=stage, t=t):
                stage(t)

    rows = width // 8

    def gw_copy(phase, d, source, target, peer):
        return pltpu.make_async_remote_copy(
            source, target, gw_sems.at[phase, 0, d], gw_sems.at[phase, 1, d], device_id=peer, device_id_type=MESH
        )

    def piece(ref, of, size=rows):
        return ref.at[pl.ds(pl.multiple_of(of * size, size), size)]

    gw_send[...] = gw_ref[pl.ds(pl.multiple_of((1 - col) * width, width), width), :].astype(gw_send.dtype)
    gives = [gw_copy(0, 0, gw_send, mate_in, mate)]
    gives[0].start()
    multiply_weight(pairs - 1)
    gives[0].wait_recv()
    mine = gw_ref[pl.ds(pl.multiple_of(col * width, width), width), :] + mate_in[...].astype(jnp.float32)
    gw_ref[0:width, :] = mine
    row_send[...] = mine.astype(row_send.dtype)
    for d in range(1, 8):
        gives.append(gw_copy(1, d, piece(row_send, lax.rem(row + d, 8)), row_in.at[d], peers[d - 1]))
        gives[-1].start()

    @pl.loop(0, pairs // 2)
    def _(p):
        collect(p)

    for to_z in range(RING):
        late_copy(to_z).wait_send()

    @pl.loop(split, units)
    def _(t):
        for kind in (0, 1, 2, 3, 4, 5, 8):
            link(kind, t, late_share).wait_send()

    own = gw_ref[pl.ds(pl.multiple_of(row * rows, rows), rows), :]
    for d in range(1, 8):
        gives[d].wait_recv()
        own += row_in[d].astype(jnp.float32)
    for d in range(RING):
        block = own[:, d * width : (d + 1) * width].astype(gw_out.dtype)
        if d == 0:
            gw_out[col, row, x] = block
        else:
            x_send[d] = block
            gives.append(gw_copy(2, d, x_send.at[d], gw_out.at[col, row, x], to_x[d]))
            gives[-1].start()

    for d in range(1, RING):
        slot = gw_out.at[col, row, lax.rem(x + RING - d, RING)]
        gw_copy(2, d, slot, slot, to_x[d]).wait_recv()
    for d in range(1, 8):
        gives.append(gw_copy(3, d, gw_out.at[col, row], gw_out.at[col, row], peers[d - 1]))
        gives[-1].start()

    @pl.loop(pairs // 2, pairs)
    def _(p):
        collect(p)

    @pl.loop(0, pairs)
    def _(p):
        for up in (True, False):
            feat_pass(up, p).wait_send()
        for d in (1, RING - 1):
            feat_copy(d, p).wait_send()
        for d in range(1, RING):
            gf_copy(d, p).wait_send()

    for d in range(1, RING):
        weight_copy(d).wait_send()
    def hand_on(d, of_col):
        slot = gw_out.at[of_col, lax.rem(row + 8 - d, 8)]
        return gw_copy(4, d, slot, slot, mate)

    gives.append(hand_on(0, col))
    gives[-1].start()
    for d in range(1, 8):
        slot = gw_out.at[col, lax.rem(row + 8 - d, 8)]
        gw_copy(3, d, slot, slot, peers[d - 1]).wait_recv()
        gives.append(hand_on(d, col))
        gives[-1].start()
    for d in range(8):
        hand_on(d, 1 - col).wait_recv()
    for give in gives:
        give.wait_send()


def flow(part, weight, features):
    _, width, cut = part.shape
    nodes = features.shape[0]
    chunks = nodes // cut
    pairs = chunks // 2
    piece = (width, cut)
    block = (width, 2 * cut)
    sixteen = jnp.bfloat16
    rows = width // 8
    return pl.pallas_call(
        flow_kernel,
        out_shape=(
            jax.ShapeDtypeStruct((nodes, width), sixteen),
            jax.ShapeDtypeStruct((2, 8, RING, rows, width), sixteen),
        ),
        in_specs=[VMEM, HBM, HBM],
        out_specs=(VMEM, VMEM),
        scratch_shapes=[
            pltpu.VMEM((2, chunks, *piece), sixteen),
            pltpu.VMEM((2, chunks, 2, *piece), sixteen),
            pltpu.VMEM((2, chunks, *piece), sixteen),
            pltpu.VMEM((chunks, 2, *piece), sixteen),
            pltpu.VMEM((3, chunks, *piece), sixteen),
            pltpu.VMEM((RING, LATE, *piece), sixteen),
            pltpu.VMEM((RING, LATE // 2, 2, *piece), sixteen),
            pltpu.VMEM((2, chunks, *piece), sixteen),
            pltpu.VMEM((2 * RING, width, width), sixteen),
            pltpu.VMEM((RING - 1, width, 2 * width), sixteen),
            pltpu.VMEM((RING, width, 2 * width), sixteen),
            pltpu.VMEM((RING, nodes, width), sixteen),
            pltpu.VMEM((pairs, *block), jnp.float32),
            pltpu.VMEM((RING - 1, pairs, *block), sixteen),
            pltpu.VMEM((RING - 1, pairs, *block), sixteen),
            pltpu.VMEM((2 * width, RING * width), jnp.float32),
            pltpu.VMEM((width, RING * width), sixteen),
            pltpu.VMEM((width, RING * width), sixteen),
            pltpu.VMEM((width, RING * width), sixteen),
            pltpu.VMEM((8, rows, RING * width), sixteen),
            pltpu.VMEM((RING, rows, width), sixteen),
            pltpu.SemaphoreType.DMA((1 + 2 * RING,)),
            pltpu.SemaphoreType.DMA((9, chunks)),
            pltpu.SemaphoreType.DMA((9, chunks)),
            pltpu.SemaphoreType.DMA((2, 3, RING, pairs)),
            pltpu.SemaphoreType.DMA((2, RING)),
            pltpu.SemaphoreType.DMA((5, 2, 8)),
        ],
        compiler_params=pltpu.CompilerParams(
            collective_id=1, has_side_effects=True, vmem_limit_bytes=24 << 20
        ),
        cost_estimate=pl.CostEstimate(
            flops=32 * nodes * width * width, bytes_accessed=16 << 20, transcendentals=0
        ),
        name="flow",
    )(part, weight, features)


def finish_kernel(gf_ref, gw_ref, gf_hbm, gw_hbm, gw_turned, sems):
    width = gw_turned.shape[0]
    write_gf = pltpu.make_async_copy(gf_ref, gf_hbm, sems.at[0])
    write_gf.start()
    for side in range(2):
        for x in range(RING):
            target = side * RING + x
            block = gw_ref[side, :, x].reshape(width, width).astype(jnp.float32)
            gw_turned[:, target * width : (target + 1) * width] = block.T
    write_gw = pltpu.make_async_copy(gw_turned, gw_hbm, sems.at[1])
    write_gw.start()
    write_gf.wait()
    write_gw.wait()


def finish(gf, gw):
    width = gf.shape[1]
    turned = (width, 2 * RING * width)
    return pl.pallas_call(
        finish_kernel,
        out_shape=(
            jax.ShapeDtypeStruct(gf.shape, gf.dtype),
            jax.ShapeDtypeStruct(turned, jnp.float32),
        ),
        in_specs=[VMEM, VMEM],
        out_specs=(HBM, HBM),
        scratch_shapes=[pltpu.VMEM(turned, jnp.float32), pltpu.SemaphoreType.DMA((2,))],
        compiler_params=pltpu.CompilerParams(vmem_limit_bytes=4 << 20),
        cost_estimate=pl.CostEstimate(flops=0, bytes_accessed=1 << 20, transcendentals=0),
        name="finish",
    )(gf, gw)


def on_device(features, pre_activation, out_grad, weight, tiles, rows, cols, counts):
    features, pre_activation, out_grad, weight, tiles, rows, cols = (
        pltpu.with_memory_space_constraint(a, pltpu.HBM)
        for a in (features, pre_activation, out_grad, weight, tiles[0, 0], rows, cols)
    )
    out_tiles = 8 * (features.shape[0] // tiles.shape[1])
    grad, early, sums, rows, cols = local_grads(
        pre_activation, out_grad, tiles, rows, cols, out_tiles
    )
    part = tile_products(rows, cols, counts, grad, early, sums, tiles, out_tiles)
    return finish(*flow(part, weight, features))


def solution(mesh):
    in_specs = (
        P(("row", "col"), "fib"),
        P(("row", "col"), "fib"),
        P(("row", "col"), "fib"),
        P("fib", None),
        P("row", "col", None, None, None),
        P("row", "col", None),
        P("row", "col", None),
        P("row", "col"),
    )
    out_specs = (P(("row", "col"), "fib"), P("fib", None))
    return jax.shard_map(
        on_device, mesh=mesh, in_specs=in_specs, out_specs=out_specs, check_vma=False
    )
```

```python
import functools

import jax
import jax.numpy as jnp
from jax import lax
from jax.experimental import pallas as pl
from jax.experimental.pallas import tpu as pltpu
from jax.sharding import PartitionSpec as P

GROUP = 16
EARLY = 32
RING = 4
LAGS = (0, 2, 5, 8, 4)
MESH = pl.DeviceIdType.MESH
VMEM = pl.BlockSpec(memory_space=pltpu.VMEM)
HBM = pl.BlockSpec(memory_space=pltpu.HBM)
SMEM = pl.BlockSpec(memory_space=pltpu.SMEM)
CHUNK = 128
LATE = 4


def greet(peers):
    barrier = pltpu.get_barrier_semaphore()
    for peer in peers:
        pl.semaphore_signal(barrier, inc=1, device_id=peer, device_id_type=MESH)
    pl.semaphore_wait(barrier, len(peers))


def position():
    return lax.axis_index("row"), lax.axis_index("col"), lax.axis_index("fib")


def grad_kernel(
    pre_hbm, out_grad_hbm, tiles_hbm, rows_hbm, cols_hbm,
    grad_ref, early_ref, sums_ref, rows_ref, cols_ref,
    pre_ref, out_grad_ref, load_sems, tile_sems, index_sems, send_sems, recv_sems,
):
    row, col, fib = position()
    own_tiles = grad_ref.shape[0] // 2
    tile = grad_ref.shape[2]
    partner = (row, 1 - col, fib)

    def loads(t):
        part = pl.ds(pl.multiple_of(t * tile, tile), tile)
        return (
            pltpu.make_async_copy(pre_hbm.at[part], pre_ref.at[part], load_sems.at[0, t]),
            pltpu.make_async_copy(out_grad_hbm.at[part], out_grad_ref.at[part], load_sems.at[1, t]),
        )

    @pl.loop(0, own_tiles)
    def _(t):
        for load in loads(t):
            load.start()

    def early(g):
        group = pl.ds(g * GROUP, GROUP)
        return pltpu.make_async_copy(tiles_hbm.at[group], early_ref.at[group], tile_sems.at[g])

    @pl.loop(0, EARLY // GROUP)
    def _(g):
        early(g).start()

    indices = [
        pltpu.make_async_copy(source, target, index_sems.at[i])
        for i, (source, target) in enumerate(((rows_hbm, rows_ref), (cols_hbm, cols_ref)))
    ]
    for load in indices:
        load.start()
    greet([partner])

    def copy(t, owner):
        slot = grad_ref.at[owner * own_tiles + t]
        return pltpu.make_async_remote_copy(
            slot, slot, send_sems.at[t], recv_sems.at[t], device_id=partner, device_id_type=MESH
        )

    @pl.loop(0, own_tiles)
    def _(t):
        for load in loads(t):
            load.wait()
        part = pl.ds(pl.multiple_of(t * tile, tile), tile)
        pre = pre_ref[part, :].astype(jnp.float32)
        sigmoid = jax.nn.sigmoid(pre)
        grad = out_grad_ref[part, :].astype(jnp.float32) * sigmoid * (1.0 + pre * (1.0 - sigmoid))
        grad_ref[col * own_tiles + t] = grad.T.astype(grad_ref.dtype)
        copy(t, col).start()

    @pl.loop(0, sums_ref.shape[0], unroll=5)
    def _(t):
        sums_ref[t] = jnp.zeros(sums_ref.shape[1:], sums_ref.dtype)

    @pl.loop(0, own_tiles)
    def _(t):
        copy(t, col).wait_send()
        copy(t, 1 - col).wait_recv()

    @pl.loop(0, EARLY // GROUP)
    def _(g):
        early(g).wait()

    for load in indices:
        load.wait()


def local_grads(pre, out_grad, tiles, rows, cols, out_tiles):
    nodes, width = pre.shape
    tile = tiles.shape[1]
    own_tiles = nodes // tile
    return pl.pallas_call(
        grad_kernel,
        out_shape=(
            jax.ShapeDtypeStruct((2 * own_tiles, width, tile), jnp.bfloat16),
            jax.ShapeDtypeStruct((EARLY, tile, tile), tiles.dtype),
            jax.ShapeDtypeStruct((out_tiles + 1, width, tile), jnp.float32),
            jax.ShapeDtypeStruct(rows.shape, rows.dtype),
            jax.ShapeDtypeStruct(cols.shape, cols.dtype),
        ),
        in_specs=[HBM] * 5,
        out_specs=(VMEM,) * 5,
        scratch_shapes=[
            pltpu.VMEM(pre.shape, pre.dtype),
            pltpu.VMEM(pre.shape, pre.dtype),
            pltpu.SemaphoreType.DMA((2, own_tiles)),
            pltpu.SemaphoreType.DMA((EARLY // GROUP,)),
            pltpu.SemaphoreType.DMA((2,)),
            pltpu.SemaphoreType.DMA((own_tiles,)),
            pltpu.SemaphoreType.DMA((own_tiles,)),
        ],
        compiler_params=pltpu.CompilerParams(
            collective_id=0, has_side_effects=True, vmem_limit_bytes=16 << 20
        ),
        cost_estimate=pl.CostEstimate(
            flops=10 * nodes * width, bytes_accessed=8 * nodes * width, transcendentals=nodes * width
        ),
        name="local_grads",
    )(pre, out_grad, tiles, rows, cols)


def tile_kernel(
    rows_ref, cols_ref, count_ref, grad_ref, early_ref, sums_ref, tiles_ref, out_ref, total,
    held, sems,
):
    slots, tile, _ = tiles_ref.shape
    cuts = tile // CHUNK
    out_tiles = out_ref.shape[0] // cuts
    row_tiles = grad_ref.shape[0]
    def copy(g):
        source = tiles_ref.at[pl.ds(g * GROUP, GROUP)]
        return pltpu.make_async_copy(
            source, held.at[pl.ds(g * GROUP - EARLY, GROUP)], sems.at[g - EARLY // GROUP]
        )

    count = jnp.clip(count_ref[0, 0], 1, slots)
    used = (count + GROUP - 1) // GROUP

    @pl.loop(EARLY // GROUP, used)
    def _(g):
        copy(g).start()

    def add_group(g, tile_at):
        for j in range(GROUP):
            slot = g * GROUP + j
            row = jnp.clip(rows_ref[0, 0, slot], 0, row_tiles - 1)
            col = jnp.clip(cols_ref[0, 0, slot], 0, out_tiles - 1)
            target = jnp.where(slot < count, col, out_tiles)
            total[target] += jnp.dot(grad_ref[row], tile_at(slot), preferred_element_type=jnp.float32)

    @pl.loop(0, jnp.minimum(used, EARLY // GROUP))
    def _(g):
        add_group(g, lambda slot: early_ref[slot])

    @pl.loop(EARLY // GROUP, used)
    def _(g):
        copy(g).wait()
        add_group(g, lambda slot: held[slot - EARLY])

    @pl.loop(0, out_tiles, unroll=4)
    def _(t):
        for cut in range(cuts):
            out_ref[t * cuts + cut] = total[t, :, cut * CHUNK : (cut + 1) * CHUNK].astype(out_ref.dtype)


def tile_products(rows, cols, count, grad, early, sums, tiles, out_tiles):
    slots, tile, _ = tiles.shape
    width = grad.shape[1]
    return pl.pallas_call(
        tile_kernel,
        out_shape=(
            jax.ShapeDtypeStruct((out_tiles * tile // CHUNK, width, CHUNK), jnp.bfloat16),
            jax.ShapeDtypeStruct(sums.shape, sums.dtype),
        ),
        input_output_aliases={5: 1},
        in_specs=[SMEM, SMEM, SMEM, VMEM, VMEM, VMEM, HBM],
        out_specs=(VMEM, VMEM),
        scratch_shapes=[
            pltpu.VMEM((slots - EARLY, tile, tile), jnp.bfloat16),
            pltpu.SemaphoreType.DMA(((slots - EARLY) // GROUP,)),
        ],
        compiler_params=pltpu.CompilerParams(vmem_limit_bytes=28 << 20),
        cost_estimate=pl.CostEstimate(
            flops=2 * slots * width * tile * tile,
            bytes_accessed=2 * slots * tile * tile,
            transcendentals=0,
        ),
        name="tile_products",
    )(rows, cols, count, grad, early, sums, tiles)[0]


def flow_kernel(
    part_all, weight_hbm, feat_hbm, gf_ref, gw_out,
    first, second, merged, half, y_in, late_in, late, whole, weight_raw, weight_send, weight_in, feat,
    gf_own, gf_send, gf_in, gw_ref, gw_send, mate_in, row_send, row_in, x_send,
    load_sems, send_sems, recv_sems, x_sems, late_sems, gw_sems,
):
    row, col, fib = position()
    l, z = row // RING, lax.rem(row, RING)
    h, x = fib // RING, lax.rem(fib, RING)
    chunks, width, nodes_t = whole.shape[1:]
    pairs, span_t = chunks // 2, 2 * nodes_t
    split = chunks - LATE
    units = split + LATE // 2
    z_up, z_down, z_far = (lax.rem(z + d, RING) for d in (1, RING - 1, 2))
    to_z_up, to_z_down = (l * RING + z_up, col, fib), (l * RING + z_down, col, fib)
    to_x = [(row, col, h * RING + lax.rem(x + d, RING)) for d in range(RING)]
    to_pair = ((1 - l) * RING + z, col, fib)
    to_cross = ((1 - l) * RING + z, col, (1 - h) * RING + x)
    to_far = (row, col, (1 - h) * RING + x)
    mate = (row, 1 - col, fib)
    peers = [(lax.rem(row + d, 8), col, fib) for d in range(1, 8)]

    def nodes_of(p):
        return pl.ds(pl.multiple_of(p * span_t, span_t), span_t)

    load_weight = [
        pltpu.make_async_copy(
            weight_hbm.at[:, k * width : (k + 1) * width], weight_raw.at[k], load_sems.at[1 + k]
        )
        for k in range(2 * RING)
    ]
    load_feat = pltpu.make_async_copy(feat_hbm, feat.at[0], load_sems.at[0])
    for load in load_weight:
        load.start()
    load_feat.start()
    greet([*to_x[1:], to_cross, to_far, mate, *peers])

    def part_at(to_l, to_z, t):
        return part_all.at[(to_l * RING + to_z) * chunks + t]

    def copy(kind, t, source, target, peer):
        return pltpu.make_async_remote_copy(
            source, target, send_sems.at[kind, t], recv_sems.at[kind, t], device_id=peer, device_id_type=MESH
        )

    def late_copy(to_z):
        source = part_all.at[pl.ds(((1 - l) * RING + to_z) * chunks + split, LATE)]
        return pltpu.make_async_remote_copy(
            source, late_in.at[to_z], late_sems.at[0, to_z], late_sems.at[1, to_z], device_id=to_pair, device_id_type=MESH
        )

    def early_share(i, to_z, t):
        return part_at(i, to_z, t)

    def late_share(i, to_z, t):
        return late.at[to_z, t - split, i]

    def link(kind, t, share=early_share):
        if kind == 0:
            return copy(0, t, share(0, z_far, t), first.at[0, t], to_z_up)
        if kind == 1:
            return copy(1, t, share(1, z_far, t), first.at[1, t], to_z_down)
        if kind == 2:
            return copy(2, t, share(1, z_up, t), second.at[0, t, 1], to_z_up)
        if kind == 3:
            return copy(3, t, share(0, z_down, t), second.at[1, t, 0], to_z_down)
        if kind == 4:
            return copy(4, t, merged.at[0, t], second.at[0, t, 0], to_z_up)
        if kind == 5:
            return copy(5, t, merged.at[1, t], second.at[1, t, 1], to_z_down)
        if kind == 6:
            return copy(6, t, half.at[t, 1 - l], y_in.at[0, t], to_pair)
        if kind == 7:
            return copy(7, t, half.at[t, 1 - l], y_in.at[1, t], to_cross)
        if share is late_share:
            both = whole.at[h, pl.ds(2 * t - split, 2)]
            return copy(8, t, both, both, to_far)
        return copy(8, t, half.at[t, l], y_in.at[2, t], to_far)

    def along_x(kind, d, p, source, target, peer=None):
        return pltpu.make_async_remote_copy(
            source,
            target,
            x_sems.at[0, kind, d, p],
            x_sems.at[1, kind, d, p],
            device_id=to_x[d] if peer is None else peer,
            device_id_type=MESH,
        )

    def feat_pass(up, p):
        part = pl.ds(pl.multiple_of(p * span_t + (0 if up else nodes_t), nodes_t), nodes_t)
        source = feat.at[RING - 1 if up else 1, part]
        return along_x(0, 2 if up else 0, p, source, feat.at[2, part], to_x[1 if up else RING - 1])

    def feat_copy(d, p):
        return along_x(0, d, p, feat.at[0, nodes_of(p)], feat.at[RING - d, nodes_of(p)])

    def gf_copy(d, p):
        return along_x(1, d, p, gf_send.at[d - 1, p], gf_in.at[d - 1, p])

    def weight_copy(d):
        return along_x(2, d, 0, weight_send.at[d - 1], weight_in.at[RING - d])

    def added(*refs):
        terms = [r[...].astype(jnp.float32) for r in refs]
        return functools.reduce(lambda a, b: a + b, terms)

    def send_shares(t):
        @pl.when(t < split)
        def _():
            for kind in range(4):
                link(kind, t).start()

        @pl.when(t == split)
        def _():
            for to_z in range(RING):
                late_copy(to_z).wait_recv()

        @pl.when(t >= split)
        def _():
            for to_z in (z_far, z_up, z_down, z):
                for i in range(2):
                    n = 2 * (t - split) + i
                    late[to_z, t - split, i] = added(
                        part_at(l, to_z, split + n), late_in.at[to_z, n]
                    ).astype(late.dtype)
            for kind in range(4):
                link(kind, t, late_share).start()

        @pl.when(t == 0)
        def _():
            for to_z in range(RING):
                late_copy(to_z).start()
            for load in load_weight:
                load.wait()
            for d in range(RING):
                at = lax.rem(x + d, RING)
                block = jnp.concatenate([weight_raw[at], weight_raw[RING + at]], axis=1)
                if d == 0:
                    weight_in[0] = block
                else:
                    weight_send[d - 1] = block
                    weight_copy(d).start()
            gw_ref[...] = jnp.zeros_like(gw_ref)
            load_feat.wait()

        @pl.when(t < pairs)
        def _():
            for d in (1, RING - 1):
                feat_copy(d, t).start()

    def pass_on(t):
        @pl.when(t < pairs)
        def _():
            feat_copy(1, t).wait_recv()
            feat_pass(True, t).start()
            feat_copy(RING - 1, t).wait_recv()
            feat_pass(False, t).start()

    def merge(t):
        def run(share):
            link(0, t, share).wait_recv()
            merged[0, t] = added(share(0, z_up, t), first.at[0, t]).astype(merged.dtype)
            link(4, t, share).start()
            link(1, t, share).wait_recv()
            merged[1, t] = added(share(1, z_down, t), first.at[1, t]).astype(merged.dtype)
            link(5, t, share).start()

        pl.when(t < split)(lambda: run(early_share))
        pl.when(t >= split)(lambda: run(late_share))

    def sum_over_z(t):
        for kind in (2, 3, 4, 5):
            link(kind, t).wait_recv()

        @pl.when(t < split)
        def _():
            for i in range(2):
                half[t, i] = added(part_at(i, z, t), second.at[0, t, i], second.at[1, t, i]).astype(
                    half.dtype
                )
            for kind in (6, 7, 8):
                link(kind, t).start()

        @pl.when(t >= split)
        def _():
            for i in range(2):
                whole[h, 2 * t - split + i] = added(
                    late.at[z, t - split, i], second.at[0, t, i], second.at[1, t, i]
                ).astype(whole.dtype)
            link(8, t, late_share).start()

    def sum_over_y(t):
        @pl.when(t < split)
        def _():
            for kind in (6, 7, 8):
                link(kind, t).wait_recv()
            whole[h, t] = added(half.at[t, l], y_in.at[0, t]).astype(whole.dtype)
            whole[1 - h, t] = added(y_in.at[1, t], y_in.at[2, t]).astype(whole.dtype)
            for kind in range(9):
                link(kind, t).wait_send()

        @pl.when(t >= split)
        def _():
            link(8, t, late_share).wait_recv()

        @pl.when((lax.rem(t, 2) == 1) | (t >= split))
        def _():
            p = jnp.where(t < split, lax.div(t, 2), t - split // 2)
            multiply_features(p)

            @pl.when(p < pairs - 1)
            def _():
                multiply_weight(p)

    def panel_of(p):
        return jnp.concatenate(
            [whole[:, 2 * p + i].reshape(2 * width, nodes_t) for i in range(2)], axis=1
        )

    def multiply_features(p):
        for up in (True, False):
            feat_pass(up, p).wait_recv()
        beside = jnp.concatenate([feat[d, nodes_of(p), :] for d in range(RING)], axis=1)
        gw_ref[...] += jnp.dot(panel_of(p), beside, preferred_element_type=jnp.float32)

    def multiply_weight(p):
        @pl.when(p == 0)
        def _():
            for d in range(1, RING):
                weight_copy(d).wait_recv()

        panel = panel_of(p)
        for d in (2, 1, 3, 0):
            block = jnp.dot(weight_in[d], panel, preferred_element_type=jnp.float32)
            if d == 0:
                gf_own[p] = block
            else:
                gf_send[d - 1, p] = block.astype(gf_send.dtype)
                gf_copy(d, p).start()

    def collect(p):
        for d in range(1, RING):
            gf_copy(d, p).wait_recv()
        block = gf_own[p] + added(*[gf_in.at[d - 1, p] for d in range(1, RING)])
        gf_ref[nodes_of(p), :] = block.T.astype(gf_ref.dtype)

    stages = (send_shares, merge, sum_over_z, sum_over_y, pass_on)

    @pl.loop(0, units + max(LAGS))
    def _(step):
        for late, stage in zip(LAGS, stages):
            t = step - late

            @pl.when((t >= 0) & (t < units))
            def _(stage=stage, t=t):
                stage(t)

    rows = width // 8

    def gw_copy(phase, d, source, target, peer):
        return pltpu.make_async_remote_copy(
            source, target, gw_sems.at[phase, 0, d], gw_sems.at[phase, 1, d], device_id=peer, device_id_type=MESH
        )

    def piece(ref, of, size=rows):
        return ref.at[pl.ds(pl.multiple_of(of * size, size), size)]

    gw_send[...] = gw_ref[pl.ds(pl.multiple_of((1 - col) * width, width), width), :].astype(gw_send.dtype)
    gives = [gw_copy(0, 0, gw_send, mate_in, mate)]
    gives[0].start()
    multiply_weight(pairs - 1)
    gives[0].wait_recv()
    mine = gw_ref[pl.ds(pl.multiple_of(col * width, width), width), :] + mate_in[...].astype(jnp.float32)
    gw_ref[0:width, :] = mine
    row_send[...] = mine.astype(row_send.dtype)
    for d in range(1, 8):
        gives.append(gw_copy(1, d, piece(row_send, lax.rem(row + d, 8)), row_in.at[d], peers[d - 1]))
        gives[-1].start()

    @pl.loop(0, pairs // 2)
    def _(p):
        collect(p)

    for to_z in range(RING):
        late_copy(to_z).wait_send()

    @pl.loop(split, units)
    def _(t):
        for kind in (0, 1, 2, 3, 4, 5, 8):
            link(kind, t, late_share).wait_send()

    own = gw_ref[pl.ds(pl.multiple_of(row * rows, rows), rows), :]
    for d in range(1, 8):
        gives[d].wait_recv()
        own += row_in[d].astype(jnp.float32)
    for d in range(RING):
        block = own[:, d * width : (d + 1) * width].astype(gw_out.dtype)
        if d == 0:
            gw_out[col, row, x] = block
        else:
            x_send[d] = block
            gives.append(gw_copy(2, d, x_send.at[d], gw_out.at[col, row, x], to_x[d]))
            gives[-1].start()

    for d in range(1, RING):
        slot = gw_out.at[col, row, lax.rem(x + RING - d, RING)]
        gw_copy(2, d, slot, slot, to_x[d]).wait_recv()
    for d in range(1, 8):
        gives.append(gw_copy(3, d, gw_out.at[col, row], gw_out.at[col, row], peers[d - 1]))
        gives[-1].start()

    @pl.loop(pairs // 2, pairs)
    def _(p):
        collect(p)

    @pl.loop(0, pairs)
    def _(p):
        for up in (True, False):
            feat_pass(up, p).wait_send()
        for d in (1, RING - 1):
            feat_copy(d, p).wait_send()
        for d in range(1, RING):
            gf_copy(d, p).wait_send()

    for d in range(1, RING):
        weight_copy(d).wait_send()
    def hand_on(d, of_col):
        slot = gw_out.at[of_col, lax.rem(row + 8 - d, 8)]
        return gw_copy(4, d, slot, slot, mate)

    gives.append(hand_on(0, col))
    gives[-1].start()
    for d in range(1, 8):
        slot = gw_out.at[col, lax.rem(row + 8 - d, 8)]
        gw_copy(3, d, slot, slot, peers[d - 1]).wait_recv()
        gives.append(hand_on(d, col))
        gives[-1].start()
    for d in range(8):
        hand_on(d, 1 - col).wait_recv()
    for give in gives:
        give.wait_send()


def flow(part, weight, features):
    _, width, cut = part.shape
    nodes = features.shape[0]
    chunks = nodes // cut
    pairs = chunks // 2
    piece = (width, cut)
    block = (width, 2 * cut)
    sixteen = jnp.bfloat16
    rows = width // 8
    return pl.pallas_call(
        flow_kernel,
        out_shape=(
            jax.ShapeDtypeStruct((nodes, width), sixteen),
            jax.ShapeDtypeStruct((2, 8, RING, rows, width), sixteen),
        ),
        in_specs=[VMEM, HBM, HBM],
        out_specs=(VMEM, VMEM),
        scratch_shapes=[
            pltpu.VMEM((2, chunks, *piece), sixteen),
            pltpu.VMEM((2, chunks, 2, *piece), sixteen),
            pltpu.VMEM((2, chunks, *piece), sixteen),
            pltpu.VMEM((chunks, 2, *piece), sixteen),
            pltpu.VMEM((3, chunks, *piece), sixteen),
            pltpu.VMEM((RING, LATE, *piece), sixteen),
            pltpu.VMEM((RING, LATE // 2, 2, *piece), sixteen),
            pltpu.VMEM((2, chunks, *piece), sixteen),
            pltpu.VMEM((2 * RING, width, width), sixteen),
            pltpu.VMEM((RING - 1, width, 2 * width), sixteen),
            pltpu.VMEM((RING, width, 2 * width), sixteen),
            pltpu.VMEM((RING, nodes, width), sixteen),
            pltpu.VMEM((pairs, *block), jnp.float32),
            pltpu.VMEM((RING - 1, pairs, *block), sixteen),
            pltpu.VMEM((RING - 1, pairs, *block), sixteen),
            pltpu.VMEM((2 * width, RING * width), jnp.float32),
            pltpu.VMEM((width, RING * width), sixteen),
            pltpu.VMEM((width, RING * width), sixteen),
            pltpu.VMEM((width, RING * width), sixteen),
            pltpu.VMEM((8, rows, RING * width), sixteen),
            pltpu.VMEM((RING, rows, width), sixteen),
            pltpu.SemaphoreType.DMA((1 + 2 * RING,)),
            pltpu.SemaphoreType.DMA((9, chunks)),
            pltpu.SemaphoreType.DMA((9, chunks)),
            pltpu.SemaphoreType.DMA((2, 3, RING, pairs)),
            pltpu.SemaphoreType.DMA((2, RING)),
            pltpu.SemaphoreType.DMA((5, 2, 8)),
        ],
        compiler_params=pltpu.CompilerParams(
            collective_id=1, has_side_effects=True, vmem_limit_bytes=24 << 20
        ),
        cost_estimate=pl.CostEstimate(
            flops=32 * nodes * width * width, bytes_accessed=16 << 20, transcendentals=0
        ),
        name="flow",
    )(part, weight, features)


def finish_kernel(gf_ref, gw_ref, gf_hbm, gw_hbm, gw_turned, sems):
    width = gw_turned.shape[0]
    write_gf = pltpu.make_async_copy(gf_ref, gf_hbm, sems.at[0])
    write_gf.start()
    for side in range(2):
        for x in range(RING):
            target = side * RING + x
            block = gw_ref[side, :, x].reshape(width, width).astype(jnp.float32)
            gw_turned[:, target * width : (target + 1) * width] = block.T
    write_gw = pltpu.make_async_copy(gw_turned, gw_hbm, sems.at[1])
    write_gw.start()
    write_gf.wait()
    write_gw.wait()


def finish(gf, gw):
    width = gf.shape[1]
    turned = (width, 2 * RING * width)
    return pl.pallas_call(
        finish_kernel,
        out_shape=(
            jax.ShapeDtypeStruct(gf.shape, gf.dtype),
            jax.ShapeDtypeStruct(turned, jnp.float32),
        ),
        in_specs=[VMEM, VMEM],
        out_specs=(HBM, HBM),
        scratch_shapes=[pltpu.VMEM(turned, jnp.float32), pltpu.SemaphoreType.DMA((2,))],
        compiler_params=pltpu.CompilerParams(vmem_limit_bytes=4 << 20),
        cost_estimate=pl.CostEstimate(flops=0, bytes_accessed=1 << 20, transcendentals=0),
        name="finish",
    )(gf, gw)


def on_device(features, pre_activation, out_grad, weight, tiles, rows, cols, counts):
    features, pre_activation, out_grad, weight, tiles, rows, cols = (
        pltpu.with_memory_space_constraint(a, pltpu.HBM)
        for a in (features, pre_activation, out_grad, weight, tiles[0, 0], rows, cols)
    )
    out_tiles = 8 * (features.shape[0] // tiles.shape[1])
    grad, early, sums, rows, cols = local_grads(
        pre_activation, out_grad, tiles, rows, cols, out_tiles
    )
    part = tile_products(rows, cols, counts, grad, early, sums, tiles, out_tiles)
    return finish(*flow(part, weight, features))


def solution(mesh):
    in_specs = (
        P(("row", "col"), "fib"),
        P(("row", "col"), "fib"),
        P(("row", "col"), "fib"),
        P("fib", None),
        P("row", "col", None, None, None),
        P("row", "col", None),
        P("row", "col", None),
        P("row", "col"),
    )
    out_specs = (P(("row", "col"), "fib"), P("fib", None))
    return jax.shard_map(
        on_device, mesh=mesh, in_specs=in_specs, out_specs=out_specs, check_vma=False
    )
```

```python
import functools

import jax
import jax.numpy as jnp
from jax import lax
from jax.experimental import pallas as pl
from jax.experimental.pallas import tpu as pltpu
from jax.sharding import PartitionSpec as P

GROUP = 32
EARLY = 64
RING = 4
LAGS = (0, 2, 5, 8, 4)
MESH = pl.DeviceIdType.MESH
VMEM = pl.BlockSpec(memory_space=pltpu.VMEM)
HBM = pl.BlockSpec(memory_space=pltpu.HBM)
SMEM = pl.BlockSpec(memory_space=pltpu.SMEM)
CHUNK = 128
LATE = 4


def greet(peers):
    barrier = pltpu.get_barrier_semaphore()
    for peer in peers:
        pl.semaphore_signal(barrier, inc=1, device_id=peer, device_id_type=MESH)
    pl.semaphore_wait(barrier, len(peers))


def position():
    return lax.axis_index("row"), lax.axis_index("col"), lax.axis_index("fib")


def grad_kernel(
    pre_hbm, out_grad_hbm, tiles_hbm, rows_hbm, cols_hbm,
    grad_ref, early_ref, sums_ref, rows_ref, cols_ref,
    pre_ref, out_grad_ref, load_sems, tile_sems, index_sems, send_sems, recv_sems,
):
    row, col, fib = position()
    own_tiles = grad_ref.shape[0] // 2
    tile = grad_ref.shape[2]
    partner = (row, 1 - col, fib)

    def loads(t):
        part = pl.ds(pl.multiple_of(t * tile, tile), tile)
        return (
            pltpu.make_async_copy(pre_hbm.at[part], pre_ref.at[part], load_sems.at[0, t]),
            pltpu.make_async_copy(out_grad_hbm.at[part], out_grad_ref.at[part], load_sems.at[1, t]),
        )

    @pl.loop(0, own_tiles)
    def _(t):
        for load in loads(t):
            load.start()

    def early(g):
        group = pl.ds(g * GROUP, GROUP)
        return pltpu.make_async_copy(tiles_hbm.at[group], early_ref.at[group], tile_sems.at[g])

    @pl.loop(0, EARLY // GROUP)
    def _(g):
        early(g).start()

    indices = [
        pltpu.make_async_copy(source, target, index_sems.at[i])
        for i, (source, target) in enumerate(((rows_hbm, rows_ref), (cols_hbm, cols_ref)))
    ]
    for load in indices:
        load.start()
    greet([partner])

    def copy(t, owner):
        slot = grad_ref.at[owner * own_tiles + t]
        return pltpu.make_async_remote_copy(
            slot, slot, send_sems.at[t], recv_sems.at[t], device_id=partner, device_id_type=MESH
        )

    @pl.loop(0, own_tiles)
    def _(t):
        for load in loads(t):
            load.wait()
        part = pl.ds(pl.multiple_of(t * tile, tile), tile)
        pre = pre_ref[part, :].astype(jnp.float32)
        sigmoid = jax.nn.sigmoid(pre)
        grad = out_grad_ref[part, :].astype(jnp.float32) * sigmoid * (1.0 + pre * (1.0 - sigmoid))
        grad_ref[col * own_tiles + t] = grad.T.astype(grad_ref.dtype)
        copy(t, col).start()

    @pl.loop(0, sums_ref.shape[0], unroll=5)
    def _(t):
        sums_ref[t] = jnp.zeros(sums_ref.shape[1:], sums_ref.dtype)

    @pl.loop(0, own_tiles)
    def _(t):
        copy(t, col).wait_send()
        copy(t, 1 - col).wait_recv()

    @pl.loop(0, EARLY // GROUP)
    def _(g):
        early(g).wait()

    for load in indices:
        load.wait()


def local_grads(pre, out_grad, tiles, rows, cols, out_tiles):
    nodes, width = pre.shape
    tile = tiles.shape[1]
    own_tiles = nodes // tile
    return pl.pallas_call(
        grad_kernel,
        out_shape=(
            jax.ShapeDtypeStruct((2 * own_tiles, width, tile), jnp.bfloat16),
            jax.ShapeDtypeStruct((EARLY, tile, tile), tiles.dtype),
            jax.ShapeDtypeStruct((out_tiles + 1, width, tile), jnp.float32),
            jax.ShapeDtypeStruct(rows.shape, rows.dtype),
            jax.ShapeDtypeStruct(cols.shape, cols.dtype),
        ),
        in_specs=[HBM] * 5,
        out_specs=(VMEM,) * 5,
        scratch_shapes=[
            pltpu.VMEM(pre.shape, pre.dtype),
            pltpu.VMEM(pre.shape, pre.dtype),
            pltpu.SemaphoreType.DMA((2, own_tiles)),
            pltpu.SemaphoreType.DMA((EARLY // GROUP,)),
            pltpu.SemaphoreType.DMA((2,)),
            pltpu.SemaphoreType.DMA((own_tiles,)),
            pltpu.SemaphoreType.DMA((own_tiles,)),
        ],
        compiler_params=pltpu.CompilerParams(
            collective_id=0, has_side_effects=True, vmem_limit_bytes=16 << 20
        ),
        cost_estimate=pl.CostEstimate(
            flops=10 * nodes * width, bytes_accessed=8 * nodes * width, transcendentals=nodes * width
        ),
        name="local_grads",
    )(pre, out_grad, tiles, rows, cols)


def tile_kernel(
    rows_ref, cols_ref, count_ref, grad_ref, early_ref, sums_ref, tiles_ref, out_ref, total,
    held, sems,
):
    slots, tile, _ = tiles_ref.shape
    cuts = tile // CHUNK
    out_tiles = out_ref.shape[0] // cuts
    row_tiles = grad_ref.shape[0]
    def copy(g):
        source = tiles_ref.at[pl.ds(g * GROUP, GROUP)]
        return pltpu.make_async_copy(
            source, held.at[pl.ds(g * GROUP - EARLY, GROUP)], sems.at[g - EARLY // GROUP]
        )

    count = jnp.clip(count_ref[0, 0], 1, slots)
    used = (count + GROUP - 1) // GROUP

    @pl.loop(EARLY // GROUP, used)
    def _(g):
        copy(g).start()

    def add_group(g, tile_at):
        for j in range(GROUP):
            slot = g * GROUP + j
            row = jnp.clip(rows_ref[0, 0, slot], 0, row_tiles - 1)
            col = jnp.clip(cols_ref[0, 0, slot], 0, out_tiles - 1)
            target = jnp.where(slot < count, col, out_tiles)
            total[target] += jnp.dot(grad_ref[row], tile_at(slot), preferred_element_type=jnp.float32)

    @pl.loop(0, jnp.minimum(used, EARLY // GROUP))
    def _(g):
        add_group(g, lambda slot: early_ref[slot])

    @pl.loop(EARLY // GROUP, used)
    def _(g):
        copy(g).wait()
        add_group(g, lambda slot: held[slot - EARLY])

    @pl.loop(0, out_tiles, unroll=4)
    def _(t):
        for cut in range(cuts):
            out_ref[t * cuts + cut] = total[t, :, cut * CHUNK : (cut + 1) * CHUNK].astype(out_ref.dtype)


def tile_products(rows, cols, count, grad, early, sums, tiles, out_tiles):
    slots, tile, _ = tiles.shape
    width = grad.shape[1]
    return pl.pallas_call(
        tile_kernel,
        out_shape=(
            jax.ShapeDtypeStruct((out_tiles * tile // CHUNK, width, CHUNK), jnp.bfloat16),
            jax.ShapeDtypeStruct(sums.shape, sums.dtype),
        ),
        input_output_aliases={5: 1},
        in_specs=[SMEM, SMEM, SMEM, VMEM, VMEM, VMEM, HBM],
        out_specs=(VMEM, VMEM),
        scratch_shapes=[
            pltpu.VMEM((slots - EARLY, tile, tile), jnp.bfloat16),
            pltpu.SemaphoreType.DMA(((slots - EARLY) // GROUP,)),
        ],
        compiler_params=pltpu.CompilerParams(vmem_limit_bytes=28 << 20),
        cost_estimate=pl.CostEstimate(
            flops=2 * slots * width * tile * tile,
            bytes_accessed=2 * slots * tile * tile,
            transcendentals=0,
        ),
        name="tile_products",
    )(rows, cols, count, grad, early, sums, tiles)[0]


def flow_kernel(
    part_all, weight_hbm, feat_hbm, gf_ref, gw_out,
    first, second, merged, half, y_in, late_in, late, whole, weight_raw, weight_send, weight_in, feat,
    gf_own, gf_send, gf_in, gw_ref, gw_send, mate_in, row_send, row_in, x_send,
    load_sems, send_sems, recv_sems, x_sems, late_sems, gw_sems,
):
    row, col, fib = position()
    l, z = row // RING, lax.rem(row, RING)
    h, x = fib // RING, lax.rem(fib, RING)
    chunks, width, nodes_t = whole.shape[1:]
    pairs, span_t = chunks // 2, 2 * nodes_t
    split = chunks - LATE
    units = split + LATE // 2
    z_up, z_down, z_far = (lax.rem(z + d, RING) for d in (1, RING - 1, 2))
    to_z_up, to_z_down = (l * RING + z_up, col, fib), (l * RING + z_down, col, fib)
    to_x = [(row, col, h * RING + lax.rem(x + d, RING)) for d in range(RING)]
    to_pair = ((1 - l) * RING + z, col, fib)
    to_cross = ((1 - l) * RING + z, col, (1 - h) * RING + x)
    to_far = (row, col, (1 - h) * RING + x)
    mate = (row, 1 - col, fib)
    peers = [(lax.rem(row + d, 8), col, fib) for d in range(1, 8)]

    def nodes_of(p):
        return pl.ds(pl.multiple_of(p * span_t, span_t), span_t)

    load_weight = [
        pltpu.make_async_copy(
            weight_hbm.at[:, k * width : (k + 1) * width], weight_raw.at[k], load_sems.at[1 + k]
        )
        for k in range(2 * RING)
    ]
    load_feat = pltpu.make_async_copy(feat_hbm, feat.at[0], load_sems.at[0])
    for load in load_weight:
        load.start()
    load_feat.start()
    greet([*to_x[1:], to_cross, to_far, mate, *peers])

    def part_at(to_l, to_z, t):
        return part_all.at[(to_l * RING + to_z) * chunks + t]

    def copy(kind, t, source, target, peer):
        return pltpu.make_async_remote_copy(
            source, target, send_sems.at[kind, t], recv_sems.at[kind, t], device_id=peer, device_id_type=MESH
        )

    def late_copy(to_z):
        source = part_all.at[pl.ds(((1 - l) * RING + to_z) * chunks + split, LATE)]
        return pltpu.make_async_remote_copy(
            source, late_in.at[to_z], late_sems.at[0, to_z], late_sems.at[1, to_z], device_id=to_pair, device_id_type=MESH
        )

    def early_share(i, to_z, t):
        return part_at(i, to_z, t)

    def late_share(i, to_z, t):
        return late.at[to_z, t - split, i]

    def link(kind, t, share=early_share):
        if kind == 0:
            return copy(0, t, share(0, z_far, t), first.at[0, t], to_z_up)
        if kind == 1:
            return copy(1, t, share(1, z_far, t), first.at[1, t], to_z_down)
        if kind == 2:
            return copy(2, t, share(1, z_up, t), second.at[0, t, 1], to_z_up)
        if kind == 3:
            return copy(3, t, share(0, z_down, t), second.at[1, t, 0], to_z_down)
        if kind == 4:
            return copy(4, t, merged.at[0, t], second.at[0, t, 0], to_z_up)
        if kind == 5:
            return copy(5, t, merged.at[1, t], second.at[1, t, 1], to_z_down)
        if kind == 6:
            return copy(6, t, half.at[t, 1 - l], y_in.at[0, t], to_pair)
        if kind == 7:
            return copy(7, t, half.at[t, 1 - l], y_in.at[1, t], to_cross)
        if share is late_share:
            both = whole.at[h, pl.ds(2 * t - split, 2)]
            return copy(8, t, both, both, to_far)
        return copy(8, t, half.at[t, l], y_in.at[2, t], to_far)

    def along_x(kind, d, p, source, target, peer=None):
        return pltpu.make_async_remote_copy(
            source,
            target,
            x_sems.at[0, kind, d, p],
            x_sems.at[1, kind, d, p],
            device_id=to_x[d] if peer is None else peer,
            device_id_type=MESH,
        )

    def feat_pass(up, p):
        part = pl.ds(pl.multiple_of(p * span_t + (0 if up else nodes_t), nodes_t), nodes_t)
        source = feat.at[RING - 1 if up else 1, part]
        return along_x(0, 2 if up else 0, p, source, feat.at[2, part], to_x[1 if up else RING - 1])

    def feat_copy(d, p):
        return along_x(0, d, p, feat.at[0, nodes_of(p)], feat.at[RING - d, nodes_of(p)])

    def gf_copy(d, p):
        return along_x(1, d, p, gf_send.at[d - 1, p], gf_in.at[d - 1, p])

    def weight_copy(d):
        return along_x(2, d, 0, weight_send.at[d - 1], weight_in.at[RING - d])

    def added(*refs):
        terms = [r[...].astype(jnp.float32) for r in refs]
        return functools.reduce(lambda a, b: a + b, terms)

    def send_shares(t):
        @pl.when(t < split)
        def _():
            for kind in range(4):
                link(kind, t).start()

        @pl.when(t == split)
        def _():
            for to_z in range(RING):
                late_copy(to_z).wait_recv()

        @pl.when(t >= split)
        def _():
            for to_z in (z_far, z_up, z_down, z):
                for i in range(2):
                    n = 2 * (t - split) + i
                    late[to_z, t - split, i] = added(
                        part_at(l, to_z, split + n), late_in.at[to_z, n]
                    ).astype(late.dtype)
            for kind in range(4):
                link(kind, t, late_share).start()

        @pl.when(t == 0)
        def _():
            for to_z in range(RING):
                late_copy(to_z).start()
            for load in load_weight:
                load.wait()
            for d in range(RING):
                at = lax.rem(x + d, RING)
                block = jnp.concatenate([weight_raw[at], weight_raw[RING + at]], axis=1)
                if d == 0:
                    weight_in[0] = block
                else:
                    weight_send[d - 1] = block
                    weight_copy(d).start()
            gw_ref[...] = jnp.zeros_like(gw_ref)
            load_feat.wait()

        @pl.when(t < pairs)
        def _():
            for d in (1, RING - 1):
                feat_copy(d, t).start()

    def pass_on(t):
        @pl.when(t < pairs)
        def _():
            feat_copy(1, t).wait_recv()
            feat_pass(True, t).start()
            feat_copy(RING - 1, t).wait_recv()
            feat_pass(False, t).start()

    def merge(t):
        def run(share):
            link(0, t, share).wait_recv()
            merged[0, t] = added(share(0, z_up, t), first.at[0, t]).astype(merged.dtype)
            link(4, t, share).start()
            link(1, t, share).wait_recv()
            merged[1, t] = added(share(1, z_down, t), first.at[1, t]).astype(merged.dtype)
            link(5, t, share).start()

        pl.when(t < split)(lambda: run(early_share))
        pl.when(t >= split)(lambda: run(late_share))

    def sum_over_z(t):
        for kind in (2, 3, 4, 5):
            link(kind, t).wait_recv()

        @pl.when(t < split)
        def _():
            for i in range(2):
                half[t, i] = added(part_at(i, z, t), second.at[0, t, i], second.at[1, t, i]).astype(
                    half.dtype
                )
            for kind in (6, 7, 8):
                link(kind, t).start()

        @pl.when(t >= split)
        def _():
            for i in range(2):
                whole[h, 2 * t - split + i] = added(
                    late.at[z, t - split, i], second.at[0, t, i], second.at[1, t, i]
                ).astype(whole.dtype)
            link(8, t, late_share).start()

    def sum_over_y(t):
        @pl.when(t < split)
        def _():
            for kind in (6, 7, 8):
                link(kind, t).wait_recv()
            whole[h, t] = added(half.at[t, l], y_in.at[0, t]).astype(whole.dtype)
            whole[1 - h, t] = added(y_in.at[1, t], y_in.at[2, t]).astype(whole.dtype)
            for kind in range(9):
                link(kind, t).wait_send()

        @pl.when(t >= split)
        def _():
            link(8, t, late_share).wait_recv()

        @pl.when((lax.rem(t, 2) == 1) | (t >= split))
        def _():
            p = jnp.where(t < split, lax.div(t, 2), t - split // 2)
            multiply_features(p)

            @pl.when(p < pairs - 1)
            def _():
                multiply_weight(p)

    def panel_of(p):
        return jnp.concatenate(
            [whole[:, 2 * p + i].reshape(2 * width, nodes_t) for i in range(2)], axis=1
        )

    def multiply_features(p):
        for up in (True, False):
            feat_pass(up, p).wait_recv()
        beside = jnp.concatenate([feat[d, nodes_of(p), :] for d in range(RING)], axis=1)
        gw_ref[...] += jnp.dot(panel_of(p), beside, preferred_element_type=jnp.float32)

    def multiply_weight(p):
        @pl.when(p == 0)
        def _():
            for d in range(1, RING):
                weight_copy(d).wait_recv()

        panel = panel_of(p)
        for d in (2, 1, 3, 0):
            block = jnp.dot(weight_in[d], panel, preferred_element_type=jnp.float32)
            if d == 0:
                gf_own[p] = block
            else:
                gf_send[d - 1, p] = block.astype(gf_send.dtype)
                gf_copy(d, p).start()

    def collect(p):
        for d in range(1, RING):
            gf_copy(d, p).wait_recv()
        block = gf_own[p] + added(*[gf_in.at[d - 1, p] for d in range(1, RING)])
        gf_ref[nodes_of(p), :] = block.T.astype(gf_ref.dtype)

    stages = (send_shares, merge, sum_over_z, sum_over_y, pass_on)

    @pl.loop(0, units + max(LAGS))
    def _(step):
        for late, stage in zip(LAGS, stages):
            t = step - late

            @pl.when((t >= 0) & (t < units))
            def _(stage=stage, t=t):
                stage(t)

    rows = width // 8

    def gw_copy(phase, d, source, target, peer):
        return pltpu.make_async_remote_copy(
            source, target, gw_sems.at[phase, 0, d], gw_sems.at[phase, 1, d], device_id=peer, device_id_type=MESH
        )

    def piece(ref, of, size=rows):
        return ref.at[pl.ds(pl.multiple_of(of * size, size), size)]

    gw_send[...] = gw_ref[pl.ds(pl.multiple_of((1 - col) * width, width), width), :].astype(gw_send.dtype)
    gives = [gw_copy(0, 0, gw_send, mate_in, mate)]
    gives[0].start()
    multiply_weight(pairs - 1)
    gives[0].wait_recv()
    mine = gw_ref[pl.ds(pl.multiple_of(col * width, width), width), :] + mate_in[...].astype(jnp.float32)
    gw_ref[0:width, :] = mine
    row_send[...] = mine.astype(row_send.dtype)
    for d in range(1, 8):
        gives.append(gw_copy(1, d, piece(row_send, lax.rem(row + d, 8)), row_in.at[d], peers[d - 1]))
        gives[-1].start()

    @pl.loop(0, pairs // 2)
    def _(p):
        collect(p)

    for to_z in range(RING):
        late_copy(to_z).wait_send()

    @pl.loop(split, units)
    def _(t):
        for kind in (0, 1, 2, 3, 4, 5, 8):
            link(kind, t, late_share).wait_send()

    own = gw_ref[pl.ds(pl.multiple_of(row * rows, rows), rows), :]
    for d in range(1, 8):
        gives[d].wait_recv()
        own += row_in[d].astype(jnp.float32)
    for d in range(RING):
        block = own[:, d * width : (d + 1) * width].astype(gw_out.dtype)
        if d == 0:
            gw_out[col, row, x] = block
        else:
            x_send[d] = block
            gives.append(gw_copy(2, d, x_send.at[d], gw_out.at[col, row, x], to_x[d]))
            gives[-1].start()

    for d in range(1, RING):
        slot = gw_out.at[col, row, lax.rem(x + RING - d, RING)]
        gw_copy(2, d, slot, slot, to_x[d]).wait_recv()
    for d in range(1, 8):
        gives.append(gw_copy(3, d, gw_out.at[col, row], gw_out.at[col, row], peers[d - 1]))
        gives[-1].start()

    @pl.loop(pairs // 2, pairs)
    def _(p):
        collect(p)

    @pl.loop(0, pairs)
    def _(p):
        for up in (True, False):
            feat_pass(up, p).wait_send()
        for d in (1, RING - 1):
            feat_copy(d, p).wait_send()
        for d in range(1, RING):
            gf_copy(d, p).wait_send()

    for d in range(1, RING):
        weight_copy(d).wait_send()
    def hand_on(d, of_col):
        slot = gw_out.at[of_col, lax.rem(row + 8 - d, 8)]
        return gw_copy(4, d, slot, slot, mate)

    gives.append(hand_on(0, col))
    gives[-1].start()
    for d in range(1, 8):
        slot = gw_out.at[col, lax.rem(row + 8 - d, 8)]
        gw_copy(3, d, slot, slot, peers[d - 1]).wait_recv()
        gives.append(hand_on(d, col))
        gives[-1].start()
    for d in range(8):
        hand_on(d, 1 - col).wait_recv()
    for give in gives:
        give.wait_send()


def flow(part, weight, features):
    _, width, cut = part.shape
    nodes = features.shape[0]
    chunks = nodes // cut
    pairs = chunks // 2
    piece = (width, cut)
    block = (width, 2 * cut)
    sixteen = jnp.bfloat16
    rows = width // 8
    return pl.pallas_call(
        flow_kernel,
        out_shape=(
            jax.ShapeDtypeStruct((nodes, width), sixteen),
            jax.ShapeDtypeStruct((2, 8, RING, rows, width), sixteen),
        ),
        in_specs=[VMEM, HBM, HBM],
        out_specs=(VMEM, VMEM),
        scratch_shapes=[
            pltpu.VMEM((2, chunks, *piece), sixteen),
            pltpu.VMEM((2, chunks, 2, *piece), sixteen),
            pltpu.VMEM((2, chunks, *piece), sixteen),
            pltpu.VMEM((chunks, 2, *piece), sixteen),
            pltpu.VMEM((3, chunks, *piece), sixteen),
            pltpu.VMEM((RING, LATE, *piece), sixteen),
            pltpu.VMEM((RING, LATE // 2, 2, *piece), sixteen),
            pltpu.VMEM((2, chunks, *piece), sixteen),
            pltpu.VMEM((2 * RING, width, width), sixteen),
            pltpu.VMEM((RING - 1, width, 2 * width), sixteen),
            pltpu.VMEM((RING, width, 2 * width), sixteen),
            pltpu.VMEM((RING, nodes, width), sixteen),
            pltpu.VMEM((pairs, *block), jnp.float32),
            pltpu.VMEM((RING - 1, pairs, *block), sixteen),
            pltpu.VMEM((RING - 1, pairs, *block), sixteen),
            pltpu.VMEM((2 * width, RING * width), jnp.float32),
            pltpu.VMEM((width, RING * width), sixteen),
            pltpu.VMEM((width, RING * width), sixteen),
            pltpu.VMEM((width, RING * width), sixteen),
            pltpu.VMEM((8, rows, RING * width), sixteen),
            pltpu.VMEM((RING, rows, width), sixteen),
            pltpu.SemaphoreType.DMA((1 + 2 * RING,)),
            pltpu.SemaphoreType.DMA((9, chunks)),
            pltpu.SemaphoreType.DMA((9, chunks)),
            pltpu.SemaphoreType.DMA((2, 3, RING, pairs)),
            pltpu.SemaphoreType.DMA((2, RING)),
            pltpu.SemaphoreType.DMA((5, 2, 8)),
        ],
        compiler_params=pltpu.CompilerParams(
            collective_id=1, has_side_effects=True, vmem_limit_bytes=24 << 20
        ),
        cost_estimate=pl.CostEstimate(
            flops=32 * nodes * width * width, bytes_accessed=16 << 20, transcendentals=0
        ),
        name="flow",
    )(part, weight, features)


def finish_kernel(gf_ref, gw_ref, gf_hbm, gw_hbm, gw_turned, sems):
    width = gw_turned.shape[0]
    write_gf = pltpu.make_async_copy(gf_ref, gf_hbm, sems.at[0])
    write_gf.start()
    for side in range(2):
        for x in range(RING):
            target = side * RING + x
            block = gw_ref[side, :, x].reshape(width, width).astype(jnp.float32)
            gw_turned[:, target * width : (target + 1) * width] = block.T
    write_gw = pltpu.make_async_copy(gw_turned, gw_hbm, sems.at[1])
    write_gw.start()
    write_gf.wait()
    write_gw.wait()


def finish(gf, gw):
    width = gf.shape[1]
    turned = (width, 2 * RING * width)
    return pl.pallas_call(
        finish_kernel,
        out_shape=(
            jax.ShapeDtypeStruct(gf.shape, gf.dtype),
            jax.ShapeDtypeStruct(turned, jnp.float32),
        ),
        in_specs=[VMEM, VMEM],
        out_specs=(HBM, HBM),
        scratch_shapes=[pltpu.VMEM(turned, jnp.float32), pltpu.SemaphoreType.DMA((2,))],
        compiler_params=pltpu.CompilerParams(vmem_limit_bytes=4 << 20),
        cost_estimate=pl.CostEstimate(flops=0, bytes_accessed=1 << 20, transcendentals=0),
        name="finish",
    )(gf, gw)


def on_device(features, pre_activation, out_grad, weight, tiles, rows, cols, counts):
    features, pre_activation, out_grad, weight, tiles, rows, cols = (
        pltpu.with_memory_space_constraint(a, pltpu.HBM)
        for a in (features, pre_activation, out_grad, weight, tiles[0, 0], rows, cols)
    )
    out_tiles = 8 * (features.shape[0] // tiles.shape[1])
    grad, early, sums, rows, cols = local_grads(
        pre_activation, out_grad, tiles, rows, cols, out_tiles
    )
    part = tile_products(rows, cols, counts, grad, early, sums, tiles, out_tiles)
    return finish(*flow(part, weight, features))


def solution(mesh):
    in_specs = (
        P(("row", "col"), "fib"),
        P(("row", "col"), "fib"),
        P(("row", "col"), "fib"),
        P("fib", None),
        P("row", "col", None, None, None),
        P("row", "col", None),
        P("row", "col", None),
        P("row", "col"),
    )
    out_specs = (P(("row", "col"), "fib"), P("fib", None))
    return jax.shard_map(
        on_device, mesh=mesh, in_specs=in_specs, out_specs=out_specs, check_vma=False
    )
```
